32 devices in a mesh: dp: 16 (over z, y, core), shard: 2 (over x).
Axes of the slice: x: 2, y: 2, z: 4, core: 2. Of those that a mesh axis runs over, the one named last changes fastest.
Arguments:
- tokens: bfloat16 [32768, 512], P(('dp', 'shard')), may hold values from -6 to 6
- segment_ids: int32 [32768], P(('dp', 'shard')), may hold values from 0 to 1024, as said below
- row_counts: int32 [32], P(('dp', 'shard')), may hold values from 512 to 1024, as said below
- global_count: int32 [1], replicated, may hold values from 32768 to 65536
- cotangent: float32 [32768, 512], P(('dp', 'shard')), may hold values from -6 to 6
- query_weight: bfloat16 [512, 512], P('shard'), may hold values from -0.25 to 0.25
- key_weight: bfloat16 [512, 512], P('shard'), may hold values from -0.25 to 0.25
- value_weight: bfloat16 [512, 512], P('shard'), may hold values from -0.25 to 0.25
- output_weight: bfloat16 [512, 512], P('shard'), may hold values from -1 to 1
- inner_weight: bfloat16 [512, 2048], P('shard'), may hold values from -0.25 to 0.25
- outer_weight: bfloat16 [2048, 512], P('shard'), may hold values from -0.125 to 0.125
- attn_gain: bfloat16 [512], P('shard'), may hold values from 0.5 to 1.5
- attn_bias: bfloat16 [512], P('shard'), may hold values from -3 to 3
- feed_gain: bfloat16 [512], P('shard'), may hold values from 0.5 to 1.5
- feed_bias: bfloat16 [512], P('shard'), may hold values from -3 to 3
Outputs:
- mixed: bfloat16 [32768, 512], P(('dp', 'shard'))
- input_grad: float32 [32768, 512], P(('dp', 'shard'))
- query_grad: float32 [512, 512], P('shard')
- key_grad: float32 [512, 512], P('shard')
- value_grad: float32 [512, 512], P('shard')
- output_grad: float32 [512, 512], P('shard')
- inner_grad: float32 [512, 2048], P('shard')
- outer_grad: float32 [2048, 512], P('shard')
- attn_gain_grad: float32 [512], P('shard')
- attn_bias_grad: float32 [512], P('shard')
- feed_gain_grad: float32 [512], P('shard')
- feed_bias_grad: float32 [512], P('shard')
The draws below stay inside these ranges and needn't reach their ends.
Inputs may be any that keep to these rules, and one draw needn't show every extreme that they name: `segment_ids`: within each row of 1024 tokens the ids never fall; a sentence (a run of one id below 1024) holds 1 to 256 tokens and some sentence holds exactly 256; the tokens from the row's count onward carry the id 1024. `row_counts`: some row uses all 1024 tokens and some row exactly half of them. `global_count`: at least the number of tokens in use over all rows.
All inputs are finite; a program needn't handle non-finite values.
Results may differ from the reference program's by a relative error of at most 0.028.
Values may be sent and summed in bfloat16 or wider, within the bound.
No kernel may reach another device: no remote copies, remote signals or barrier semaphores. Data moves between devices by JAX's collectives and lax.ppermute only.
A program may use at most 256 MiB of HBM per device.

```python
import math
import jax
import jax.numpy as jnp
from jax import lax

D = 512
H = 8
FF = 2048
HD = 64
L = 1024
SEG_MOST = 256
POSITIONS = 2
ROWS = 32
TOKENS = 32768


def row_lengths(key):
    base = jax.random.fold_in(key, 41)
    counts = jax.random.randint(jax.random.fold_in(base, 1), (ROWS,), L // 2, L + 1)
    full_row = jax.random.randint(jax.random.fold_in(base, 2), (), 0, ROWS)
    half_row = (full_row + jax.random.randint(jax.random.fold_in(base, 3), (), 1, ROWS)) % ROWS
    index = jnp.arange(ROWS)
    counts = jnp.where(index == full_row, L, counts)
    counts = jnp.where(index == half_row, L // 2, counts)
    return counts.astype(jnp.int32)


def draw_row_counts(key, part):
    return row_lengths(key)


def draw_segment_ids(key, part):
    counts = row_lengths(key)
    key = jax.random.fold_in(key, 9)
    lengths = jax.random.randint(jax.random.fold_in(key, 1), (ROWS, L), 1, SEG_MOST + 1)
    chosen = jax.random.randint(jax.random.fold_in(key, 2), (), 0, ROWS)
    column = jnp.arange(L)
    first = (jnp.arange(ROWS)[:, None] == chosen) & (column[None, :] == 0)
    lengths = jnp.where(first, SEG_MOST, lengths)
    ends = jnp.cumsum(lengths, axis=1)
    labels = jax.vmap(lambda row_ends: jnp.searchsorted(row_ends, column, side='right'))(ends)
    labels = jnp.where(column[None, :] < counts[:, None], labels, L)
    return labels.reshape(-1).astype(jnp.int32)


def spiked(values, stream_key, source, target, shards_of, factor):
    def block_of(axis_at):
        return (jnp.arange(values.shape[axis_at]) // (values.shape[axis_at] // shards_of)).reshape((-1,) + (1,) * (values.ndim - 1 - axis_at))

    one_side = jax.random.permutation(stream_key, shards_of)[block_of(target)]
    second = (block_of(target) + shards_of // 2) % shards_of
    return jnp.where((block_of(source) == one_side) | (block_of(source) == second), factor * values, values)


def steps_of(key, extent, cuts, low, top_value):
    factor_of, own = 1.0, jax.random.fold_in(key, 6)
    for dim, blocks in cuts:
        steps = jnp.exp(jax.random.uniform(jax.random.fold_in(own, dim), (blocks,), jnp.float32, low / len(cuts), top_value / len(cuts)))
        factor_of = factor_of * jnp.repeat(steps, extent[dim] // blocks).reshape([-1 if axis == dim else 1 for axis in range(len(extent))])
    return factor_of


def noise(key, dims, width, limit, cuts=(), dtype=jnp.bfloat16):
    values = jax.random.normal(key, dims, jnp.float32) * width
    if len(cuts) > 0:
        values = steps_of(key, dims, cuts, -0.22, 0.18) * values
    return jnp.clip(values, min=-limit, max=limit).astype(dtype)


def gaussian_with(own_key, extent, width, reach, shards, heavy, held_as=jnp.bfloat16):
    drawn = width * jax.random.normal(own_key, extent, jnp.float32)
    if shards:
        drawn = drawn * steps_of(own_key, extent, shards, -0.22, 0.18)
    return jnp.clip(spiked(drawn, jax.random.fold_in(own_key, 3), *heavy), -reach, reach).astype(held_as)


def setup_inputs(seed: int = 0) -> dict:
    streams_of = jax.random.split(jax.random.key(seed), 16)
    tokens = noise(streams_of[0], (TOKENS, D), 1.0, 6.0, ((0, 32),))
    segment_ids = draw_segment_ids(jax.random.fold_in(streams_of[15], 71), 0)
    row_counts = draw_row_counts(jax.random.fold_in(streams_of[15], 71), 0)
    global_count = jax.random.randint(streams_of[3], (1,), TOKENS, 2 * TOKENS + 1).astype(jnp.int32)
    cotangent = gaussian_with(streams_of[4], (TOKENS, D), 1.0, 6.0, ((0, 32),), (0, 1, 32, 2.75), jnp.float32)
    query_weight = noise(streams_of[5], (D, D), D ** -0.5, 0.25, ((0, 2),))
    key_weight = noise(streams_of[6], (D, D), D ** -0.5, 0.25, ((0, 2),))
    value_weight = noise(streams_of[7], (D, D), D ** -0.5, 0.25, ((0, 2),))
    output_weight = noise(streams_of[8], (D, D), (D // 16) ** -0.5, 1.0, ((0, 2),))
    inner_weight = noise(streams_of[9], (D, FF), D ** -0.5, 0.25, ((0, 2),))
    outer_weight = noise(streams_of[10], (FF, D), FF ** -0.5, 0.125, ((0, 2),))
    attn_gain = jnp.clip(1.0 + 0.1 * jax.random.normal(streams_of[11], (D,), jnp.float32), 0.5, 1.5).astype(jnp.bfloat16)
    attn_bias = noise(streams_of[12], (D,), 0.5, 3.0, ((0, 2),))
    feed_gain = jnp.clip(1.0 + 0.1 * jax.random.normal(streams_of[13], (D,), jnp.float32), 0.5, 1.5).astype(jnp.bfloat16)
    feed_bias = noise(streams_of[14], (D,), 0.5, 3.0, ((0, 2),))
    return {"tokens": tokens, "segment_ids": segment_ids, "row_counts": row_counts, "global_count": global_count, "cotangent": cotangent, "query_weight": query_weight, "key_weight": key_weight, "value_weight": value_weight, "output_weight": output_weight, "inner_weight": inner_weight, "outer_weight": outer_weight, "attn_gain": attn_gain, "attn_bias": attn_bias, "feed_gain": feed_gain, "feed_bias": feed_bias}


@jax.custom_vjp
def low(v):
    return lax.optimization_barrier(v.astype(jnp.bfloat16)).astype(jnp.float32)

@jax.custom_vjp
def low_back(v):
    return v

def low_keep(v):
    return (low(v), None)

def low_pass(kept, grad):
    return (grad,)

def back_keep(v):
    return (v, None)

def back_low(kept, grad):
    return (low(grad),)
low.defvjp(low_keep, low_pass)
low_back.defvjp(back_keep, back_low)
masked_score = -1e+30
norm_eps = 1e-05

def matmul(left, right):
    return jnp.dot(left, right, precision=lax.Precision.HIGHEST)

def layer_norm(values, gain, shift):
    center = values - lax.optimization_barrier(jnp.mean(values, axis=-1, keepdims=True))
    spread = lax.optimization_barrier(jnp.mean(center * center, axis=-1, keepdims=True))
    return center * lax.rsqrt(spread + norm_eps) * gain + shift

def one_row(row_items):
    query_row, key_row, value_row, seg_row = row_items
    scores = jnp.einsum('qhd,khd->hqk', query_row, key_row, precision=lax.Precision.HIGHEST)
    scores = low_back(scores * (1.0 / math.sqrt(HD)))
    same_segment = seg_row[:, None] == seg_row[None, :]
    scores = jnp.where(same_segment[None], scores, masked_score)
    shifted = jnp.exp(scores - lax.optimization_barrier(jnp.max(scores, axis=-1, keepdims=True)))
    soft_weights = shifted / lax.optimization_barrier(jnp.sum(shifted, axis=-1, keepdims=True))
    return jnp.einsum('hqk,khd->qhd', low(soft_weights), value_row, precision=lax.Precision.HIGHEST)

def attend_rows(query, key, value, seg_rows):
    shaped = (ROWS, L, H, HD)
    outputs = lax.map(jax.checkpoint(one_row), (query.reshape(shaped), key.reshape(shaped), value.reshape(shaped), seg_rows))
    return outputs.reshape(TOKENS, D)

def position(hidden, weights, seg_rows):
    query_w, key_w, value_w, out_w, inner_w, outer_w, gain_one, bias_one, gain_two, bias_two = weights
    low_in = low(hidden)
    query = low_back(low(matmul(low_in, query_w)))
    key = low_back(low(matmul(low_in, key_w)))
    value = low_back(low(matmul(low_in, value_w)))
    heads_out = low_back(low(attend_rows(query, key, value, seg_rows)))
    branch = low_back(matmul(heads_out, out_w))
    normed = layer_norm(hidden + branch, gain_one, bias_one)
    inner = low_back(matmul(low(normed), inner_w))
    active = low(jax.nn.gelu(inner))
    outer = low_back(matmul(active, outer_w))
    return layer_norm(normed + outer, gain_two, bias_two)

def reference(tokens, segment_ids, row_counts, global_count, cotangent, query_weight, key_weight, value_weight, output_weight, inner_weight, outer_weight, attn_gain, attn_bias, feed_gain, feed_bias):
    params = [w.astype(jnp.float32) for w in (query_weight, key_weight, value_weight, output_weight, inner_weight, outer_weight, attn_gain, attn_bias, feed_gain, feed_bias)]
    seg_rows = segment_ids.reshape(ROWS, L)

    def forward(hidden, *weights):
        for step in range(POSITIONS):
            hidden = position(hidden, weights, seg_rows)
        return hidden
    output, back = jax.vjp(forward, tokens.astype(jnp.float32), *params)
    valid = (jnp.arange(L)[None, :] < row_counts[:, None]).astype(jnp.float32).reshape(TOKENS)
    factor = jnp.float32(TOKENS) / global_count[0].astype(jnp.float32)
    seed_grad = cotangent * valid[:, None] * factor
    grads = back(seed_grad)
    return (output.astype(jnp.bfloat16), grads[0], grads[1], grads[2], grads[3], grads[4], grads[5], grads[6], grads[7], grads[8], grads[9], grads[10])
```

```python
import functools

import jax
import jax.numpy as jnp
from jax import lax
from jax.experimental import pallas as pl
from jax.experimental.pallas import tpu as pltpu
from jax.sharding import PartitionSpec as P

H = 8
B = 256
CHUNK = 256
norm_eps = 1e-05
masked_score = -1e30
bf16 = jnp.bfloat16
f32 = jnp.float32


def nn(left, right):
    return lax.dot_general(left, right, (((1,), (0,)), ((), ())), preferred_element_type=f32)


def nt(left, right):
    return lax.dot_general(left, right, (((1,), (1,)), ((), ())), preferred_element_type=f32)


def band(block, blocks):
    return max(0, block - 1) * B, min(blocks, block + 2) * B


def fill_bias(seg_ref, bias_ref):
    column = seg_ref[...].T[:, 0:1]
    blocks = bias_ref.shape[0] // B
    for block in range(blocks):
        low, high = band(block, blocks)
        tile = slice(block * B, (block + 1) * B)
        same = column[low:high] == seg_ref[0:1, tile]
        bias_ref[low:high, tile] = jnp.where(same, 0.0, masked_score)


def attend_head(head, size, qkv_ref, bias_ref, o_ref, lse_ref):
    blocks = qkv_ref.shape[2] // B
    rows = pl.ds(pl.multiple_of(head * size, size), size)
    key = qkv_ref[1, rows, :].T
    for block in range(blocks):
        low, high = band(block, blocks)
        tile = slice(block * B, (block + 1) * B)
        score = nn(key[low:high], qkv_ref[0, rows, tile]) + bias_ref[low:high, tile]
        top = jnp.max(score, axis=0, keepdims=True)
        weight = jnp.exp(score - top)
        total = jnp.sum(weight, axis=0, keepdims=True)
        mixed = nn(qkv_ref[2, rows, low:high], weight.astype(bf16)) * (1.0 / total)
        o_ref[rows, tile] = mixed.astype(bf16)
        lse_ref[head, :, tile] = jnp.broadcast_to(top + jnp.log(total), (8, B))


def attend_head_back(
    head, out, size, qkv_ref, o_ref, do_ref, lse_ref, bias_ref, prob_ref, ds_ref, dqkv_ref
):
    length = qkv_ref.shape[2]
    blocks = length // B
    scale = size**-0.5
    rows = pl.ds(pl.multiple_of(head * size, size), size)
    outs = pl.ds(pl.multiple_of(out * size, size), size)
    key_t = qkv_ref[1, rows, :]
    key = key_t.T
    value = qkv_ref[2, rows, :].T
    do_t = do_ref[rows, :]
    delta = jnp.sum(do_t.astype(f32) * o_ref[rows, :].astype(f32), axis=0, keepdims=True)
    for block in range(blocks):
        low, high = band(block, blocks)
        tile = slice(block * B, (block + 1) * B)
        score = nn(key[low:high], qkv_ref[0, rows, tile]) + bias_ref[low:high, tile]
        prob = jnp.exp(score - lse_ref[head, 0:1, tile])
        prob_ref[low:high, tile] = prob.astype(bf16)
        dprob = nn(value[low:high], do_t[:, tile])
        dscore = (prob * (dprob - delta[:, tile])).astype(bf16)
        ds_ref[low:high, tile] = dscore
        dq = nn(key_t[:, low:high], dscore) * scale
        dqkv_ref[0, outs, tile] = dq.astype(bf16)
    query = qkv_ref[0, rows, :].T
    do = do_t.T
    for block in range(blocks):
        low, high = band(block, blocks)
        tile = slice(block * B, (block + 1) * B)
        dv = nn(prob_ref[tile, low:high], do[low:high])
        dqkv_ref[2, outs, tile] = dv.astype(bf16).T
        dk = nn(ds_ref[tile, low:high], query[low:high])
        dqkv_ref[1, outs, tile] = dk.astype(bf16).T


def normalize(values):
    center = values - jnp.mean(values, axis=0, keepdims=True)
    spread = jnp.mean(center * center, axis=0, keepdims=True)
    scale = lax.rsqrt(spread + norm_eps)
    return center * scale, scale


def normalize_back(dn, n, scale):
    mean_one = jnp.mean(dn, axis=0, keepdims=True)
    mean_two = jnp.mean(dn * n, axis=0, keepdims=True)
    return (dn - mean_one - n * mean_two) * scale


def gelu_pair(u):
    c0 = 0.7978845608028654
    c1 = c0 * 0.044715
    square = u * u
    t = jnp.tanh(u * (c0 + c1 * square))
    half = 0.5 * u
    cdf = 0.5 + 0.5 * t
    z = u * cdf
    slope = cdf + half * (1.0 - t * t) * (c0 + (3.0 * c1) * square)
    return z, slope


def lanes_sum(values):
    return values[:, :128] + values[:, 128:]


def turn_kernel(x_ref, x_t_ref):
    x_t_ref[...] = x_ref[...].T


def attend_kernel(first, size, x_ref, w_ref, seg_ref, *refs):
    if first:
        w_t_ref = refs[0]
        w_t_ref[...] = w_ref[...].T
        refs = refs[1:]
    else:
        w_t_ref = w_ref
    qkv_ref, o_ref, lse_ref, bias_ref = refs
    rows = o_ref.shape[0]
    fill_bias(seg_ref, bias_ref)
    for at in range(0, x_ref.shape[1], B):
        cols = slice(at, at + B)
        query = nn(w_t_ref[:rows, :], x_ref[:, cols]).astype(bf16)
        qkv_ref[0, :, cols] = query * jnp.asarray(size**-0.5, bf16)
        qkv_ref[1, :, cols] = nn(w_t_ref[rows : 2 * rows, :], x_ref[:, cols]).astype(bf16)
        qkv_ref[2, :, cols] = nn(w_t_ref[2 * rows :, :], x_ref[:, cols]).astype(bf16)

    def two_heads(pair, carry):
        for one in range(2):
            attend_head(2 * pair + one, size, qkv_ref, bias_ref, o_ref, lse_ref)
        return carry

    lax.fori_loop(0, rows // size // 2, two_heads, 0)


def join_heads(oa_ref, ob_ref, o_ref):
    rows = oa_ref.shape[0]
    o_ref[:rows, :] = oa_ref[...]
    o_ref[rows:, :] = ob_ref[...]


def feed_in_kernel(
    oa_ref,
    ob_ref,
    x_ref,
    wop_ref,
    wi_ref,
    o_ref,
    wo_t_ref,
    wi_t_ref,
    y_ref,
    n1_ref,
    stat_ref,
    yr_ref,
    z_ref,
    slope_ref,
):
    width, hidden = wi_ref.shape
    join_heads(oa_ref, ob_ref, o_ref)
    wo_t_ref[...] = wop_ref[:, :width].T
    wi_t_ref[...] = wi_ref[...].T
    params = wop_ref[:, width:].astype(f32)
    gain_one, bias_one = params[:, 0:1], params[:, 1:2]
    for at in range(0, x_ref.shape[1], B):
        cols = slice(at, at + B)
        h = x_ref[:, cols].astype(f32) + nn(wo_t_ref[...], o_ref[:, cols])
        n1, s1 = normalize(h)
        n1_ref[:, cols] = n1.astype(bf16)
        stat_ref[:, cols] = jnp.broadcast_to(s1, (8, B))
        y = n1 * gain_one + bias_one
        yr_ref[:, cols] = y.astype(bf16)
        y_ref[:, cols] = y
        for f in range(0, hidden, CHUNK):
            u = nn(wi_t_ref[f : f + CHUNK, :], yr_ref[:, cols])
            z, slope = gelu_pair(u)
            z_ref[f : f + CHUNK, cols] = z.astype(bf16)
            slope_ref[f : f + CHUNK, cols] = slope.astype(bf16)


def feed_out_kernel(
    y_ref, z_ref, wop_ref, wu_ref, wu_t_ref, next_ref, x2_ref, n2_ref, stat_ref
):
    width = wu_ref.shape[1]
    wu_t_ref[...] = wu_ref[...].T
    params = wop_ref[:, width:].astype(f32)
    gain_two, bias_two = params[:, 2:3], params[:, 3:4]
    for at in range(0, y_ref.shape[1], B):
        cols = slice(at, at + B)
        h2 = y_ref[:, cols] + nn(wu_t_ref[...], z_ref[:, cols])
        n2, s2 = normalize(h2)
        n2_ref[:, cols] = n2.astype(bf16)
        stat_ref[:, cols] = jnp.broadcast_to(s2, (8, B))
        out = n2 * gain_two + bias_two
        next_ref[:, cols] = out
        x2_ref[:, cols] = out.astype(bf16)


def feed_last_kernel(
    oa_ref,
    ob_ref,
    x_ref,
    wop_ref,
    wi_ref,
    wu_ref,
    wo_t_ref,
    wi_t_ref,
    wu_t_ref,
    cot_ref,
    scale_ref,
    o_ref,
    mixed_ref,
    z_ref,
    du_ref,
    yr_ref,
    dfr_ref,
    dar_ref,
    dh_ref,
    do_ref,
    acc_ref,
    n1_ref,
    slope_ref,
    y_ref,
):
    width, hidden = wi_ref.shape
    join_heads(oa_ref, ob_ref, o_ref)
    params = wop_ref[:, width:].astype(f32)
    gain_one, bias_one = params[:, 0:1], params[:, 1:2]
    gain_two, bias_two = params[:, 2:3], params[:, 3:4]
    acc_ref[...] = jnp.zeros_like(acc_ref)

    for at in range(0, x_ref.shape[1], B):
        cols = slice(at, at + B)
        slot = at // B % 2
        h = x_ref[:, cols] + nn(wo_t_ref[...], o_ref[:, cols])
        n1, s1 = normalize(h)
        n1_ref[slot] = n1
        y = n1 * gain_one + bias_one
        yr_ref[:, cols] = y.astype(bf16)
        y_ref[slot] = y
        for f in range(0, hidden, CHUNK):
            u = nn(wi_t_ref[f : f + CHUNK, :], yr_ref[:, cols])
            z, slope = gelu_pair(u)
            z_ref[f : f + CHUNK, cols] = z.astype(bf16)
            slope_ref[slot, f : f + CHUNK, :] = slope
        h2 = y_ref[slot] + nn(wu_t_ref[...], z_ref[:, cols])
        n2, s2 = normalize(h2)
        out = n2 * gain_two + bias_two
        mixed_ref[cols, :] = out.astype(bf16).T
        grad = cot_ref[cols, :].T * scale_ref[0:1, cols]
        acc_ref[2] += lanes_sum(grad * n2)
        acc_ref[3] += lanes_sum(grad)
        dh2 = normalize_back(grad * gain_two, n2, s2)
        y_ref[slot] = dh2
        dfr_ref[:, cols] = dh2.astype(bf16)
        for f in range(0, hidden, CHUNK):
            dz = nn(wu_ref[f : f + CHUNK, :], dfr_ref[:, cols])
            du_ref[f : f + CHUNK, cols] = (dz * slope_ref[slot, f : f + CHUNK, :]).astype(bf16)
        dy = y_ref[slot] + nn(wi_ref[...], du_ref[:, cols])
        acc_ref[0] += lanes_sum(dy * n1_ref[slot])
        acc_ref[1] += lanes_sum(dy)
        dh = normalize_back(dy * gain_one, n1_ref[slot], s1)
        dh_ref[:, cols] = dh
        dar_ref[:, cols] = dh.astype(bf16)
        do_ref[:, cols] = nn(wop_ref[:, :width], dar_ref[:, cols]).astype(bf16)


def feed_back_kernel(
    g_ref,
    n1_ref,
    n2_ref,
    stat1_ref,
    stat2_ref,
    slope_ref,
    wop_ref,
    wi_ref,
    wu_ref,
    acc_in_ref,
    dh_ref,
    do_ref,
    du_ref,
    dfr_ref,
    dar_ref,
    acc_ref,
    y_ref,
):
    width, hidden = wi_ref.shape
    params = wop_ref[:, width:].astype(f32)
    gain_one, gain_two = params[:, 0:1], params[:, 2:3]
    acc_ref[...] = acc_in_ref[...]
    for at in range(0, g_ref.shape[1], B):
        cols = slice(at, at + B)
        slot = at // B % 2
        grad = g_ref[:, cols]
        n2 = n2_ref[:, cols].astype(f32)
        acc_ref[2] += lanes_sum(grad * n2)
        acc_ref[3] += lanes_sum(grad)
        dh2 = normalize_back(grad * gain_two, n2, stat2_ref[0:1, cols])
        y_ref[slot] = dh2
        dfr_ref[:, cols] = dh2.astype(bf16)
        for f in range(0, hidden, CHUNK):
            dz = nn(wu_ref[f : f + CHUNK, :], dfr_ref[:, cols])
            slope = slope_ref[f : f + CHUNK, cols].astype(f32)
            du_ref[f : f + CHUNK, cols] = (dz * slope).astype(bf16)
        dy = y_ref[slot] + nn(wi_ref[...], du_ref[:, cols])
        n1 = n1_ref[:, cols].astype(f32)
        acc_ref[0] += lanes_sum(dy * n1)
        acc_ref[1] += lanes_sum(dy)
        dh = normalize_back(dy * gain_one, n1, stat1_ref[0:1, cols])
        dh_ref[:, cols] = dh
        dar_ref[:, cols] = dh.astype(bf16)
        do_ref[:, cols] = nn(wop_ref[:, :width], dar_ref[:, cols]).astype(bf16)


def place(value, first, unit, core, keep_ref, send_ref, cols):
    for at in range(0, value.shape[0], unit):
        block = (first + at) // unit
        rows = slice(block // 2 * unit, block // 2 * unit + unit)
        part = value[at : at + unit]

        @pl.when(core == block % 2)
        def _():
            keep_ref[rows, cols] = part

        @pl.when(core != block % 2)
        def _():
            send_ref[rows, cols] = part


def outer_grad_kernel(shards, core_ref, z1_ref, z2_ref, dfr1_ref, dfr2_ref, keep_ref, send_ref):
    core = core_ref[0]
    hidden, width = z1_ref.shape[0], dfr1_ref.shape[0]
    unit = width // shards // 2
    groups = hidden // width
    per_group = hidden // shards // groups
    for first in range(0, hidden, 256):
        part = slice(first, first + 256)
        dwu = nt(z1_ref[part, :], dfr1_ref[...]) + nt(z2_ref[part, :], dfr2_ref[...])
        dwu = dwu.astype(bf16)
        for at in range(0, 256, per_group):
            block = (first + at) // per_group
            shard, group = block // groups, block % groups
            cols = slice(group * width, (group + 1) * width)
            rows = dwu[at : at + per_group]
            place(rows, shard * per_group, unit, core, keep_ref, send_ref, cols)


def inner_grad_kernel(
    shards,
    core_ref,
    yr1_ref,
    yr2_ref,
    du1_ref,
    du2_ref,
    o1_ref,
    o2_ref,
    dar1_ref,
    dar2_ref,
    acc_ref,
    keep_ref,
    send_ref,
):
    core = core_ref[0]
    width, hidden = yr1_ref.shape[0], du1_ref.shape[0]
    unit = width // shards // 2
    for first in range(0, hidden, CHUNK):
        part = slice(first, first + CHUNK)
        dwi = nt(yr1_ref[...], du1_ref[part, :]) + nt(yr2_ref[...], du2_ref[part, :])
        place(dwi.astype(bf16), 0, unit, core, keep_ref, send_ref, part)
    for first in range(0, width, CHUNK):
        part = slice(first, first + CHUNK)
        cols = slice(hidden + first, hidden + first + CHUNK)
        dwo = nt(o1_ref[...], dar1_ref[part, :]) + nt(o2_ref[...], dar2_ref[part, :])
        place(dwo.astype(bf16), 0, unit, core, keep_ref, send_ref, cols)
    lane = lax.broadcasted_iota(jnp.int32, (width, 128), 1)
    dpar = jnp.zeros((width, 128), f32)
    for i in range(4):
        dpar = jnp.where(lane == i, jnp.sum(acc_ref[i], axis=1, keepdims=True), dpar)
    last = slice(hidden + width, hidden + width + 128)
    place(dpar.astype(bf16), 0, unit, core, keep_ref, send_ref, last)


def attend_back_kernel(first, size, qkv_ref, o_ref, do_ref, lse_ref, seg_ref, dqkv_ref, *refs):
    bias_ref, prob_ref, ds_ref = refs
    rows = dqkv_ref.shape[1]
    fill_bias(seg_ref, bias_ref)
    here = slice(first, first + rows)

    def two_heads(pair, carry):
        for one in range(2):
            head = 2 * pair + one
            attend_head_back(
                head,
                head,
                size,
                qkv_ref,
                o_ref.at[here],
                do_ref.at[here],
                lse_ref,
                bias_ref,
                prob_ref.at[one],
                ds_ref.at[one],
                dqkv_ref,
            )
        return carry

    lax.fori_loop(0, rows // size // 2, two_heads, 0)


def attend_part_kernel(
    p, size, shards, qkv_ref, o_ref, do_ref, lse_ref, seg_ref, *refs
):
    grads = p % 2 == 1
    if grads:
        core_ref, x1_ref, x2_ref, before_ref, second_ref = refs[:5]
        dqkv_ref, keep_ref, send_ref, bias_ref, prob_ref, ds_ref = refs[5:]
    else:
        dqkv_ref, bias_ref, prob_ref, ds_ref = refs
    fill_bias(seg_ref, bias_ref)
    rows = qkv_ref.shape[1]
    here = slice(p // 2 * rows, (p // 2 + 1) * rows)
    for one in range(2):
        attend_head_back(
            p % 2 * 2 + one,
            one,
            size,
            qkv_ref,
            o_ref.at[here],
            do_ref.at[here],
            lse_ref,
            bias_ref,
            prob_ref.at[one],
            ds_ref.at[one],
            dqkv_ref,
        )
    if not grads:
        return
    core = core_ref[0]
    unit = x1_ref.shape[0] // shards // 2
    for i in range(3):
        joined = jnp.concatenate([before_ref[i], dqkv_ref[i]], axis=0)
        dw = nt(x1_ref[...], joined) + nt(x2_ref[...], second_ref[i])
        place(dw.astype(bf16), 0, unit, core, keep_ref, send_ref, slice(i * rows, (i + 1) * rows))


def input_kernel(turned, wa_ref, wb_ref, dh_ref, *refs):
    parts, grad_ref, join_ref = refs[:-2], refs[-2], refs[-1]
    length = dh_ref.shape[1]
    at = 0
    each = len(parts) // 2
    for group in range(2):
        for i in range(3):
            for part in parts[group * each : (group + 1) * each]:
                rows = part.shape[1]
                join_ref[at : at + rows, :] = part[i]
                at += rows
    half = at // 2
    for at in range(0, length, B):
        cols = slice(at, at + B)
        grad = dh_ref[:, cols] + nn(wa_ref[...], join_ref[:half, cols])
        grad += nn(wb_ref[...], join_ref[half:, cols])
        if turned:
            grad_ref[cols, :] = grad.T
        else:
            grad_ref[:, cols] = grad


VM = pl.BlockSpec(memory_space=pltpu.VMEM)
SM = pl.BlockSpec(memory_space=pltpu.SMEM)


def call(kernel, outs, scratch, args, specs=None, cost=10, limit=24):
    return pl.pallas_call(
        kernel,
        out_shape=[jax.ShapeDtypeStruct(shape, dtype) for shape, dtype in outs],
        in_specs=specs if specs else [VM] * len(args),
        out_specs=[VM] * len(outs),
        scratch_shapes=[pltpu.VMEM(shape, dtype) for shape, dtype in scratch],
        cost_estimate=pl.CostEstimate(
            flops=cost * 1000000000, bytes_accessed=cost * 3000000, transcendentals=0
        ),
        compiler_params=pltpu.CompilerParams(vmem_limit_bytes=limit * 2**20),
    )(*args)


def flip(value, axis, bit):
    count = lax.axis_size(axis)
    return lax.ppermute(value, axis, [(i, i ^ bit) for i in range(count)])


def bit_of(axis, bit):
    return lax.rem(lax.div(lax.axis_index(axis), bit), 2)


def bits_of(axis):
    count = lax.axis_size(axis)
    found = []
    bit = count // 2
    while bit:
        found.append((axis, bit))
        bit //= 2
    return found


def both(bit, mine, other, dim):
    low = jnp.concatenate([mine, other], axis=dim)
    high = jnp.concatenate([other, mine], axis=dim)
    return jnp.where(bit == 0, low, high)


def my_half(block):
    rows = block.shape[0] // 2
    return lax.dynamic_slice_in_dim(block, bit_of("dp", 1) * rows, rows, axis=0)[None]


def over_shards(mine):
    for axis, bit in reversed(bits_of("shard")):
        mine = both(bit_of(axis, bit), mine, flip(mine, axis, bit), 0)
    return mine


def over_cores(mine):
    full = both(bit_of("dp", 1), mine, flip(mine, "dp", 1), 1)
    return full.reshape(-1, mine.shape[-1])


class Sum:
    def __init__(self, keep, send):
        self.labels = bits_of("shard") + bits_of("dp")[:-1]
        self.cols = keep.shape[1]
        self.unit = keep.shape[0] // 2 ** len(self.labels)
        self.keep = keep
        self.sent = send
        self.came = [flip(send, "dp", 1)]
        self.value = None
        self.left = list(self.labels)

    def after(self, other):
        if self.value is None:
            self.keep = tie(self.keep, other)
        else:
            self.value = tie(self.value, other)

    def settle(self):
        if self.value is not None:
            return
        total = self.keep.astype(f32)
        for came in self.came:
            total += came.astype(f32)
        self.value = total.astype(bf16).reshape((2,) * len(self.left) + (self.unit, self.cols))

    def halve(self, axis, bit):
        self.settle()
        dim = self.left.index((axis, bit))
        me = bit_of(axis, bit)
        self.sent = lax.dynamic_index_in_dim(self.value, 1 - me, dim, keepdims=False)
        self.keep = lax.dynamic_index_in_dim(self.value, me, dim, keepdims=False)
        self.came = [flip(self.sent, axis, bit)]
        self.left.remove((axis, bit))
        self.value = None

    def masks(self):
        count = len(self.last)
        for k in range(1, 2**count):
            bits = (bit for i, (_, bit) in enumerate(self.last) if k >> (count - 1 - i) & 1)
            yield k, sum(bits)

    def scatter(self):
        self.settle()
        self.last = list(self.left)
        value = self.value.reshape(-1, self.unit, self.cols)
        me = 0
        for axis, bit in self.last:
            me = 2 * me + bit_of(axis, bit)
        self.keep = lax.dynamic_index_in_dim(value, me, 0, keepdims=False)
        self.came = []
        for k, mask in self.masks():
            send = lax.dynamic_index_in_dim(value, lax.bitwise_xor(me, k), 0, keepdims=False)
            self.came.append(flip(send, "dp", mask))
        self.left = []
        self.value = None

    def collect(self):
        self.settle()
        pieces = [self.value]
        for _, mask in self.masks():
            pieces.append(flip(self.value, "dp", mask))
        for axis, bit in reversed(self.last):
            me = bit_of(axis, bit)
            pairs = zip(pieces[::2], pieces[1::2])
            pieces = [both(me, low[None], high[None], 0) for low, high in pairs]
        self.value = pieces[0]
        self.left = list(self.last)

    def double(self, axis, bit):
        order = [label for label in self.labels if label in self.left or label == (axis, bit)]
        dim = order.index((axis, bit))
        mine = jnp.expand_dims(self.value, dim)
        self.value = both(bit_of(axis, bit), mine, flip(mine, axis, bit), dim)
        self.left = order

    def finish(self):
        self.value = self.value.reshape(-1, self.cols)
        self.other = flip(self.value, "dp", 1)

    def columns(self, first, last):
        mine, other = self.value[:, first:last], self.other[:, first:last]
        return both(bit_of("dp", 1), mine, other, 0).astype(f32)


def tie(value, *others):
    return lax.optimization_barrier((value,) + others)[0]


def compute(tokens, seg_rows, scale_rows, cotangent, blocks):
    wa_half, wb_half, wop_half, wi_half, wu_half = blocks
    length, width = tokens.shape
    hidden = wi_half.shape[2]
    size = width // H
    rows = width // 2
    shards = lax.axis_size("shard")
    core = bit_of("dp", 1).reshape(1)
    tall = ((width, length), bf16)
    tall32 = ((width, length), f32)
    wide = ((hidden, length), bf16)
    bias = ((length, length), f32)
    pair = ((2, length, length), bf16)
    heads = [((3, rows, length), bf16), ((rows, length), bf16), ((H // 2, 8, length), f32)]

    wa_mine = over_shards(wa_half)
    wa = over_cores(wa_mine)
    wb_mine = over_shards(tie(wb_half, wa_mine))
    wop_mine, wi_mine, wu_mine = (
        over_shards(tie(half, wb_mine)) for half in (wop_half, wi_half, wu_half)
    )
    (x1,) = call(turn_kernel, [tall], [], (tokens,), None, 1)
    wb = over_cores(wb_mine)
    first_attend = functools.partial(attend_kernel, True, size)
    turned = [((3 * rows, width), bf16)]
    wa_t, qkv1a, o1a, lse1a = call(first_attend, turned + heads, [bias], (x1, wa, seg_rows))
    wi, wop = over_cores(wi_mine), over_cores(wop_mine)
    seg_b = tie(seg_rows, o1a, wi_mine, wop_mine)
    wb_t, qkv1b, o1b, lse1b = call(first_attend, turned + heads, [bias], (x1, wb, seg_b))
    o1, wo_t, wi_t, y1, n11, stat11, yr1, z1, slope1 = call(
        feed_in_kernel,
        [tall, ((width, width), bf16), ((hidden, width), bf16), tall32, tall]
        + [((8, length), f32), tall, wide, wide],
        [],
        (tie(o1a, wu_mine), o1b, x1, wop, wi),
    )
    wu = over_cores(wu_mine)
    wu_t, next1, x2, n21, stat12 = call(
        feed_out_kernel,
        [((width, hidden), bf16), tall32, tall, tall, ((8, length), f32)],
        [],
        (y1, z1, wop, wu),
    )
    attend = functools.partial(attend_kernel, False, size)
    qkv2a, o2a, lse2a = call(attend, heads, [bias], (x2, wa_t, seg_rows))
    qkv2b, o2b, lse2b = call(attend, heads, [bias], (x2, wb_t, seg_rows))
    o2, mixed, z2, du2, yr2, dfr2, dar2, dh2, do2, acc = call(
        feed_last_kernel,
        [tall, ((length, width), bf16), wide, wide, tall, tall, tall, tall32, tall]
        + [((4, width, 128), f32)],
        [((2, width, B), f32), ((2, hidden, B), f32), ((2, width, B), f32)],
        (o2a, o2b, next1, wop, wi, wu, wo_t, wi_t, wu_t, cotangent, scale_rows),
    )
    back = [bias, pair, pair]
    dqkv2 = []
    for group, (qkv, lse) in enumerate(((qkv2a, lse2a), (qkv2b, lse2b))):
        kernel = functools.partial(attend_back_kernel, group * rows, size)
        dqkv2 += call(kernel, heads[:1], back, (qkv, o2, do2, lse, seg_rows))
    joined = [((3 * width, length), bf16)]
    (grad1,) = call(
        functools.partial(input_kernel, False), [tall32], joined, (wa, wb, dh2, *dqkv2), None, 3
    )
    dh1, do1, du1, dfr1, dar1, acc = call(
        feed_back_kernel,
        [tall32, tall, wide, tall, tall, ((4, width, 128), f32)],
        [((2, width, B), f32)],
        (grad1, n11, n21, stat11, stat12, slope1, wop, wi, wu, acc),
    )
    half = width // 2
    keep_u, send_u = call(
        functools.partial(outer_grad_kernel, shards),
        [((half, hidden), bf16)] * 2,
        [],
        (core, z1, z2, dfr1, dfr2),
        [SM] + [VM] * 4,
    )
    outer = Sum(keep_u, send_u)
    keep_i, send_i = call(
        functools.partial(inner_grad_kernel, shards),
        [((half, hidden + width + 128), bf16)] * 2,
        [],
        (tie(core, send_u), yr1, yr2, du1, du2, o1, o2, dar1, dar2, acc),
        [SM] + [VM] * 9,
    )
    inner = Sum(keep_i, send_i)
    parts = []

    def part(p, seg):
        qkv, lse = ((qkv1a, lse1a), (qkv1b, lse1b))[p // 2]
        args = (qkv, o1, do1, lse, seg)
        specs = [VM] * 5
        outs = [((3, 2 * size, length), bf16)]
        if p % 2:
            args += (core, x1, x2, parts[-1], dqkv2[p // 2])
            specs += [SM] + [VM] * 4
            outs += [((half, 3 * rows), bf16)] * 2
        kernel = functools.partial(attend_part_kernel, p, size, shards)
        results = call(kernel, outs, back, args, specs, 1)
        parts.append(results[0])
        return results[1:]

    z_bits, y_bit = bits_of("dp")[:-2], bits_of("dp")[-2]
    x_bits = bits_of("shard")
    for label in x_bits:
        outer.halve(*label)
    part(0, tie(seg_rows, outer.sent, send_i))
    inner.halve(*y_bit)
    first = Sum(*part(1, tie(seg_rows, inner.sent)))
    outer.halve(*y_bit)
    part(2, tie(seg_rows, outer.sent, first.sent))
    for label in x_bits:
        first.halve(*label)
    for label in x_bits:
        inner.halve(*label)
    outer.scatter()
    second = Sum(*part(3, tie(seg_rows, inner.sent, first.sent, outer.keep)))
    for one in (first, inner, outer):
        one.after(second.sent)
    outer.settle()
    (input_grad,) = call(
        functools.partial(input_kernel, True),
        [((length, width), f32)],
        joined,
        (wa, wb, tie(dh1, second.sent, outer.value), *parts),
        None,
        1,
    )
    for label in x_bits:
        second.halve(*label)
    for one in (first, inner, outer):
        one.after(second.sent)
    first.scatter()
    inner.scatter()
    outer.collect()
    second.scatter()
    first.settle()
    inner.settle()
    for one in (first, inner, outer):
        one.after(second.keep)
    first.collect()
    inner.collect()
    outer.double(*y_bit)
    second.settle()
    for one in (first, inner, outer):
        one.after(second.value)
    second.collect()
    first.finish()
    inner.double(*y_bit)
    outer.finish()
    second.finish()
    inner.finish()
    return mixed, input_grad, outer, inner, first, second


def body(
    tokens,
    segment_ids,
    row_counts,
    global_count,
    cotangent,
    query_weight,
    key_weight,
    value_weight,
    output_weight,
    inner_weight,
    outer_weight,
    attn_gain,
    attn_bias,
    feed_gain,
    feed_bias,
):
    length, width = tokens.shape
    hidden = inner_weight.shape[1]
    half = width // 2
    qkv = [my_half(w) for w in (query_weight, key_weight, value_weight)]
    stacked = jnp.stack([attn_gain, attn_bias, feed_gain, feed_bias], axis=1)
    stacked = jnp.pad(stacked, ((0, 0), (0, 124)))
    blocks = (
        jnp.concatenate([w[..., :half] for w in qkv], axis=-1),
        jnp.concatenate([w[..., half:] for w in qkv], axis=-1),
        my_half(jnp.concatenate([output_weight, stacked], axis=1)),
        my_half(inner_weight),
        my_half(outer_weight),
    )
    seg_rows = jnp.broadcast_to(segment_ids.astype(f32)[None], (8, length))
    valid = (jnp.arange(length) < row_counts[0]).astype(f32)
    tokens_total = lax.axis_size("dp") * lax.axis_size("shard") * length
    factor = jnp.float32(tokens_total) / global_count[0].astype(f32)
    scale_rows = jnp.broadcast_to((valid * factor)[None], (8, length))
    mixed, input_grad, outer, inner, first, second = compute(
        tokens, seg_rows, scale_rows, cotangent, blocks
    )
    dqkv = (
        jnp.concatenate([part.columns(at, at + half) for part in (first, second)], axis=1)
        for at in range(0, 3 * half, half)
    )
    dwu = [outer.columns(at, at + width) for at in range(0, hidden, width)]
    dpar = inner.columns(hidden + width, hidden + width + 128)
    return (
        mixed,
        input_grad,
        *dqkv,
        inner.columns(hidden, hidden + width),
        inner.columns(0, hidden),
        jnp.concatenate(dwu, axis=0),
        dpar[:, 0],
        dpar[:, 1],
        dpar[:, 2],
        dpar[:, 3],
    )


def solution(mesh):
    rows = P(("dp", "shard"))
    rows_two = P(("dp", "shard"), None)
    two = P("shard", None)
    one = P("shard")
    in_specs = (rows_two, rows, rows, P(), rows_two) + (two,) * 6 + (one,) * 4
    out_specs = (rows_two, rows_two) + (two,) * 6 + (one,) * 4
    return jax.shard_map(body, mesh=mesh, in_specs=in_specs, out_specs=out_specs, check_vma=False)
```

```python
import functools

import jax
import jax.numpy as jnp
from jax import lax
from jax.experimental import pallas as pl
from jax.experimental.pallas import tpu as pltpu
from jax.sharding import PartitionSpec as P

H = 8
B = 256
CHUNK = 256
norm_eps = 1e-05
masked_score = -1e30
bf16 = jnp.bfloat16
f32 = jnp.float32


def nn(left, right):
    return lax.dot_general(left, right, (((1,), (0,)), ((), ())), preferred_element_type=f32)


def nt(left, right):
    return lax.dot_general(left, right, (((1,), (1,)), ((), ())), preferred_element_type=f32)


def band(block, blocks):
    return max(0, block - 1) * B, min(blocks, block + 2) * B


def key_blocks(block, blocks):
    low, high = band(block, blocks)
    for at in range(low, high, B):
        step = (block * B - at) // B + 1
        yield slice(at, at + B), slice(step * B, (step + 1) * B), slice(at - low, at - low + B)


def query_blocks(block, blocks):
    low, high = band(block, blocks)
    first = low - block * B + B
    return slice(low, high), slice(first, first + high - low)


def fill_bias(seg_ref, bias_ref):
    column = seg_ref[...].T[:, 0:1]
    blocks = bias_ref.shape[0] // B
    for block in range(blocks):
        row = seg_ref[0:1, block * B : (block + 1) * B]
        for keys, cols, _ in key_blocks(block, blocks):
            bias_ref[keys, cols] = jnp.where(column[keys] == row, 0.0, masked_score)


def bias_of(bias_ref, block, blocks):
    parts = [bias_ref[keys, cols] for keys, cols, _ in key_blocks(block, blocks)]
    return jnp.concatenate(parts, axis=0)


def attend_head(head, size, qkv_ref, bias_ref, o_ref, lse_ref):
    blocks = qkv_ref.shape[2] // B
    rows = pl.ds(pl.multiple_of(head * size, size), size)
    key = qkv_ref[1, rows, :].T
    for block in range(blocks):
        low, high = band(block, blocks)
        tile = slice(block * B, (block + 1) * B)
        score = nn(key[low:high], qkv_ref[0, rows, tile]) + bias_of(bias_ref, block, blocks)
        top = jnp.max(score, axis=0, keepdims=True)
        weight = jnp.exp(score - top)
        total = jnp.sum(weight, axis=0, keepdims=True)
        mixed = nn(qkv_ref[2, rows, low:high], weight.astype(bf16)) * (1.0 / total)
        o_ref[rows, tile] = mixed.astype(bf16)
        lse_ref[head, :, tile] = jnp.broadcast_to(top + jnp.log(total), (8, B))


def attend_head_back(
    head, out, size, qkv_ref, o_ref, do_ref, lse_ref, bias_ref, prob_ref, ds_ref, dqkv_ref
):
    length = qkv_ref.shape[2]
    blocks = length // B
    scale = size**-0.5
    rows = pl.ds(pl.multiple_of(head * size, size), size)
    outs = pl.ds(pl.multiple_of(out * size, size), size)
    key_t = qkv_ref[1, rows, :]
    key = key_t.T
    value = qkv_ref[2, rows, :].T
    do_t = do_ref[rows, :]
    delta = jnp.sum(do_t.astype(f32) * o_ref[rows, :].astype(f32), axis=0, keepdims=True)
    for block in range(blocks):
        low, high = band(block, blocks)
        tile = slice(block * B, (block + 1) * B)
        score = nn(key[low:high], qkv_ref[0, rows, tile]) + bias_of(bias_ref, block, blocks)
        prob = jnp.exp(score - lse_ref[head, 0:1, tile])
        prob_low = prob.astype(bf16)
        dprob = nn(value[low:high], do_t[:, tile])
        dscore = (prob * (dprob - delta[:, tile])).astype(bf16)
        for keys, cols, part in key_blocks(block, blocks):
            prob_ref[keys, cols] = prob_low[part]
            ds_ref[keys, cols] = dscore[part]
        dq = nn(key_t[:, low:high], dscore) * scale
        dqkv_ref[0, outs, tile] = dq.astype(bf16)
    query = qkv_ref[0, rows, :].T
    do = do_t.T
    for block in range(blocks):
        tile = slice(block * B, (block + 1) * B)
        queries, cols = query_blocks(block, blocks)
        dv = nn(prob_ref[tile, cols], do[queries])
        dqkv_ref[2, outs, tile] = dv.astype(bf16).T
        dk = nn(ds_ref[tile, cols], query[queries])
        dqkv_ref[1, outs, tile] = dk.astype(bf16).T


def normalize(values):
    center = values - jnp.mean(values, axis=0, keepdims=True)
    spread = jnp.mean(center * center, axis=0, keepdims=True)
    scale = lax.rsqrt(spread + norm_eps)
    return center * scale, scale


def normalize_back(dn, n, scale):
    mean_one = jnp.mean(dn, axis=0, keepdims=True)
    mean_two = jnp.mean(dn * n, axis=0, keepdims=True)
    return (dn - mean_one - n * mean_two) * scale


def gelu_pair(u):
    c0 = 0.7978845608028654
    c1 = c0 * 0.044715
    square = u * u
    t = jnp.tanh(u * (c0 + c1 * square))
    half = 0.5 * u
    cdf = 0.5 + 0.5 * t
    z = u * cdf
    slope = cdf + half * (1.0 - t * t) * (c0 + (3.0 * c1) * square)
    return z, slope


def lanes_sum(values):
    return values[:, :128] + values[:, 128:]


def turn_kernel(x_ref, x_t_ref):
    x_t_ref[...] = x_ref[...].T


def attend_kernel(first, size, x_ref, w_ref, seg_ref, *refs):
    if first:
        w_t_ref = refs[0]
        w_t_ref[...] = w_ref[...].T
        refs = refs[1:]
    else:
        w_t_ref = w_ref
    qkv_ref, o_ref, lse_ref, bias_ref = refs
    rows = o_ref.shape[0]
    fill_bias(seg_ref, bias_ref)
    for at in range(0, x_ref.shape[1], B):
        cols = slice(at, at + B)
        query = nn(w_t_ref[:rows, :], x_ref[:, cols]).astype(bf16)
        qkv_ref[0, :, cols] = query * jnp.asarray(size**-0.5, bf16)
        qkv_ref[1, :, cols] = nn(w_t_ref[rows : 2 * rows, :], x_ref[:, cols]).astype(bf16)
        qkv_ref[2, :, cols] = nn(w_t_ref[2 * rows :, :], x_ref[:, cols]).astype(bf16)

    def two_heads(pair, carry):
        for one in range(2):
            attend_head(2 * pair + one, size, qkv_ref, bias_ref, o_ref, lse_ref)
        return carry

    lax.fori_loop(0, rows // size // 2, two_heads, 0)


def join_heads(oa_ref, ob_ref, o_ref):
    rows = oa_ref.shape[0]
    o_ref[:rows, :] = oa_ref[...]
    o_ref[rows:, :] = ob_ref[...]


def z_copy(z_ref, z_hbm_ref, sem_ref, step):
    slot = step % 2
    there = z_hbm_ref.at[:, step * B : (step + 1) * B]
    return pltpu.make_async_copy(z_ref.at[slot], there, sem_ref.at[slot])


def feed_in_kernel(
    oa_ref,
    ob_ref,
    x_ref,
    wop_ref,
    wi_ref,
    o_ref,
    wo_t_ref,
    wi_t_ref,
    y_ref,
    n1_ref,
    stat_ref,
    yr_ref,
    z_hbm_ref,
    slope_ref,
    z_ref,
    sem_ref,
):
    width, hidden = wi_ref.shape
    join_heads(oa_ref, ob_ref, o_ref)
    wo_t_ref[...] = wop_ref[:, :width].T
    wi_t_ref[...] = wi_ref[...].T
    params = wop_ref[:, width:].astype(f32)
    gain_one, bias_one = params[:, 0:1], params[:, 1:2]
    copies = []
    for at in range(0, x_ref.shape[1], B):
        cols = slice(at, at + B)
        step = at // B
        copies.append(z_copy(z_ref, z_hbm_ref, sem_ref, step))
        if step > 1:
            copies[step - 2].wait()
        h = x_ref[:, cols].astype(f32) + nn(wo_t_ref[...], o_ref[:, cols])
        n1, s1 = normalize(h)
        n1_ref[:, cols] = n1.astype(bf16)
        stat_ref[:, cols] = jnp.broadcast_to(s1, (8, B))
        y = n1 * gain_one + bias_one
        yr_ref[:, cols] = y.astype(bf16)
        y_ref[:, cols] = y
        for f in range(0, hidden, CHUNK):
            u = nn(wi_t_ref[f : f + CHUNK, :], yr_ref[:, cols])
            z, slope = gelu_pair(u)
            z_ref[step % 2, f : f + CHUNK, :] = z.astype(bf16)
            slope_ref[f : f + CHUNK, cols] = slope.astype(bf16)
        copies[step].start()
    for copy in copies[-2:]:
        copy.wait()


def feed_out_kernel(
    y_ref, z_hbm_ref, wop_ref, wu_ref, wu_t_ref, next_ref, x2_ref, n2_ref, stat_ref, z_ref, sem_ref
):
    width = wu_ref.shape[1]
    length = y_ref.shape[1]

    def fetch(step):
        slot = step % 2
        there = z_hbm_ref.at[:, step * B : (step + 1) * B]
        return pltpu.make_async_copy(there, z_ref.at[slot], sem_ref.at[slot])

    copies = [fetch(step) for step in range(length // B)]
    copies[0].start()
    wu_t_ref[...] = wu_ref[...].T
    params = wop_ref[:, width:].astype(f32)
    gain_two, bias_two = params[:, 2:3], params[:, 3:4]
    for at in range(0, y_ref.shape[1], B):
        cols = slice(at, at + B)
        step = at // B
        if step + 1 < len(copies):
            copies[step + 1].start()
        copies[step].wait()
        h2 = y_ref[:, cols] + nn(wu_t_ref[...], z_ref[step % 2])
        n2, s2 = normalize(h2)
        n2_ref[:, cols] = n2.astype(bf16)
        stat_ref[:, cols] = jnp.broadcast_to(s2, (8, B))
        out = n2 * gain_two + bias_two
        next_ref[:, cols] = out
        x2_ref[:, cols] = out.astype(bf16)


def feed_last_kernel(
    oa_ref,
    ob_ref,
    x_ref,
    wop_ref,
    wi_ref,
    wu_ref,
    wo_t_ref,
    wi_t_ref,
    wu_t_ref,
    cot_ref,
    scale_ref,
    o_ref,
    mixed_ref,
    z_hbm_ref,
    du_ref,
    yr_ref,
    dfr_ref,
    dar_ref,
    dh_ref,
    do_ref,
    acc_ref,
    n1_ref,
    z_ref,
    sem_ref,
):
    width, hidden = wi_ref.shape
    join_heads(oa_ref, ob_ref, o_ref)
    params = wop_ref[:, width:].astype(f32)
    gain_one, bias_one = params[:, 0:1], params[:, 1:2]
    gain_two, bias_two = params[:, 2:3], params[:, 3:4]
    acc_ref[...] = jnp.zeros_like(acc_ref)

    copies = []
    for at in range(0, x_ref.shape[1], B):
        cols = slice(at, at + B)
        step = at // B
        slot = step % 2
        copies.append(z_copy(z_ref, z_hbm_ref, sem_ref, step))
        if step > 1:
            copies[step - 2].wait()
        h = x_ref[:, cols] + nn(wo_t_ref[...], o_ref[:, cols])
        n1, s1 = normalize(h)
        n1_ref[slot] = n1
        y = n1 * gain_one + bias_one
        yr_ref[:, cols] = y.astype(bf16)
        dh_ref[:, cols] = y
        for f in range(0, hidden, CHUNK):
            u = nn(wi_t_ref[f : f + CHUNK, :], yr_ref[:, cols])
            z, slope = gelu_pair(u)
            z_ref[slot, f : f + CHUNK, :] = z.astype(bf16)
            du_ref[f : f + CHUNK, cols] = slope.astype(bf16)
        copies[step].start()
        h2 = dh_ref[:, cols] + nn(wu_t_ref[...], z_ref[slot])
        n2, s2 = normalize(h2)
        out = n2 * gain_two + bias_two
        mixed_ref[cols, :] = out.astype(bf16).T
        grad = cot_ref[cols, :].T * scale_ref[0:1, cols]
        acc_ref[2] += lanes_sum(grad * n2)
        acc_ref[3] += lanes_sum(grad)
        dh2 = normalize_back(grad * gain_two, n2, s2)
        dh_ref[:, cols] = dh2
        dfr_ref[:, cols] = dh2.astype(bf16)
        for f in range(0, hidden, CHUNK):
            dz = nn(wu_ref[f : f + CHUNK, :], dfr_ref[:, cols])
            slope = du_ref[f : f + CHUNK, cols].astype(f32)
            du_ref[f : f + CHUNK, cols] = (dz * slope).astype(bf16)
        dy = dh_ref[:, cols] + nn(wi_ref[...], du_ref[:, cols])
        acc_ref[0] += lanes_sum(dy * n1_ref[slot])
        acc_ref[1] += lanes_sum(dy)
        dh = normalize_back(dy * gain_one, n1_ref[slot], s1)
        dh_ref[:, cols] = dh
        dar_ref[:, cols] = dh.astype(bf16)
        do_ref[:, cols] = nn(wop_ref[:, :width], dar_ref[:, cols]).astype(bf16)
    for copy in copies[-2:]:
        copy.wait()


def feed_back_kernel(
    g_ref,
    n1_ref,
    n2_ref,
    stat1_ref,
    stat2_ref,
    slope_ref,
    wop_ref,
    wi_ref,
    wu_ref,
    acc_in_ref,
    dh_ref,
    do_ref,
    du_ref,
    dfr_ref,
    dar_ref,
    acc_ref,
):
    width, hidden = wi_ref.shape
    params = wop_ref[:, width:].astype(f32)
    gain_one, gain_two = params[:, 0:1], params[:, 2:3]
    acc_ref[...] = acc_in_ref[...]
    for at in range(0, g_ref.shape[1], B):
        cols = slice(at, at + B)
        grad = g_ref[:, cols]
        n2 = n2_ref[:, cols].astype(f32)
        acc_ref[2] += lanes_sum(grad * n2)
        acc_ref[3] += lanes_sum(grad)
        dh2 = normalize_back(grad * gain_two, n2, stat2_ref[0:1, cols])
        dh_ref[:, cols] = dh2
        dfr_ref[:, cols] = dh2.astype(bf16)
        for f in range(0, hidden, CHUNK):
            dz = nn(wu_ref[f : f + CHUNK, :], dfr_ref[:, cols])
            slope = slope_ref[f : f + CHUNK, cols].astype(f32)
            du_ref[f : f + CHUNK, cols] = (dz * slope).astype(bf16)
        dy = dh_ref[:, cols] + nn(wi_ref[...], du_ref[:, cols])
        n1 = n1_ref[:, cols].astype(f32)
        acc_ref[0] += lanes_sum(dy * n1)
        acc_ref[1] += lanes_sum(dy)
        dh = normalize_back(dy * gain_one, n1, stat1_ref[0:1, cols])
        dh_ref[:, cols] = dh
        dar_ref[:, cols] = dh.astype(bf16)
        do_ref[:, cols] = nn(wop_ref[:, :width], dar_ref[:, cols]).astype(bf16)


def place(value, first, unit, core, keep_ref, send_ref, cols):
    for at in range(0, value.shape[0], unit):
        block = (first + at) // unit
        rows = slice(block // 2 * unit, block // 2 * unit + unit)
        part = value[at : at + unit]

        @pl.when(core == block % 2)
        def _():
            keep_ref[rows, cols] = part

        @pl.when(core != block % 2)
        def _():
            send_ref[rows, cols] = part


def outer_grad_kernel(
    shards,
    core_ref,
    z1_hbm_ref,
    z2_hbm_ref,
    dfr1_ref,
    dfr2_ref,
    keep_ref,
    send_ref,
    z1_ref,
    z2_ref,
    sem_ref,
):
    core = core_ref[0]
    hidden, width = z1_hbm_ref.shape[0], dfr1_ref.shape[0]
    unit = width // shards // 2
    groups = hidden // width
    per_group = hidden // shards // groups

    def fetch(step, which, hbm_ref, vmem_ref):
        slot = step % 2
        there = hbm_ref.at[step * 256 : (step + 1) * 256]
        return pltpu.make_async_copy(there, vmem_ref.at[slot], sem_ref.at[which, slot])

    copies = [
        (fetch(step, 0, z1_hbm_ref, z1_ref), fetch(step, 1, z2_hbm_ref, z2_ref))
        for step in range(hidden // 256)
    ]
    for copy in copies[0]:
        copy.start()
    for step in range(hidden // 256):
        first = step * 256
        if step + 1 < len(copies):
            for copy in copies[step + 1]:
                copy.start()
        for copy in copies[step]:
            copy.wait()
        slot = step % 2
        dwu = nt(z1_ref[slot], dfr1_ref[...]) + nt(z2_ref[slot], dfr2_ref[...])
        dwu = dwu.astype(bf16)
        for at in range(0, 256, per_group):
            block = (first + at) // per_group
            shard, group = block // groups, block % groups
            cols = slice(group * width, (group + 1) * width)
            rows = dwu[at : at + per_group]
            place(rows, shard * per_group, unit, core, keep_ref, send_ref, cols)


def inner_grad_kernel(
    shards,
    core_ref,
    yr1_ref,
    yr2_ref,
    du1_ref,
    du2_ref,
    o1_ref,
    o2_ref,
    dar1_ref,
    dar2_ref,
    acc_ref,
    keep_ref,
    send_ref,
):
    core = core_ref[0]
    width, hidden = yr1_ref.shape[0], du1_ref.shape[0]
    unit = width // shards // 2
    for first in range(0, hidden, CHUNK):
        part = slice(first, first + CHUNK)
        dwi_t = nt(du1_ref[part, :], yr1_ref[...]) + nt(du2_ref[part, :], yr2_ref[...])
        place(dwi_t.astype(bf16).T, 0, unit, core, keep_ref, send_ref, part)
    for first in range(0, width, CHUNK):
        part = slice(first, first + CHUNK)
        cols = slice(hidden + first, hidden + first + CHUNK)
        dwo = nt(o1_ref[...], dar1_ref[part, :]) + nt(o2_ref[...], dar2_ref[part, :])
        place(dwo.astype(bf16), 0, unit, core, keep_ref, send_ref, cols)
    lane = lax.broadcasted_iota(jnp.int32, (width, 128), 1)
    dpar = jnp.zeros((width, 128), f32)
    for i in range(4):
        dpar = jnp.where(lane == i, jnp.sum(acc_ref[i], axis=1, keepdims=True), dpar)
    last = slice(hidden + width, hidden + width + 128)
    place(dpar.astype(bf16), 0, unit, core, keep_ref, send_ref, last)


def attend_back_kernel(first, size, qkv_ref, o_ref, do_ref, lse_ref, seg_ref, dqkv_ref, *refs):
    bias_ref, prob_ref, ds_ref = refs
    rows = dqkv_ref.shape[1]
    fill_bias(seg_ref, bias_ref)
    here = slice(first, first + rows)

    def two_heads(pair, carry):
        for one in range(2):
            head = 2 * pair + one
            attend_head_back(
                head,
                head,
                size,
                qkv_ref,
                o_ref.at[here],
                do_ref.at[here],
                lse_ref,
                bias_ref,
                prob_ref.at[one],
                ds_ref.at[one],
                dqkv_ref,
            )
        return carry

    lax.fori_loop(0, rows // size // 2, two_heads, 0)


def attend_part_kernel(
    p, size, shards, qkv_ref, o_ref, do_ref, lse_ref, seg_ref, *refs
):
    grads = p % 2 == 1
    if grads:
        core_ref, x1_ref, x2_ref, before_ref, second_ref = refs[:5]
        dqkv_ref, keep_ref, send_ref, bias_ref, prob_ref, ds_ref = refs[5:]
    else:
        dqkv_ref, bias_ref, prob_ref, ds_ref = refs
    fill_bias(seg_ref, bias_ref)
    rows = qkv_ref.shape[1]
    here = slice(p // 2 * rows, (p // 2 + 1) * rows)
    for one in range(2):
        attend_head_back(
            p % 2 * 2 + one,
            one,
            size,
            qkv_ref,
            o_ref.at[here],
            do_ref.at[here],
            lse_ref,
            bias_ref,
            prob_ref.at[one],
            ds_ref.at[one],
            dqkv_ref,
        )
    if not grads:
        return
    core = core_ref[0]
    unit = x1_ref.shape[0] // shards // 2
    for i in range(3):
        joined = jnp.concatenate([before_ref[i], dqkv_ref[i]], axis=0)
        dw = nt(x1_ref[...], joined) + nt(x2_ref[...], second_ref[i])
        place(dw.astype(bf16), 0, unit, core, keep_ref, send_ref, slice(i * rows, (i + 1) * rows))


def input_kernel(turned, wa_ref, wb_ref, dh_ref, *refs):
    parts, grad_ref, join_ref = refs[:-2], refs[-2], refs[-1]
    length = dh_ref.shape[1]
    at = 0
    each = len(parts) // 2
    for group in range(2):
        for i in range(3):
            for part in parts[group * each : (group + 1) * each]:
                rows = part.shape[1]
                join_ref[at : at + rows, :] = part[i]
                at += rows
    half = at // 2
    for at in range(0, length, B):
        cols = slice(at, at + B)
        grad = dh_ref[:, cols] + nn(wa_ref[...], join_ref[:half, cols])
        grad += nn(wb_ref[...], join_ref[half:, cols])
        if turned:
            grad_ref[cols, :] = grad.T
        else:
            grad_ref[:, cols] = grad


VM = pl.BlockSpec(memory_space=pltpu.VMEM)
SM = pl.BlockSpec(memory_space=pltpu.SMEM)
HB = pl.BlockSpec(memory_space=pltpu.HBM)


def call(kernel, outs, scratch, args, specs=None, cost=10, limit=8, far=(), alias={}):
    return pl.pallas_call(
        kernel,
        out_shape=[jax.ShapeDtypeStruct(shape, dtype) for shape, dtype in outs],
        in_specs=specs if specs else [VM] * len(args),
        out_specs=[HB if i in far else VM for i in range(len(outs))],
        scratch_shapes=[pltpu.VMEM(*one) if isinstance(one, tuple) else one for one in scratch],
        input_output_aliases=alias,
        cost_estimate=pl.CostEstimate(
            flops=cost * 1000000000, bytes_accessed=cost * 3000000, transcendentals=0
        ),
        compiler_params=pltpu.CompilerParams(vmem_limit_bytes=limit * 2**20),
    )(*args)


def flip(value, axis, bit):
    count = lax.axis_size(axis)
    return lax.ppermute(value, axis, [(i, i ^ bit) for i in range(count)])


def bit_of(axis, bit):
    return lax.rem(lax.div(lax.axis_index(axis), bit), 2)


def bits_of(axis):
    count = lax.axis_size(axis)
    found = []
    bit = count // 2
    while bit:
        found.append((axis, bit))
        bit //= 2
    return found


def both(bit, mine, other, dim):
    low = jnp.concatenate([mine, other], axis=dim)
    high = jnp.concatenate([other, mine], axis=dim)
    return jnp.where(bit == 0, low, high)


def my_half(block):
    rows = block.shape[0] // 2
    return lax.dynamic_slice_in_dim(block, bit_of("dp", 1) * rows, rows, axis=0)[None]


def my_quarter(block):
    rows = block.shape[0] // 4
    place = 2 * bit_of("dp", 1) + bit_of("dp", 2)
    return lax.dynamic_slice_in_dim(block, place * rows, rows, axis=0)[None]


def over_shards(mine):
    for axis, bit in reversed(bits_of("shard")):
        mine = both(bit_of(axis, bit), mine, flip(mine, axis, bit), 0)
    return mine


def over_cores(mine):
    full = both(bit_of("dp", 1), mine, flip(mine, "dp", 1), 1)
    return full.reshape(-1, mine.shape[-1])


class Sum:
    def __init__(self, keep, send):
        self.labels = bits_of("shard") + bits_of("dp")[:-1]
        self.cols = keep.shape[1]
        self.unit = keep.shape[0] // 2 ** len(self.labels)
        self.keep = keep
        self.sent = send
        self.came = [flip(send, "dp", 1)]
        self.value = None
        self.left = list(self.labels)

    def after(self, other):
        if self.value is None:
            self.keep = tie(self.keep, other)
        else:
            self.value = tie(self.value, other)

    def settle(self):
        if self.value is not None:
            return
        total = self.keep.astype(f32)
        for came in self.came:
            total += came.astype(f32)
        self.value = total.astype(bf16).reshape((2,) * len(self.left) + (self.unit, self.cols))

    def halve(self, axis, bit):
        self.settle()
        dim = self.left.index((axis, bit))
        me = bit_of(axis, bit)
        self.sent = lax.dynamic_index_in_dim(self.value, 1 - me, dim, keepdims=False)
        self.keep = lax.dynamic_index_in_dim(self.value, me, dim, keepdims=False)
        self.came = [flip(self.sent, axis, bit)]
        self.left.remove((axis, bit))
        self.value = None

    def masks(self):
        count = len(self.last)
        for k in range(1, 2**count):
            bits = (bit for i, (_, bit) in enumerate(self.last) if k >> (count - 1 - i) & 1)
            yield k, sum(bits)

    def scatter(self):
        self.settle()
        self.last = list(self.left)
        value = self.value.reshape(-1, self.unit, self.cols)
        me = 0
        for axis, bit in self.last:
            me = 2 * me + bit_of(axis, bit)
        self.keep = lax.dynamic_index_in_dim(value, me, 0, keepdims=False)
        self.came = []
        for k, mask in self.masks():
            send = lax.dynamic_index_in_dim(value, lax.bitwise_xor(me, k), 0, keepdims=False)
            self.came.append(flip(send, "dp", mask))
        self.left = []
        self.value = None

    def collect(self):
        self.settle()
        pieces = [self.value]
        for _, mask in self.masks():
            pieces.append(flip(self.value, "dp", mask))
        for axis, bit in reversed(self.last):
            me = bit_of(axis, bit)
            pairs = zip(pieces[::2], pieces[1::2])
            pieces = [both(me, low[None], high[None], 0) for low, high in pairs]
        self.value = pieces[0]
        self.left = list(self.last)

    def double(self, axis, bit):
        order = [label for label in self.labels if label in self.left or label == (axis, bit)]
        dim = order.index((axis, bit))
        mine = jnp.expand_dims(self.value, dim)
        self.value = both(bit_of(axis, bit), mine, flip(mine, axis, bit), dim)
        self.left = order

    def finish(self):
        self.value = self.value.reshape(-1, self.cols)
        self.other = flip(self.value, "dp", 1)

    def columns(self, first, last):
        mine, other = self.value[:, first:last], self.other[:, first:last]
        return both(bit_of("dp", 1), mine, other, 0).astype(f32)


def join(*sums):
    for one in sums:
        one.settle()
    joined = object.__new__(Sum)
    joined.labels, joined.unit, joined.left = sums[0].labels, sums[0].unit, sums[0].left
    joined.last = getattr(sums[0], "last", None)
    joined.cols = sum(one.cols for one in sums)
    joined.value = jnp.concatenate([one.value for one in sums], axis=-1)
    return joined


def tie_all(*values):
    return lax.optimization_barrier(values)[:-1]


def tie(value, *others):
    return lax.optimization_barrier((value,) + others)[0]


def compute(tokens, seg_rows, scale_rows, cotangent, blocks):
    wa_half, wb_half, wop_half, wi_half, wu_part = blocks
    length, width = tokens.shape
    hidden = wi_half.shape[2]
    size = width // H
    rows = width // 2
    shards = lax.axis_size("shard")
    core = bit_of("dp", 1).reshape(1)
    tall = ((width, length), bf16)
    tall32 = ((width, length), f32)
    wide = ((hidden, length), bf16)
    bias = ((length, 3 * B), f32)
    pair = ((2, length, 3 * B), bf16)
    z_tiles = [((2, hidden, B), bf16), pltpu.SemaphoreType.DMA((2,))]
    heads = [((3, rows, length), bf16), ((rows, length), bf16), ((H // 2, 8, length), f32)]

    wa_mine = over_shards(wa_half)
    wa = over_cores(wa_mine)
    wb_mine, wop_mine, wi_mine, wu_mine = (
        over_shards(tie(part, wa_mine)) for part in (wb_half, wop_half, wi_half, wu_part)
    )
    (x1,) = call(turn_kernel, [tall], [], (tokens,), None, 1)
    first_attend = functools.partial(attend_kernel, True, size)
    turned = [((3 * rows, width), bf16)]
    wa_t, qkv1a, o1a, lse1a = call(first_attend, turned + heads, [bias], (x1, wa, seg_rows), limit=8)
    wb_mine, wop_mine, wi_mine, wu_mine = tie_all(wb_mine, wop_mine, wi_mine, wu_mine, o1a)
    wb = over_cores(wb_mine)
    wi, wop = over_cores(wi_mine), over_cores(wop_mine)
    wu_mine = both(bit_of("dp", 2), wu_mine, flip(wu_mine, "dp", 2), 1)
    seg_b = tie(seg_rows, wi_mine, wop_mine)
    wb_t, qkv1b, o1b, lse1b = call(first_attend, turned + heads, [bias], (x1, wb, seg_b), limit=8)
    o1, wo_t, wi_t, y1, n11, stat11, yr1, z1, slope1 = call(
        feed_in_kernel,
        [tall, ((width, width), bf16), ((hidden, width), bf16), tall32, tall]
        + [((8, length), f32), tall, wide, wide],
        z_tiles,
        (tie(o1a, wu_mine), o1b, x1, wop, wi),
        far=(7,),
    )
    wu = over_cores(wu_mine)
    wu_t, next1, x2, n21, stat12 = call(
        feed_out_kernel,
        [((width, hidden), bf16), tall32, tall, tall, ((8, length), f32)],
        z_tiles,
        (y1, z1, wop, wu),
        [VM, HB, VM, VM],
    )
    attend = functools.partial(attend_kernel, False, size)
    qkv2a, o2a, lse2a = call(attend, heads, [bias], (x2, wa_t, seg_rows), limit=8)
    qkv2b, o2b, lse2b = call(attend, heads, [bias], (x2, wb_t, seg_rows), limit=8)
    o2, mixed, z2, du2, yr2, dfr2, dar2, dh2, do2, acc = call(
        feed_last_kernel,
        [tall, ((length, width), bf16), wide, wide, tall, tall, tall, tall32, tall]
        + [((4, width, 128), f32)],
        [((2, width, B), f32)] + z_tiles,
        (o2a, o2b, next1, wop, wi, wu, wo_t, wi_t, wu_t, cotangent, scale_rows),
        limit=12,
        far=(2,),
    )
    back = [bias, pair, pair]
    dqkv2 = []
    for group, (qkv, lse) in enumerate(((qkv2a, lse2a), (qkv2b, lse2b))):
        kernel = functools.partial(attend_back_kernel, group * rows, size)
        dqkv2 += call(kernel, heads[:1], back, (qkv, o2, do2, lse, seg_rows), limit=14)
    joined = [((3 * width, length), bf16)]
    (grad1,) = call(
        functools.partial(input_kernel, False), [tall32], joined, (wa, wb, dh2, *dqkv2), None, 3, 8
    )
    dh1, do1, du1, dfr1, dar1, acc = call(
        feed_back_kernel,
        [tall32, tall, wide, tall, tall, ((4, width, 128), f32)],
        [],
        (grad1, n11, n21, stat11, stat12, slope1, wop, wi, wu, acc),
        alias={5: 2, 9: 5},
    )
    half = width // 2
    keep_i, send_i = call(
        functools.partial(inner_grad_kernel, shards),
        [((half, hidden + width + 128), bf16)] * 2,
        [],
        (core, yr1, yr2, du1, du2, o1, o2, dar1, dar2, acc),
        [SM] + [VM] * 9,
    )
    inner = Sum(keep_i, send_i)
    keep_u, send_u = call(
        functools.partial(outer_grad_kernel, shards),
        [((half, hidden), bf16)] * 2,
        [((2, 256, length), bf16)] * 2 + [pltpu.SemaphoreType.DMA((2, 2))],
        (tie(core, send_i), z1, z2, dfr1, dfr2),
        [SM, HB, HB, VM, VM],
    )
    parts = []

    def part(p, seg):
        qkv, lse = ((qkv1a, lse1a), (qkv1b, lse1b))[p // 2]
        args = (qkv, o1, do1, lse, seg)
        specs = [VM] * 5
        outs = [((3, 2 * size, length), bf16)]
        if p % 2:
            args += (core, x1, x2, parts[-1], dqkv2[p // 2])
            specs += [SM] + [VM] * 4
            outs += [((half, 3 * rows), bf16)] * 2
        kernel = functools.partial(attend_part_kernel, p, size, shards)
        results = call(kernel, outs, back, args, specs, 15, 14)
        parts.append(results[0])
        return results[1:]

    y_bit = bits_of("dp")[-2]
    x_bits = bits_of("shard")
    inner.after(send_u)
    for label in x_bits:
        inner.halve(*label)
    outer = Sum(keep_u, tie(send_u, inner.sent))
    part(0, tie(seg_rows, inner.sent))
    outer.after(parts[0])
    outer.halve(*y_bit)
    first = Sum(*part(1, tie(seg_rows, outer.sent)))
    inner.after(parts[1])
    inner.halve(*y_bit)
    outer.after(parts[1])
    for label in x_bits:
        outer.halve(*label)
    part(2, tie(seg_rows, inner.sent, outer.sent, first.sent))
    for one in (first, inner, outer):
        one.after(parts[2])
    for label in x_bits:
        first.halve(*label)
    inner.scatter()
    outer.scatter()
    second = Sum(*part(3, tie(seg_rows, inner.keep, outer.keep, first.sent)))
    for one in (first, inner, outer):
        one.after(second.sent)
    feed = join(inner, outer)
    (input_grad,) = call(
        functools.partial(input_kernel, True),
        [((length, width), f32)],
        joined,
        (wa, wb, tie(dh1, second.sent, feed.value), *parts),
        None,
        5,
        10,
    )
    feed.collect()
    for label in x_bits:
        second.halve(*label)
    heads = join(first, second)
    heads.halve(*y_bit)
    feed.after(heads.sent)
    feed.double(*y_bit)
    heads.scatter()
    heads.settle()
    feed.after(heads.value)
    heads.collect()
    feed.finish()
    heads.double(*y_bit)
    heads.finish()
    return mixed, input_grad, feed, heads


def body(
    tokens,
    segment_ids,
    row_counts,
    global_count,
    cotangent,
    query_weight,
    key_weight,
    value_weight,
    output_weight,
    inner_weight,
    outer_weight,
    attn_gain,
    attn_bias,
    feed_gain,
    feed_bias,
):
    length, width = tokens.shape
    hidden = inner_weight.shape[1]
    half = width // 2
    qkv = [my_half(w) for w in (query_weight, key_weight, value_weight)]
    stacked = jnp.stack([attn_gain, attn_bias, feed_gain, feed_bias], axis=1)
    stacked = jnp.pad(stacked, ((0, 0), (0, 124)))
    blocks = (
        jnp.concatenate([w[..., :half] for w in qkv], axis=-1),
        jnp.concatenate([w[..., half:] for w in qkv], axis=-1),
        my_half(jnp.concatenate([output_weight, stacked], axis=1)),
        my_half(inner_weight),
        my_quarter(outer_weight),
    )
    seg_rows = jnp.broadcast_to(segment_ids.astype(f32)[None], (8, length))
    valid = (jnp.arange(length) < row_counts[0]).astype(f32)
    tokens_total = lax.axis_size("dp") * lax.axis_size("shard") * length
    factor = jnp.float32(tokens_total) / global_count[0].astype(f32)
    scale_rows = jnp.broadcast_to((valid * factor)[None], (8, length))
    mixed, input_grad, feed, heads = compute(tokens, seg_rows, scale_rows, cotangent, blocks)
    dqkv = (
        jnp.concatenate([heads.columns(c, c + half) for c in (at, at + 3 * half)], axis=1)
        for at in range(0, 3 * half, half)
    )
    outer = hidden + width + 128
    dwu = [feed.columns(at, at + width) for at in range(outer, outer + hidden, width)]
    dpar = feed.columns(hidden + width, outer)
    return (
        mixed,
        input_grad,
        *dqkv,
        feed.columns(hidden, hidden + width),
        feed.columns(0, hidden),
        jnp.concatenate(dwu, axis=0),
        dpar[:, 0],
        dpar[:, 1],
        dpar[:, 2],
        dpar[:, 3],
    )


def solution(mesh):
    rows = P(("dp", "shard"))
    rows_two = P(("dp", "shard"), None)
    two = P("shard", None)
    one = P("shard")
    in_specs = (rows_two, rows, rows, P(), rows_two) + (two,) * 6 + (one,) * 4
    out_specs = (rows_two, rows_two) + (two,) * 6 + (one,) * 4
    return jax.shard_map(body, mesh=mesh, in_specs=in_specs, out_specs=out_specs, check_vma=False)
```

```python
import functools

import jax
import jax.numpy as jnp
from jax import lax
from jax.experimental import pallas as pl
from jax.experimental.pallas import tpu as pltpu
from jax.sharding import PartitionSpec as P

H = 8
B = 256
CHUNK = 256
norm_eps = 1e-05
masked_score = -1e30
bf16 = jnp.bfloat16
f32 = jnp.float32


def nn(left, right):
    return lax.dot_general(left, right, (((1,), (0,)), ((), ())), preferred_element_type=f32)


def nt(left, right):
    return lax.dot_general(left, right, (((1,), (1,)), ((), ())), preferred_element_type=f32)


def band(block, blocks):
    return max(0, block - 1) * B, min(blocks, block + 2) * B


def key_blocks(block, blocks):
    low, high = band(block, blocks)
    for at in range(low, high, B):
        step = (block * B - at) // B + 1
        yield slice(at, at + B), slice(step * B, (step + 1) * B), slice(at - low, at - low + B)


def query_blocks(block, blocks):
    low, high = band(block, blocks)
    first = low - block * B + B
    return slice(low, high), slice(first, first + high - low)


def fill_bias(seg_ref, bias_ref):
    column = seg_ref[...].T[:, 0:1]
    blocks = bias_ref.shape[0] // B
    for block in range(blocks):
        row = seg_ref[0:1, block * B : (block + 1) * B]
        for keys, cols, _ in key_blocks(block, blocks):
            bias_ref[keys, cols] = jnp.where(column[keys] == row, 0.0, masked_score)


def bias_of(bias_ref, block, blocks):
    parts = [bias_ref[keys, cols] for keys, cols, _ in key_blocks(block, blocks)]
    return jnp.concatenate(parts, axis=0)


def attend_head(head, size, qkv_ref, bias_ref, o_ref, lse_ref):
    blocks = qkv_ref.shape[2] // B
    rows = pl.ds(pl.multiple_of(head * size, size), size)
    key = qkv_ref[1, rows, :].T
    for block in range(blocks):
        low, high = band(block, blocks)
        tile = slice(block * B, (block + 1) * B)
        score = nn(key[low:high], qkv_ref[0, rows, tile]) + bias_of(bias_ref, block, blocks)
        top = jnp.max(score, axis=0, keepdims=True)
        weight = jnp.exp(score - top)
        total = jnp.sum(weight, axis=0, keepdims=True)
        mixed = nn(qkv_ref[2, rows, low:high], weight.astype(bf16)) * (1.0 / total)
        o_ref[rows, tile] = mixed.astype(bf16)
        lse_ref[head, :, tile] = jnp.broadcast_to(top + jnp.log(total), (8, B))


def attend_head_back(
    head, out, size, qkv_ref, o_ref, do_ref, lse_ref, bias_ref, prob_ref, ds_ref, dqkv_ref
):
    length = qkv_ref.shape[2]
    blocks = length // B
    scale = size**-0.5
    rows = pl.ds(pl.multiple_of(head * size, size), size)
    outs = pl.ds(pl.multiple_of(out * size, size), size)
    key_t = qkv_ref[1, rows, :]
    key = key_t.T
    value = qkv_ref[2, rows, :].T
    do_t = do_ref[rows, :]
    delta = jnp.sum(do_t.astype(f32) * o_ref[rows, :].astype(f32), axis=0, keepdims=True)
    for block in range(blocks):
        low, high = band(block, blocks)
        tile = slice(block * B, (block + 1) * B)
        score = nn(key[low:high], qkv_ref[0, rows, tile]) + bias_of(bias_ref, block, blocks)
        prob = jnp.exp(score - lse_ref[head, 0:1, tile])
        prob_low = prob.astype(bf16)
        dprob = nn(value[low:high], do_t[:, tile])
        dscore = (prob * (dprob - delta[:, tile])).astype(bf16)
        for keys, cols, part in key_blocks(block, blocks):
            prob_ref[keys, cols] = prob_low[part]
            ds_ref[keys, cols] = dscore[part]
        dq = nn(key_t[:, low:high], dscore) * scale
        dqkv_ref[0, outs, tile] = dq.astype(bf16)
    query = qkv_ref[0, rows, :].T
    do = do_t.T
    for block in range(blocks):
        tile = slice(block * B, (block + 1) * B)
        queries, cols = query_blocks(block, blocks)
        dv = nn(prob_ref[tile, cols], do[queries])
        dqkv_ref[2, outs, tile] = dv.astype(bf16).T
        dk = nn(ds_ref[tile, cols], query[queries])
        dqkv_ref[1, outs, tile] = dk.astype(bf16).T


def normalize(values):
    center = values - jnp.mean(values, axis=0, keepdims=True)
    spread = jnp.mean(center * center, axis=0, keepdims=True)
    scale = lax.rsqrt(spread + norm_eps)
    return center * scale, scale


def normalize_back(dn, n, scale):
    mean_one = jnp.mean(dn, axis=0, keepdims=True)
    mean_two = jnp.mean(dn * n, axis=0, keepdims=True)
    return (dn - mean_one - n * mean_two) * scale


def gelu_pair(u):
    c0 = 0.7978845608028654
    c1 = c0 * 0.044715
    square = u * u
    t = jnp.tanh(u * (c0 + c1 * square))
    half = 0.5 * u
    cdf = 0.5 + 0.5 * t
    z = u * cdf
    slope = cdf + half * (1.0 - t * t) * (c0 + (3.0 * c1) * square)
    return z, slope


def lanes_sum(values):
    return values[:, :128] + values[:, 128:]


def turn_kernel(x_ref, x_t_ref):
    x_t_ref[...] = x_ref[...].T


def attend_kernel(first, size, x_ref, w_ref, seg_ref, *refs):
    if first:
        group, w_t_ref = first - 1, refs[0]
        count = w_t_ref.shape[0]
        w_t_ref[...] = w_ref[:, group * count : (group + 1) * count].T
        refs = refs[1:]
    else:
        w_t_ref = w_ref
    qkv_ref, o_ref, lse_ref, bias_ref = refs
    rows = o_ref.shape[0]
    fill_bias(seg_ref, bias_ref)
    for at in range(0, x_ref.shape[1], B):
        cols = slice(at, at + B)
        query = nn(w_t_ref[:rows, :], x_ref[:, cols]).astype(bf16)
        qkv_ref[0, :, cols] = query * jnp.asarray(size**-0.5, bf16)
        qkv_ref[1, :, cols] = nn(w_t_ref[rows : 2 * rows, :], x_ref[:, cols]).astype(bf16)
        qkv_ref[2, :, cols] = nn(w_t_ref[2 * rows :, :], x_ref[:, cols]).astype(bf16)

    def two_heads(pair, carry):
        for one in range(2):
            attend_head(2 * pair + one, size, qkv_ref, bias_ref, o_ref, lse_ref)
        return carry

    lax.fori_loop(0, rows // size // 2, two_heads, 0)


def join_heads(oa_ref, ob_ref, o_ref):
    rows = oa_ref.shape[0]
    o_ref[:rows, :] = oa_ref[...]
    o_ref[rows:, :] = ob_ref[...]


def feed_in_kernel(
    oa_ref,
    ob_ref,
    x_ref,
    wio_ref,
    o_ref,
    wo_t_ref,
    wi_t_ref,
    y_ref,
    n1_ref,
    stat_ref,
    yr_ref,
    z_ref,
    slope_ref,
):
    width = wio_ref.shape[0]
    hidden = wio_ref.shape[1] - width - 128
    join_heads(oa_ref, ob_ref, o_ref)
    wo_t_ref[...] = wio_ref[:, hidden : hidden + width].T
    wi_t_ref[...] = wio_ref[:, :hidden].T
    params = wio_ref[:, hidden + width :].astype(f32)
    gain_one, bias_one = params[:, 0:1], params[:, 1:2]
    for at in range(0, x_ref.shape[1], B):
        cols = slice(at, at + B)
        h = x_ref[:, cols].astype(f32) + nn(wo_t_ref[...], o_ref[:, cols])
        n1, s1 = normalize(h)
        n1_ref[:, cols] = n1.astype(bf16)
        stat_ref[:, cols] = jnp.broadcast_to(s1, (8, B))
        y = n1 * gain_one + bias_one
        yr_ref[:, cols] = y.astype(bf16)
        y_ref[:, cols] = y
        for f in range(0, hidden, CHUNK):
            u = nn(wi_t_ref[f : f + CHUNK, :], yr_ref[:, cols])
            z, slope = gelu_pair(u)
            z_ref[f : f + CHUNK, cols] = z.astype(bf16)
            slope_ref[f : f + CHUNK, cols] = slope.astype(bf16)


def feed_out_kernel(
    shards,
    y_ref,
    z_ref,
    wio_ref,
    groups_ref,
    wu_ref,
    wu_t_ref,
    next_ref,
    x2_ref,
    n2_ref,
    stat_ref,
):
    hidden, width = wu_ref.shape
    count = hidden // width
    rows = width // shards
    for shard in range(shards):
        for group in range(count):
            at = (shard * count + group) * rows
            part = slice(shard * rows, (shard + 1) * rows)
            wu_ref[at : at + rows, :] = groups_ref[part, group * width : (group + 1) * width]
    wu_t_ref[...] = wu_ref[...].T
    params = wio_ref[:, hidden + width :].astype(f32)
    gain_two, bias_two = params[:, 2:3], params[:, 3:4]
    for at in range(0, y_ref.shape[1], B):
        cols = slice(at, at + B)
        h2 = y_ref[:, cols] + nn(wu_t_ref[...], z_ref[:, cols])
        n2, s2 = normalize(h2)
        n2_ref[:, cols] = n2.astype(bf16)
        stat_ref[:, cols] = jnp.broadcast_to(s2, (8, B))
        out = n2 * gain_two + bias_two
        next_ref[:, cols] = out
        x2_ref[:, cols] = out.astype(bf16)


def feed_last_kernel(
    oa_ref,
    ob_ref,
    x_ref,
    wio_ref,
    wu_ref,
    wo_t_ref,
    wi_t_ref,
    wu_t_ref,
    cot_ref,
    scale_ref,
    o_ref,
    mixed_ref,
    z_ref,
    du_ref,
    yr_ref,
    dfr_ref,
    dar_ref,
    dh_ref,
    do_ref,
    acc_ref,
    n1_ref,
):
    width = wio_ref.shape[0]
    hidden = wio_ref.shape[1] - width - 128
    join_heads(oa_ref, ob_ref, o_ref)
    params = wio_ref[:, hidden + width :].astype(f32)
    gain_one, bias_one = params[:, 0:1], params[:, 1:2]
    gain_two, bias_two = params[:, 2:3], params[:, 3:4]
    acc_ref[...] = jnp.zeros_like(acc_ref)

    for at in range(0, x_ref.shape[1], B):
        cols = slice(at, at + B)
        slot = at // B % 2
        h = x_ref[:, cols] + nn(wo_t_ref[...], o_ref[:, cols])
        n1, s1 = normalize(h)
        n1_ref[slot] = n1
        y = n1 * gain_one + bias_one
        yr_ref[:, cols] = y.astype(bf16)
        dh_ref[:, cols] = y
        for f in range(0, hidden, CHUNK):
            u = nn(wi_t_ref[f : f + CHUNK, :], yr_ref[:, cols])
            z, slope = gelu_pair(u)
            z_ref[f : f + CHUNK, cols] = z.astype(bf16)
            du_ref[f : f + CHUNK, cols] = slope.astype(bf16)
        h2 = dh_ref[:, cols] + nn(wu_t_ref[...], z_ref[:, cols])
        n2, s2 = normalize(h2)
        out = n2 * gain_two + bias_two
        mixed_ref[cols, :] = out.astype(bf16).T
        grad = cot_ref[cols, :].T * scale_ref[0:1, cols]
        acc_ref[2] += lanes_sum(grad * n2)
        acc_ref[3] += lanes_sum(grad)
        dh2 = normalize_back(grad * gain_two, n2, s2)
        dh_ref[:, cols] = dh2
        dfr_ref[:, cols] = dh2.astype(bf16)
        for f in range(0, hidden, CHUNK):
            dz = nn(wu_ref[f : f + CHUNK, :], dfr_ref[:, cols])
            slope = du_ref[f : f + CHUNK, cols].astype(f32)
            du_ref[f : f + CHUNK, cols] = (dz * slope).astype(bf16)
        dy = dh_ref[:, cols] + nn(wio_ref[:, :hidden], du_ref[:, cols])
        acc_ref[0] += lanes_sum(dy * n1_ref[slot])
        acc_ref[1] += lanes_sum(dy)
        dh = normalize_back(dy * gain_one, n1_ref[slot], s1)
        dh_ref[:, cols] = dh
        dar_ref[:, cols] = dh.astype(bf16)
        do_ref[:, cols] = nn(wio_ref[:, hidden : hidden + width], dar_ref[:, cols]).astype(bf16)


def feed_back_kernel(
    g_ref,
    n1_ref,
    n2_ref,
    stat1_ref,
    stat2_ref,
    slope_ref,
    wio_ref,
    wu_ref,
    acc_in_ref,
    dh_ref,
    do_ref,
    du_ref,
    dfr_ref,
    dar_ref,
    acc_ref,
):
    width = wio_ref.shape[0]
    hidden = wio_ref.shape[1] - width - 128
    params = wio_ref[:, hidden + width :].astype(f32)
    gain_one, gain_two = params[:, 0:1], params[:, 2:3]
    acc_ref[...] = acc_in_ref[...]
    for at in range(0, g_ref.shape[1], B):
        cols = slice(at, at + B)
        grad = g_ref[:, cols]
        n2 = n2_ref[:, cols].astype(f32)
        acc_ref[2] += lanes_sum(grad * n2)
        acc_ref[3] += lanes_sum(grad)
        dh2 = normalize_back(grad * gain_two, n2, stat2_ref[0:1, cols])
        dh_ref[:, cols] = dh2
        dfr_ref[:, cols] = dh2.astype(bf16)
        for f in range(0, hidden, CHUNK):
            dz = nn(wu_ref[f : f + CHUNK, :], dfr_ref[:, cols])
            slope = slope_ref[f : f + CHUNK, cols].astype(f32)
            du_ref[f : f + CHUNK, cols] = (dz * slope).astype(bf16)
        dy = dh_ref[:, cols] + nn(wio_ref[:, :hidden], du_ref[:, cols])
        n1 = n1_ref[:, cols].astype(f32)
        acc_ref[0] += lanes_sum(dy * n1)
        acc_ref[1] += lanes_sum(dy)
        dh = normalize_back(dy * gain_one, n1, stat1_ref[0:1, cols])
        dh_ref[:, cols] = dh
        dar_ref[:, cols] = dh.astype(bf16)
        do_ref[:, cols] = nn(wio_ref[:, hidden : hidden + width], dar_ref[:, cols]).astype(bf16)


def place(value, first, unit, core, keep_ref, send_ref, cols):
    for at in range(0, value.shape[0], unit):
        block = (first + at) // unit
        rows = slice(block // 2 * unit, block // 2 * unit + unit)
        part = value[at : at + unit]

        @pl.when(core == block % 2)
        def _():
            keep_ref[rows, cols] = part

        @pl.when(core != block % 2)
        def _():
            send_ref[rows, cols] = part


def outer_grad_kernel(shards, core_ref, z1_ref, z2_ref, dfr1_ref, dfr2_ref, keep_ref, send_ref):
    core = core_ref[0]
    hidden, width = z1_ref.shape[0], dfr1_ref.shape[0]
    unit = width // shards // 2
    groups = hidden // width
    per_group = hidden // shards // groups
    for first in range(0, hidden, 256):
        part = slice(first, first + 256)
        dwu = nt(z1_ref[part, :], dfr1_ref[...]) + nt(z2_ref[part, :], dfr2_ref[...])
        dwu = dwu.astype(bf16)
        for at in range(0, 256, per_group):
            block = (first + at) // per_group
            shard, group = block // groups, block % groups
            cols = slice(group * width, (group + 1) * width)
            rows = dwu[at : at + per_group]
            place(rows, shard * per_group, unit, core, keep_ref, send_ref, cols)


def inner_grad_kernel(
    shards,
    core_ref,
    yr1_ref,
    yr2_ref,
    du1_ref,
    du2_ref,
    o1_ref,
    o2_ref,
    dar1_ref,
    dar2_ref,
    acc_ref,
    keep_ref,
    send_ref,
):
    core = core_ref[0]
    width, hidden = yr1_ref.shape[0], du1_ref.shape[0]
    unit = width // shards // 2
    for first in range(0, hidden, CHUNK):
        part = slice(first, first + CHUNK)
        dwi_t = nt(du1_ref[part, :], yr1_ref[...]) + nt(du2_ref[part, :], yr2_ref[...])
        place(dwi_t.astype(bf16).T, 0, unit, core, keep_ref, send_ref, part)
    for first in range(0, width, CHUNK):
        part = slice(first, first + CHUNK)
        cols = slice(hidden + first, hidden + first + CHUNK)
        dwo = nt(o1_ref[...], dar1_ref[part, :]) + nt(o2_ref[...], dar2_ref[part, :])
        place(dwo.astype(bf16), 0, unit, core, keep_ref, send_ref, cols)
    lane = lax.broadcasted_iota(jnp.int32, (width, 128), 1)
    dpar = jnp.zeros((width, 128), f32)
    for i in range(4):
        dpar = jnp.where(lane == i, jnp.sum(acc_ref[i], axis=1, keepdims=True), dpar)
    last = slice(hidden + width, hidden + width + 128)
    place(dpar.astype(bf16), 0, unit, core, keep_ref, send_ref, last)


def attend_back_kernel(first, size, qkv_ref, o_ref, do_ref, lse_ref, seg_ref, dqkv_ref, *refs):
    bias_ref, prob_ref, ds_ref = refs
    rows = dqkv_ref.shape[1]
    fill_bias(seg_ref, bias_ref)
    here = slice(first, first + rows)

    def two_heads(pair, carry):
        for one in range(2):
            head = 2 * pair + one
            attend_head_back(
                head,
                head,
                size,
                qkv_ref,
                o_ref.at[here],
                do_ref.at[here],
                lse_ref,
                bias_ref,
                prob_ref.at[one],
                ds_ref.at[one],
                dqkv_ref,
            )
        return carry

    lax.fori_loop(0, rows // size // 2, two_heads, 0)


def attend_part_kernel(
    p, size, shards, qkv_ref, o_ref, do_ref, lse_ref, seg_ref, *refs
):
    grads = p % 2 == 1
    if grads:
        core_ref, x1_ref, x2_ref, before_ref, second_ref = refs[:5]
        dqkv_ref, keep_ref, send_ref, bias_ref, prob_ref, ds_ref = refs[5:]
    else:
        dqkv_ref, bias_ref, prob_ref, ds_ref = refs
    fill_bias(seg_ref, bias_ref)
    rows = qkv_ref.shape[1]
    here = slice(p // 2 * rows, (p // 2 + 1) * rows)
    for one in range(2):
        attend_head_back(
            p % 2 * 2 + one,
            one,
            size,
            qkv_ref,
            o_ref.at[here],
            do_ref.at[here],
            lse_ref,
            bias_ref,
            prob_ref.at[one],
            ds_ref.at[one],
            dqkv_ref,
        )
    if not grads:
        return
    core = core_ref[0]
    unit = x1_ref.shape[0] // shards // 2
    for i in range(3):
        joined = jnp.concatenate([before_ref[i], dqkv_ref[i]], axis=0)
        dw = nt(x1_ref[...], joined) + nt(x2_ref[...], second_ref[i])
        place(dw.astype(bf16), 0, unit, core, keep_ref, send_ref, slice(i * rows, (i + 1) * rows))


def input_kernel(turned, w_ref, dh_ref, *refs):
    parts, grad_ref, join_ref = refs[:-2], refs[-2], refs[-1]
    length = dh_ref.shape[1]
    at = 0
    each = len(parts) // 2
    for group in range(2):
        for i in range(3):
            for part in parts[group * each : (group + 1) * each]:
                rows = part.shape[1]
                join_ref[at : at + rows, :] = part[i]
                at += rows
    for at in range(0, length, B):
        cols = slice(at, at + B)
        grad = dh_ref[:, cols] + nn(w_ref[...], join_ref[:, cols])
        if turned:
            grad_ref[cols, :] = grad.T
        else:
            grad_ref[:, cols] = grad


VM = pl.BlockSpec(memory_space=pltpu.VMEM)
SM = pl.BlockSpec(memory_space=pltpu.SMEM)


def call(kernel, outs, scratch, args, specs=None, cost=10, limit=8, alias={}):
    return pl.pallas_call(
        kernel,
        out_shape=[jax.ShapeDtypeStruct(shape, dtype) for shape, dtype in outs],
        in_specs=specs if specs else [VM] * len(args),
        out_specs=[VM] * len(outs),
        scratch_shapes=[pltpu.VMEM(*one) for one in scratch],
        input_output_aliases=alias,
        cost_estimate=pl.CostEstimate(
            flops=cost * 1000000000, bytes_accessed=cost * 3000000, transcendentals=0
        ),
        compiler_params=pltpu.CompilerParams(vmem_limit_bytes=limit * 2**20),
    )(*args)


def flip(value, axis, bit):
    count = lax.axis_size(axis)
    return lax.ppermute(value, axis, [(i, i ^ bit) for i in range(count)])


def bit_of(axis, bit):
    return lax.rem(lax.div(lax.axis_index(axis), bit), 2)


def bits_of(axis):
    count = lax.axis_size(axis)
    found = []
    bit = count // 2
    while bit:
        found.append((axis, bit))
        bit //= 2
    return found


def both(bit, mine, other, dim):
    low = jnp.concatenate([mine, other], axis=dim)
    high = jnp.concatenate([other, mine], axis=dim)
    return jnp.where(bit == 0, low, high)


def my_half(block):
    rows = block.shape[0] // 2
    return lax.dynamic_slice_in_dim(block, bit_of("dp", 1) * rows, rows, axis=0)[None]


class Gather:
    def __init__(self, mine):
        *steps, self.last = reversed(bits_of("shard"))
        for axis, bit in steps:
            mine = both(bit_of(axis, bit), mine, flip(mine, axis, bit), 0)
        self.mine = mine
        self.came = flip(mine, *self.last)

    def merge(self, *after):
        came = tie(self.came, *after) if after else self.came
        return both(bit_of(*self.last), self.mine, came, 0)


def over_cores(mine):
    full = both(bit_of("dp", 1), mine, flip(mine, "dp", 1), 1)
    return full.reshape(-1, mine.shape[-1])


class Sum:
    def __init__(self, keep, send):
        self.labels = bits_of("shard") + bits_of("dp")[:-1]
        self.cols = keep.shape[1]
        self.unit = keep.shape[0] // 2 ** len(self.labels)
        self.keep = keep
        self.sent = send
        self.came = [flip(send, "dp", 1)]
        self.value = None
        self.left = list(self.labels)

    def after(self, other):
        if self.value is None:
            self.keep = tie(self.keep, other)
        else:
            self.value = tie(self.value, other)

    def settle(self):
        if self.value is not None:
            return
        total = self.keep.astype(f32)
        for came in self.came:
            total += came.astype(f32)
        self.value = total.astype(bf16).reshape((2,) * len(self.left) + (self.unit, self.cols))

    def halve(self, axis, bit):
        self.settle()
        dim = self.left.index((axis, bit))
        me = bit_of(axis, bit)
        self.sent = lax.dynamic_index_in_dim(self.value, 1 - me, dim, keepdims=False)
        self.keep = lax.dynamic_index_in_dim(self.value, me, dim, keepdims=False)
        self.came = [flip(self.sent, axis, bit)]
        self.left.remove((axis, bit))
        self.value = None

    def masks(self):
        count = len(self.last)
        for k in range(1, 2**count):
            bits = (bit for i, (_, bit) in enumerate(self.last) if k >> (count - 1 - i) & 1)
            yield k, sum(bits)

    def scatter(self):
        self.settle()
        self.last = list(self.left)
        value = self.value.reshape(-1, self.unit, self.cols)
        me = 0
        for axis, bit in self.last:
            me = 2 * me + bit_of(axis, bit)
        self.keep = lax.dynamic_index_in_dim(value, me, 0, keepdims=False)
        self.came = []
        for k, mask in self.masks():
            send = lax.dynamic_index_in_dim(value, lax.bitwise_xor(me, k), 0, keepdims=False)
            self.came.append(flip(send, "dp", mask))
        self.left = []
        self.value = None

    def collect(self):
        self.settle()
        pieces = [self.value]
        for _, mask in self.masks():
            pieces.append(flip(self.value, "dp", mask))
        for axis, bit in reversed(self.last):
            me = bit_of(axis, bit)
            pairs = zip(pieces[::2], pieces[1::2])
            pieces = [both(me, low[None], high[None], 0) for low, high in pairs]
        self.value = pieces[0]
        self.left = list(self.last)

    def double(self, axis, bit):
        order = [label for label in self.labels if label in self.left or label == (axis, bit)]
        dim = order.index((axis, bit))
        mine = jnp.expand_dims(self.value, dim)
        self.value = both(bit_of(axis, bit), mine, flip(mine, axis, bit), dim)
        self.left = order

    def finish(self):
        self.value = self.value.reshape(-1, self.cols)
        self.other = flip(self.value, "dp", 1)

    def columns(self, first, last):
        mine, other = self.value[:, first:last], self.other[:, first:last]
        return both(bit_of("dp", 1), mine, other, 0).astype(f32)


def join(*sums):
    for one in sums:
        one.settle()
    joined = object.__new__(Sum)
    joined.labels, joined.unit, joined.left = sums[0].labels, sums[0].unit, sums[0].left
    joined.last = getattr(sums[0], "last", None)
    joined.cols = sum(one.cols for one in sums)
    joined.value = jnp.concatenate([one.value for one in sums], axis=-1)
    return joined


def tie(value, *others):
    return lax.optimization_barrier((value,) + others)[0]


def compute(tokens, seg_rows, scale_rows, cotangent, weights, hidden):
    length, width = tokens.shape
    *qkv, wo_block, vectors, wi_block, wu_block = weights

    def later(done):
        *args, _ = lax.optimization_barrier((wo_block, wi_block, wu_block, *vectors, done))
        wo, wi, wu, *params = args
        stacked = jnp.pad(jnp.stack(params, axis=1), ((0, 0), (0, 128 - len(params))))
        groups = jnp.split(wu, hidden // width, axis=0)
        parts = ((wi, wo, stacked), groups)
        return [jnp.concatenate([my_half(w) for w in part], axis=-1) for part in parts]

    size = width // H
    rows = width // 2
    shards = lax.axis_size("shard")
    core = bit_of("dp", 1).reshape(1)
    tall = ((width, length), bf16)
    tall32 = ((width, length), f32)
    wide = ((hidden, length), bf16)
    bias = ((length, 3 * B), f32)
    pair = ((2, length, 3 * B), bf16)
    shapes = [((3, rows, length), bf16), ((rows, length), bf16), ((H // 2, 8, length), f32)]

    half = width // 2
    cols = [w[:, at : at + half] for at in (0, half) for w in qkv]
    packed = jnp.concatenate([my_half(w) for w in cols], axis=-1)
    mine = Gather(packed).merge()
    wqkv = over_cores(mine)
    wio_part, wu_part = later(packed)
    wio_gather = Gather(tie(wio_part, mine))
    (x1,) = call(turn_kernel, [tall], [], (tie(tokens, packed),), None, 1)
    attend = functools.partial(attend_kernel, 1, size)
    turned = [((3 * rows, width), bf16)]
    wa_t, qkv1a, o1a, lse1a = call(attend, turned + shapes, [bias], (x1, wqkv, seg_rows))
    wio_mine = wio_gather.merge(o1a)
    wio = over_cores(wio_mine)
    wu_part = tie(wu_part, wio_mine)
    wu_gather = Gather(wu_part)
    attend = functools.partial(attend_kernel, 2, size)
    wb_t, qkv1b, o1b, lse1b = call(
        attend, turned + shapes, [bias], (x1, wqkv, tie(seg_rows, wio_mine, wu_part))
    )
    o1, wo_t, wi_t, y1, n11, stat11, yr1, z1, slope1 = call(
        feed_in_kernel,
        [tall, ((width, width), bf16), ((hidden, width), bf16), tall32, tall]
        + [((8, length), f32), tall, wide, wide],
        [],
        (o1a, o1b, x1, wio),
    )
    wu_groups = over_cores(wu_gather.merge(o1b))
    wu, wu_t, next1, x2, n21, stat12 = call(
        functools.partial(feed_out_kernel, shards),
        [((hidden, width), bf16), ((width, hidden), bf16), tall32, tall, tall]
        + [((8, length), f32)],
        [],
        (y1, z1, wio, wu_groups),
    )
    attend = functools.partial(attend_kernel, 0, size)
    qkv2a, o2a, lse2a = call(attend, shapes, [bias], (x2, wa_t, seg_rows), limit=8)
    qkv2b, o2b, lse2b = call(attend, shapes, [bias], (x2, wb_t, seg_rows), limit=8)
    o2, mixed, z2, du2, yr2, dfr2, dar2, dh2, do2, acc = call(
        feed_last_kernel,
        [tall, ((length, width), bf16), wide, wide, tall, tall, tall, tall32, tall]
        + [((4, width, 128), f32)],
        [((2, width, B), f32)],
        (o2a, o2b, next1, wio, wu, wo_t, wi_t, wu_t, cotangent, scale_rows),
        limit=10,
    )
    back = [bias, pair, pair]
    dqkv2 = []
    for group, (qkv, lse) in enumerate(((qkv2a, lse2a), (qkv2b, lse2b))):
        kernel = functools.partial(attend_back_kernel, group * rows, size)
        dqkv2 += call(kernel, shapes[:1], back, (qkv, o2, do2, lse, seg_rows), limit=14)
    joined = [((3 * width, length), bf16)]
    (grad1,) = call(
        functools.partial(input_kernel, False), [tall32], joined, (wqkv, dh2, *dqkv2), None, 3, 8
    )
    dh1, do1, du1, dfr1, dar1, acc = call(
        feed_back_kernel,
        [tall32, tall, wide, tall, tall, ((4, width, 128), f32)],
        [],
        (grad1, n11, n21, stat11, stat12, slope1, wio, wu, acc),
        alias={5: 2, 8: 5},
    )
    keep_i, send_i = call(
        functools.partial(inner_grad_kernel, shards),
        [((half, hidden + width + 128), bf16)] * 2,
        [],
        (core, yr1, yr2, du1, du2, o1, o2, dar1, dar2, acc),
        [SM] + [VM] * 9,
    )
    inner = Sum(keep_i, send_i)
    keep_u, send_u = call(
        functools.partial(outer_grad_kernel, shards),
        [((half, hidden), bf16)] * 2,
        [],
        (tie(core, send_i), z1, z2, dfr1, dfr2),
        [SM] + [VM] * 4,
    )
    parts = []

    def part(p, seg):
        qkv, lse = ((qkv1a, lse1a), (qkv1b, lse1b))[p // 2]
        args = (qkv, o1, do1, lse, seg)
        specs = [VM] * 5
        outs = [((3, 2 * size, length), bf16)]
        if p % 2:
            args += (core, x1, x2, parts[-1], dqkv2[p // 2])
            specs += [SM] + [VM] * 4
            outs += [((half, 3 * rows), bf16)] * 2
        kernel = functools.partial(attend_part_kernel, p, size, shards)
        results = call(kernel, outs, back, args, specs, 15, 14)
        parts.append(results[0])
        return results[1:]

    y_bit = bits_of("dp")[-2]
    x_bits = bits_of("shard")
    inner.after(send_u)
    for label in x_bits:
        inner.halve(*label)
    outer = Sum(keep_u, tie(send_u, inner.sent))
    part(0, tie(seg_rows, inner.sent))
    outer.after(parts[0])
    outer.halve(*y_bit)
    first = Sum(*part(1, tie(seg_rows, outer.sent)))
    inner.after(parts[1])
    inner.halve(*y_bit)
    outer.after(parts[1])
    for label in x_bits:
        outer.halve(*label)
    part(2, tie(seg_rows, inner.sent, outer.sent, first.sent))
    for one in (first, inner, outer):
        one.after(parts[2])
    for label in x_bits:
        first.halve(*label)
    feed = join(inner, outer)
    feed.scatter()
    second = Sum(*part(3, tie(seg_rows, feed.keep, first.sent)))
    feed.after(second.sent)
    feed.settle()
    (input_grad,) = call(
        functools.partial(input_kernel, True),
        [((length, width), f32)],
        joined,
        (wqkv, tie(dh1, second.sent, feed.value), *parts),
        None,
        15,
        10,
    )
    second.after(input_grad)
    for label in x_bits:
        second.halve(*label)
    feed.after(second.sent)
    feed.collect()
    first.after(second.sent)
    heads = join(first, second)
    heads.halve(*y_bit)
    heads.scatter()
    heads.settle()
    heads.after(feed.value)
    feed.after(heads.keep)
    feed.double(*y_bit)
    heads.collect()
    heads.after(feed.value)
    heads.double(*y_bit)
    feed.finish()
    heads.finish()
    return mixed, input_grad, feed, heads


def body(
    tokens,
    segment_ids,
    row_counts,
    global_count,
    cotangent,
    query_weight,
    key_weight,
    value_weight,
    output_weight,
    inner_weight,
    outer_weight,
    attn_gain,
    attn_bias,
    feed_gain,
    feed_bias,
):
    length, width = tokens.shape
    hidden = inner_weight.shape[1]
    half = width // 2
    weights = (query_weight, key_weight, value_weight, output_weight)
    weights += ((attn_gain, attn_bias, feed_gain, feed_bias), inner_weight, outer_weight)
    seg_rows = jnp.broadcast_to(segment_ids.astype(f32)[None], (8, length))
    valid = (jnp.arange(length) < row_counts[0]).astype(f32)
    tokens_total = lax.axis_size("dp") * lax.axis_size("shard") * length
    factor = jnp.float32(tokens_total) / global_count[0].astype(f32)
    scale_rows = jnp.broadcast_to((valid * factor)[None], (8, length))
    mixed, input_grad, feed, heads = compute(
        tokens, seg_rows, scale_rows, cotangent, weights, hidden
    )
    dqkv = (
        jnp.concatenate([heads.columns(c, c + half) for c in (at, at + 3 * half)], axis=1)
        for at in range(0, 3 * half, half)
    )
    outer = hidden + width + 128
    dwu = [feed.columns(at, at + width) for at in range(outer, outer + hidden, width)]
    dpar = feed.columns(hidden + width, outer)
    return (
        mixed,
        input_grad,
        *dqkv,
        feed.columns(hidden, hidden + width),
        feed.columns(0, hidden),
        jnp.concatenate(dwu, axis=0),
        dpar[:, 0],
        dpar[:, 1],
        dpar[:, 2],
        dpar[:, 3],
    )


def solution(mesh):
    rows = P(("dp", "shard"))
    rows_two = P(("dp", "shard"), None)
    two = P("shard", None)
    one = P("shard")
    in_specs = (rows_two, rows, rows, P(), rows_two) + (two,) * 6 + (one,) * 4
    out_specs = (rows_two, rows_two) + (two,) * 6 + (one,) * 4
    return jax.shard_map(body, mesh=mesh, in_specs=in_specs, out_specs=out_specs, check_vma=False)
```

```python
import functools

import jax
import jax.numpy as jnp
from jax import lax
from jax.experimental import pallas as pl
from jax.experimental.pallas import tpu as pltpu
from jax.sharding import PartitionSpec as P

H = 8
B = 256
CHUNK = 256
norm_eps = 1e-05
masked_score = -1e30
bf16 = jnp.bfloat16
f32 = jnp.float32


def nn(left, right):
    return lax.dot_general(left, right, (((1,), (0,)), ((), ())), preferred_element_type=f32)


def nt(left, right):
    return lax.dot_general(left, right, (((1,), (1,)), ((), ())), preferred_element_type=f32)


def band(block, blocks):
    return max(0, block - 1) * B, min(blocks, block + 2) * B


def key_blocks(block, blocks):
    low, high = band(block, blocks)
    for at in range(low, high, B):
        step = (block * B - at) // B + 1
        yield slice(at, at + B), slice(step * B, (step + 1) * B), slice(at - low, at - low + B)


def query_blocks(block, blocks):
    low, high = band(block, blocks)
    first = low - block * B + B
    return slice(low, high), slice(first, first + high - low)


def fill_bias(seg_ref, bias_ref):
    column = seg_ref[...].T[:, 0:1]
    blocks = bias_ref.shape[0] // B
    for block in range(blocks):
        row = seg_ref[0:1, block * B : (block + 1) * B]
        for keys, cols, _ in key_blocks(block, blocks):
            bias_ref[keys, cols] = jnp.where(column[keys] == row, 0.0, masked_score)


def bias_of(bias_ref, block, blocks):
    parts = [bias_ref[keys, cols] for keys, cols, _ in key_blocks(block, blocks)]
    return jnp.concatenate(parts, axis=0)


def attend_head(head, size, qkv_ref, bias_ref, o_ref, lse_ref):
    blocks = qkv_ref.shape[2] // B
    rows = pl.ds(pl.multiple_of(head * size, size), size)
    key = qkv_ref[1, rows, :].T
    for block in range(blocks):
        low, high = band(block, blocks)
        tile = slice(block * B, (block + 1) * B)
        score = nn(key[low:high], qkv_ref[0, rows, tile]) + bias_of(bias_ref, block, blocks)
        top = jnp.max(score, axis=0, keepdims=True)
        weight = jnp.exp(score - top)
        total = jnp.sum(weight, axis=0, keepdims=True)
        mixed = nn(qkv_ref[2, rows, low:high], weight.astype(bf16)) * (1.0 / total)
        o_ref[rows, tile] = mixed.astype(bf16)
        lse_ref[head, :, tile] = jnp.broadcast_to(top + jnp.log(total), (8, B))


def attend_head_back(
    head, out, size, qkv_ref, o_ref, do_ref, lse_ref, bias_ref, prob_ref, ds_ref, dqkv_ref
):
    length = qkv_ref.shape[2]
    blocks = length // B
    scale = size**-0.5
    rows = pl.ds(pl.multiple_of(head * size, size), size)
    outs = pl.ds(pl.multiple_of(out * size, size), size)
    key_t = qkv_ref[1, rows, :]
    key = key_t.T
    value = qkv_ref[2, rows, :].T
    do_t = do_ref[rows, :]
    delta = jnp.sum(do_t.astype(f32) * o_ref[rows, :].astype(f32), axis=0, keepdims=True)
    for block in range(blocks):
        low, high = band(block, blocks)
        tile = slice(block * B, (block + 1) * B)
        score = nn(key[low:high], qkv_ref[0, rows, tile]) + bias_of(bias_ref, block, blocks)
        prob = jnp.exp(score - lse_ref[head, 0:1, tile])
        prob_low = prob.astype(bf16)
        dprob = nn(value[low:high], do_t[:, tile])
        dscore = (prob * (dprob - delta[:, tile])).astype(bf16)
        for keys, cols, part in key_blocks(block, blocks):
            prob_ref[keys, cols] = prob_low[part]
            ds_ref[keys, cols] = dscore[part]
        dq = nn(key_t[:, low:high], dscore) * scale
        dqkv_ref[0, outs, tile] = dq.astype(bf16)
    query = qkv_ref[0, rows, :].T
    do = do_t.T
    for block in range(blocks):
        tile = slice(block * B, (block + 1) * B)
        queries, cols = query_blocks(block, blocks)
        dv = nn(prob_ref[tile, cols], do[queries])
        dqkv_ref[2, outs, tile] = dv.astype(bf16).T
        dk = nn(ds_ref[tile, cols], query[queries])
        dqkv_ref[1, outs, tile] = dk.astype(bf16).T


def normalize(values):
    center = values - jnp.mean(values, axis=0, keepdims=True)
    spread = jnp.mean(center * center, axis=0, keepdims=True)
    scale = lax.rsqrt(spread + norm_eps)
    return center * scale, scale


def normalize_back(dn, n, scale):
    mean_one = jnp.mean(dn, axis=0, keepdims=True)
    mean_two = jnp.mean(dn * n, axis=0, keepdims=True)
    return (dn - mean_one - n * mean_two) * scale


def gelu_pair(u):
    c0 = 0.7978845608028654
    c1 = c0 * 0.044715
    square = u * u
    t = jnp.tanh(u * (c0 + c1 * square))
    half = 0.5 * u
    cdf = 0.5 + 0.5 * t
    z = u * cdf
    slope = cdf + half * (1.0 - t * t) * (c0 + (3.0 * c1) * square)
    return z, slope


def lanes_sum(values):
    return values[:, :128] + values[:, 128:]


def turn_kernel(x_ref, x_t_ref):
    x_t_ref[...] = x_ref[...].T


def attend_kernel(first, size, x_ref, w_ref, seg_ref, *refs):
    if first:
        group, w_t_ref = first - 1, refs[0]
        count = w_t_ref.shape[0] // 3
        for i in range(3):
            at = i * x_ref.shape[0] + group * count
            w_t_ref[i * count : (i + 1) * count, :] = w_ref[:, at : at + count].T
        refs = refs[1:]
    else:
        w_t_ref = w_ref
    qkv_ref, o_ref, lse_ref, bias_ref = refs
    rows = o_ref.shape[0]
    fill_bias(seg_ref, bias_ref)
    for at in range(0, x_ref.shape[1], B):
        cols = slice(at, at + B)
        query = nn(w_t_ref[:rows, :], x_ref[:, cols]).astype(bf16)
        qkv_ref[0, :, cols] = query * jnp.asarray(size**-0.5, bf16)
        qkv_ref[1, :, cols] = nn(w_t_ref[rows : 2 * rows, :], x_ref[:, cols]).astype(bf16)
        qkv_ref[2, :, cols] = nn(w_t_ref[2 * rows :, :], x_ref[:, cols]).astype(bf16)

    def two_heads(pair, carry):
        for one in range(2):
            attend_head(2 * pair + one, size, qkv_ref, bias_ref, o_ref, lse_ref)
        return carry

    lax.fori_loop(0, rows // size // 2, two_heads, 0)


def join_heads(oa_ref, ob_ref, o_ref):
    rows = oa_ref.shape[0]
    o_ref[:rows, :] = oa_ref[...]
    o_ref[rows:, :] = ob_ref[...]


def feed_in_kernel(
    oa_ref,
    ob_ref,
    x_ref,
    wio_ref,
    o_ref,
    wo_t_ref,
    wi_t_ref,
    y_ref,
    n1_ref,
    stat_ref,
    yr_ref,
    z_ref,
    slope_ref,
):
    width = wio_ref.shape[0]
    hidden = wio_ref.shape[1] - width - 128
    join_heads(oa_ref, ob_ref, o_ref)
    wo_t_ref[...] = wio_ref[:, hidden : hidden + width].T
    wi_t_ref[...] = wio_ref[:, :hidden].T
    params = wio_ref[:, hidden + width :].astype(f32)
    gain_one, bias_one = params[:, 0:1], params[:, 1:2]
    for at in range(0, x_ref.shape[1], B):
        cols = slice(at, at + B)
        h = x_ref[:, cols].astype(f32) + nn(wo_t_ref[...], o_ref[:, cols])
        n1, s1 = normalize(h)
        n1_ref[:, cols] = n1.astype(bf16)
        stat_ref[:, cols] = jnp.broadcast_to(s1, (8, B))
        y = n1 * gain_one + bias_one
        yr_ref[:, cols] = y.astype(bf16)
        y_ref[:, cols] = y
        for f in range(0, hidden, CHUNK):
            u = nn(wi_t_ref[f : f + CHUNK, :], yr_ref[:, cols])
            z, slope = gelu_pair(u)
            z_ref[f : f + CHUNK, cols] = z.astype(bf16)
            slope_ref[f : f + CHUNK, cols] = slope.astype(bf16)


def feed_out_kernel(
    shards,
    y_ref,
    z_ref,
    wio_ref,
    groups_ref,
    wu_ref,
    wu_t_ref,
    next_ref,
    x2_ref,
    n2_ref,
    stat_ref,
):
    hidden, width = wu_ref.shape
    count = hidden // width
    rows = width // shards
    for shard in range(shards):
        for group in range(count):
            at = (shard * count + group) * rows
            part = slice(shard * rows, (shard + 1) * rows)
            wu_ref[at : at + rows, :] = groups_ref[part, group * width : (group + 1) * width]
    wu_t_ref[...] = wu_ref[...].T
    params = wio_ref[:, hidden + width :].astype(f32)
    gain_two, bias_two = params[:, 2:3], params[:, 3:4]
    for at in range(0, y_ref.shape[1], B):
        cols = slice(at, at + B)
        h2 = y_ref[:, cols] + nn(wu_t_ref[...], z_ref[:, cols])
        n2, s2 = normalize(h2)
        n2_ref[:, cols] = n2.astype(bf16)
        stat_ref[:, cols] = jnp.broadcast_to(s2, (8, B))
        out = n2 * gain_two + bias_two
        next_ref[:, cols] = out
        x2_ref[:, cols] = out.astype(bf16)


def feed_last_kernel(
    oa_ref,
    ob_ref,
    x_ref,
    wio_ref,
    wu_ref,
    wo_t_ref,
    wi_t_ref,
    wu_t_ref,
    cot_ref,
    scale_ref,
    o_ref,
    mixed_ref,
    z_ref,
    du_ref,
    yr_ref,
    dfr_ref,
    dar_ref,
    dh_ref,
    do_ref,
    acc_ref,
    n1_ref,
):
    width = wio_ref.shape[0]
    hidden = wio_ref.shape[1] - width - 128
    join_heads(oa_ref, ob_ref, o_ref)
    params = wio_ref[:, hidden + width :].astype(f32)
    gain_one, bias_one = params[:, 0:1], params[:, 1:2]
    gain_two, bias_two = params[:, 2:3], params[:, 3:4]
    acc_ref[...] = jnp.zeros_like(acc_ref)

    for at in range(0, x_ref.shape[1], B):
        cols = slice(at, at + B)
        slot = at // B % 2
        h = x_ref[:, cols] + nn(wo_t_ref[...], o_ref[:, cols])
        n1, s1 = normalize(h)
        n1_ref[slot] = n1
        y = n1 * gain_one + bias_one
        yr_ref[:, cols] = y.astype(bf16)
        dh_ref[:, cols] = y
        for f in range(0, hidden, CHUNK):
            u = nn(wi_t_ref[f : f + CHUNK, :], yr_ref[:, cols])
            z, slope = gelu_pair(u)
            z_ref[f : f + CHUNK, cols] = z.astype(bf16)
            du_ref[f : f + CHUNK, cols] = slope.astype(bf16)
        h2 = dh_ref[:, cols] + nn(wu_t_ref[...], z_ref[:, cols])
        n2, s2 = normalize(h2)
        out = n2 * gain_two + bias_two
        mixed_ref[cols, :] = out.astype(bf16).T
        grad = cot_ref[cols, :].T * scale_ref[0:1, cols]
        acc_ref[2] += lanes_sum(grad * n2)
        acc_ref[3] += lanes_sum(grad)
        dh2 = normalize_back(grad * gain_two, n2, s2)
        dh_ref[:, cols] = dh2
        dfr_ref[:, cols] = dh2.astype(bf16)
        for f in range(0, hidden, CHUNK):
            dz = nn(wu_ref[f : f + CHUNK, :], dfr_ref[:, cols])
            slope = du_ref[f : f + CHUNK, cols].astype(f32)
            du_ref[f : f + CHUNK, cols] = (dz * slope).astype(bf16)
        dy = dh_ref[:, cols] + nn(wio_ref[:, :hidden], du_ref[:, cols])
        acc_ref[0] += lanes_sum(dy * n1_ref[slot])
        acc_ref[1] += lanes_sum(dy)
        dh = normalize_back(dy * gain_one, n1_ref[slot], s1)
        dh_ref[:, cols] = dh
        dar_ref[:, cols] = dh.astype(bf16)
        do_ref[:, cols] = nn(wio_ref[:, hidden : hidden + width], dar_ref[:, cols]).astype(bf16)


def feed_back_kernel(
    g_ref,
    n1_ref,
    n2_ref,
    stat1_ref,
    stat2_ref,
    slope_ref,
    wio_ref,
    wu_ref,
    acc_in_ref,
    dh_ref,
    do_ref,
    du_ref,
    dfr_ref,
    dar_ref,
    acc_ref,
):
    width = wio_ref.shape[0]
    hidden = wio_ref.shape[1] - width - 128
    params = wio_ref[:, hidden + width :].astype(f32)
    gain_one, gain_two = params[:, 0:1], params[:, 2:3]
    acc_ref[...] = acc_in_ref[...]
    for at in range(0, g_ref.shape[1], B):
        cols = slice(at, at + B)
        grad = g_ref[:, cols]
        n2 = n2_ref[:, cols].astype(f32)
        acc_ref[2] += lanes_sum(grad * n2)
        acc_ref[3] += lanes_sum(grad)
        dh2 = normalize_back(grad * gain_two, n2, stat2_ref[0:1, cols])
        dh_ref[:, cols] = dh2
        dfr_ref[:, cols] = dh2.astype(bf16)
        for f in range(0, hidden, CHUNK):
            dz = nn(wu_ref[f : f + CHUNK, :], dfr_ref[:, cols])
            slope = slope_ref[f : f + CHUNK, cols].astype(f32)
            du_ref[f : f + CHUNK, cols] = (dz * slope).astype(bf16)
        dy = dh_ref[:, cols] + nn(wio_ref[:, :hidden], du_ref[:, cols])
        n1 = n1_ref[:, cols].astype(f32)
        acc_ref[0] += lanes_sum(dy * n1)
        acc_ref[1] += lanes_sum(dy)
        dh = normalize_back(dy * gain_one, n1, stat1_ref[0:1, cols])
        dh_ref[:, cols] = dh
        dar_ref[:, cols] = dh.astype(bf16)
        do_ref[:, cols] = nn(wio_ref[:, hidden : hidden + width], dar_ref[:, cols]).astype(bf16)


def place(value, first, unit, core, keep_ref, send_ref, cols):
    for at in range(0, value.shape[0], unit):
        block = (first + at) // unit
        rows = slice(block // 2 * unit, block // 2 * unit + unit)
        part = value[at : at + unit]

        @pl.when(core == block % 2)
        def _():
            keep_ref[rows, cols] = part

        @pl.when(core != block % 2)
        def _():
            send_ref[rows, cols] = part


def outer_grad_kernel(
    shards,
    core_ref,
    z1_ref,
    z2_ref,
    dfr1_ref,
    dfr2_ref,
    o1_ref,
    o2_ref,
    dar1_ref,
    dar2_ref,
    acc_ref,
    keep_ref,
    send_ref,
):
    core = core_ref[0]
    hidden, width = z1_ref.shape[0], dfr1_ref.shape[0]
    unit = width // shards // 2
    groups = hidden // width
    per_group = hidden // shards // groups
    for first in range(0, hidden, 256):
        part = slice(first, first + 256)
        dwu = nt(z1_ref[part, :], dfr1_ref[...]) + nt(z2_ref[part, :], dfr2_ref[...])
        dwu = dwu.astype(bf16)
        for at in range(0, 256, per_group):
            block = (first + at) // per_group
            shard, group = block // groups, block % groups
            cols = slice(group * width, (group + 1) * width)
            rows = dwu[at : at + per_group]
            place(rows, shard * per_group, unit, core, keep_ref, send_ref, cols)
    for first in range(0, width, CHUNK):
        part = slice(first, first + CHUNK)
        cols = slice(hidden + first, hidden + first + CHUNK)
        dwo = nt(o1_ref[...], dar1_ref[part, :]) + nt(o2_ref[...], dar2_ref[part, :])
        place(dwo.astype(bf16), 0, unit, core, keep_ref, send_ref, cols)
    lane = lax.broadcasted_iota(jnp.int32, (width, 128), 1)
    dpar = jnp.zeros((width, 128), f32)
    for i in range(4):
        dpar = jnp.where(lane == i, jnp.sum(acc_ref[i], axis=1, keepdims=True), dpar)
    last = slice(hidden + width, hidden + width + 128)
    place(dpar.astype(bf16), 0, unit, core, keep_ref, send_ref, last)


def inner_grad_kernel(
    shards, core_ref, yr1_ref, yr2_ref, du1_ref, du2_ref, keep_ref, send_ref
):
    core = core_ref[0]
    width, hidden = yr1_ref.shape[0], du1_ref.shape[0]
    unit = width // shards // 2
    for first in range(0, hidden, CHUNK):
        part = slice(first, first + CHUNK)
        dwi_t = nt(du1_ref[part, :], yr1_ref[...]) + nt(du2_ref[part, :], yr2_ref[...])
        place(dwi_t.astype(bf16).T, 0, unit, core, keep_ref, send_ref, part)


def attend_back_kernel(first, size, qkv_ref, o_ref, do_ref, lse_ref, seg_ref, dqkv_ref, *refs):
    bias_ref, prob_ref, ds_ref = refs
    rows = dqkv_ref.shape[1]
    fill_bias(seg_ref, bias_ref)
    here = slice(first, first + rows)

    def two_heads(pair, carry):
        for one in range(2):
            head = 2 * pair + one
            attend_head_back(
                head,
                head,
                size,
                qkv_ref,
                o_ref.at[here],
                do_ref.at[here],
                lse_ref,
                bias_ref,
                prob_ref.at[one],
                ds_ref.at[one],
                dqkv_ref,
            )
        return carry

    lax.fori_loop(0, rows // size // 2, two_heads, 0)


def attend_part_kernel(
    p, size, shards, qkv_ref, o_ref, do_ref, lse_ref, seg_ref, *refs
):
    grads = p % 2 == 1
    if grads:
        core_ref, x1_ref, x2_ref, before_ref, second_ref = refs[:5]
        dqkv_ref, keep_ref, send_ref, bias_ref, prob_ref, ds_ref = refs[5:]
    else:
        dqkv_ref, bias_ref, prob_ref, ds_ref = refs
    fill_bias(seg_ref, bias_ref)
    rows = qkv_ref.shape[1]
    here = slice(p // 2 * rows, (p // 2 + 1) * rows)
    for one in range(2):
        attend_head_back(
            p % 2 * 2 + one,
            one,
            size,
            qkv_ref,
            o_ref.at[here],
            do_ref.at[here],
            lse_ref,
            bias_ref,
            prob_ref.at[one],
            ds_ref.at[one],
            dqkv_ref,
        )
    if not grads:
        return
    core = core_ref[0]
    unit = x1_ref.shape[0] // shards // 2
    for i in range(3):
        joined = jnp.concatenate([before_ref[i], dqkv_ref[i]], axis=0)
        dw = nt(x1_ref[...], joined) + nt(x2_ref[...], second_ref[i])
        place(dw.astype(bf16), 0, unit, core, keep_ref, send_ref, slice(i * rows, (i + 1) * rows))


def input_kernel(turned, w_ref, dh_ref, *refs):
    parts, grad_ref, join_ref = refs[:-2], refs[-2], refs[-1]
    length = dh_ref.shape[1]
    at = 0
    for i in range(3):
        for part in parts:
            rows = part.shape[1]
            join_ref[at : at + rows, :] = part[i]
            at += rows
    for at in range(0, length, B):
        cols = slice(at, at + B)
        grad = dh_ref[:, cols] + nn(w_ref[...], join_ref[:, cols])
        if turned:
            grad_ref[cols, :] = grad.T
        else:
            grad_ref[:, cols] = grad


VM = pl.BlockSpec(memory_space=pltpu.VMEM)
SM = pl.BlockSpec(memory_space=pltpu.SMEM)


def call(kernel, outs, scratch, args, specs=None, cost=10, limit=6, alias={}, deps=()):
    count, after = len(args), len(args) + len(deps)

    def run(*refs):
        kernel(*refs[:count], *refs[after:])

    return pl.pallas_call(
        run,
        out_shape=[jax.ShapeDtypeStruct(shape, dtype) for shape, dtype in outs],
        in_specs=(specs if specs else [VM] * count) + [pl.BlockSpec(memory_space=pl.ANY)] * len(deps),
        out_specs=[VM] * len(outs),
        scratch_shapes=[pltpu.VMEM(*one) for one in scratch],
        input_output_aliases=alias,
        cost_estimate=pl.CostEstimate(
            flops=cost * 1000000000, bytes_accessed=cost * 3000000, transcendentals=0
        ),
        compiler_params=pltpu.CompilerParams(vmem_limit_bytes=limit * 2**20),
    )(*args, *deps)


def flip(value, axis, bit):
    count = lax.axis_size(axis)
    return lax.ppermute(value, axis, [(i, i ^ bit) for i in range(count)])


def bit_of(axis, bit):
    return lax.rem(lax.div(lax.axis_index(axis), bit), 2)


def bits_of(axis):
    count = lax.axis_size(axis)
    found = []
    bit = count // 2
    while bit:
        found.append((axis, bit))
        bit //= 2
    return found


def both(bit, mine, other, dim):
    low = jnp.concatenate([mine, other], axis=dim)
    high = jnp.concatenate([other, mine], axis=dim)
    return jnp.where(bit == 0, low, high)


def my_half(block):
    rows = block.shape[0] // 2
    return lax.dynamic_slice_in_dim(block, bit_of("dp", 1) * rows, rows, axis=0)[None]


class Gather:
    def __init__(self, mine):
        *steps, self.last = reversed(bits_of("shard"))
        for axis, bit in steps:
            mine = both(bit_of(axis, bit), mine, flip(mine, axis, bit), 0)
        self.mine = mine
        self.came = flip(mine, *self.last)

    def merge(self, *after):
        came = tie(self.came, *after) if after else self.came
        return both(bit_of(*self.last), self.mine, came, 0)


def over_cores(mine):
    full = both(bit_of("dp", 1), mine, flip(mine, "dp", 1), 1)
    return full.reshape(-1, mine.shape[-1])


class Sum:
    def __init__(self, keep, send):
        self.labels = bits_of("shard") + bits_of("dp")[:-1]
        self.cols = keep.shape[1]
        self.unit = keep.shape[0] // 2 ** len(self.labels)
        self.keep = keep
        self.sent = send
        self.came = [flip(send, "dp", 1)]
        self.value = None
        self.left = list(self.labels)

    def after(self, other):
        if self.value is None:
            self.keep = tie(self.keep, other)
        else:
            self.value = tie(self.value, other)

    def settle(self):
        if self.value is not None:
            return
        total = self.keep.astype(f32)
        for came in self.came:
            total += came.astype(f32)
        self.value = total.astype(bf16).reshape((2,) * len(self.left) + (self.unit, self.cols))

    def halve(self, axis, bit):
        self.settle()
        dim = self.left.index((axis, bit))
        me = bit_of(axis, bit)
        self.sent = lax.dynamic_index_in_dim(self.value, 1 - me, dim, keepdims=False)
        self.keep = lax.dynamic_index_in_dim(self.value, me, dim, keepdims=False)
        self.came = [flip(self.sent, axis, bit)]
        self.left.remove((axis, bit))
        self.value = None

    def masks(self):
        count = len(self.last)
        for k in range(1, 2**count):
            bits = (bit for i, (_, bit) in enumerate(self.last) if k >> (count - 1 - i) & 1)
            yield k, sum(bits)

    def scatter(self):
        self.settle()
        self.last = list(self.left)
        value = self.value.reshape(-1, self.unit, self.cols)
        me = 0
        for axis, bit in self.last:
            me = 2 * me + bit_of(axis, bit)
        self.keep = lax.dynamic_index_in_dim(value, me, 0, keepdims=False)
        self.came = []
        for k, mask in self.masks():
            send = lax.dynamic_index_in_dim(value, lax.bitwise_xor(me, k), 0, keepdims=False)
            self.came.append(flip(send, "dp", mask))
        self.left = []
        self.value = None

    def collect(self):
        self.settle()
        pieces = [self.value]
        for _, mask in self.masks():
            pieces.append(flip(self.value, "dp", mask))
        for axis, bit in reversed(self.last):
            me = bit_of(axis, bit)
            pairs = zip(pieces[::2], pieces[1::2])
            pieces = [both(me, low[None], high[None], 0) for low, high in pairs]
        self.value = pieces[0]
        self.left = list(self.last)

    def double(self, axis, bit):
        order = [label for label in self.labels if label in self.left or label == (axis, bit)]
        dim = order.index((axis, bit))
        mine = jnp.expand_dims(self.value, dim)
        self.value = both(bit_of(axis, bit), mine, flip(mine, axis, bit), dim)
        self.left = order

    def finish(self):
        self.value = self.value.reshape(-1, self.cols)
        self.other = flip(self.value, "dp", 1)

    def columns(self, first, last):
        mine, other = self.value[:, first:last], self.other[:, first:last]
        return both(bit_of("dp", 1), mine, other, 0).astype(f32)


def copy_kernel(value_ref, copy_ref):
    copy_ref[...] = value_ref[...]


def copy_after(value, *deps):
    flat = value.reshape(-1, value.shape[-1])
    out = [(flat.shape, flat.dtype)]
    (copy,) = call(copy_kernel, out, [], (flat,), None, 1, deps=deps)
    return copy.reshape(value.shape)


def join(*sums):
    for one in sums:
        one.settle()
    joined = object.__new__(Sum)
    joined.labels, joined.unit, joined.left = sums[0].labels, sums[0].unit, sums[0].left
    joined.last = getattr(sums[0], "last", None)
    joined.cols = sum(one.cols for one in sums)
    joined.value = jnp.concatenate([one.value for one in sums], axis=-1)
    return joined


def tie(value, *others):
    return lax.optimization_barrier((value,) + others)[0]


def compute(tokens, seg_rows, scale_rows, cotangent, weights, hidden):
    length, width = tokens.shape
    *qkv, wo_block, vectors, wi_block, wu_block = weights

    def later(done):
        *args, _ = lax.optimization_barrier((wo_block, wi_block, wu_block, *vectors, done))
        wo, wi, wu, *params = args
        stacked = jnp.pad(jnp.stack(params, axis=1), ((0, 0), (0, 128 - len(params))))
        groups = jnp.split(wu, hidden // width, axis=0)
        parts = ((wi, wo, stacked), groups)
        return [jnp.concatenate([my_half(w) for w in part], axis=-1) for part in parts]

    size = width // H
    rows = width // 2
    shards = lax.axis_size("shard")
    core = bit_of("dp", 1).reshape(1)
    tall = ((width, length), bf16)
    tall32 = ((width, length), f32)
    wide = ((hidden, length), bf16)
    bias = ((length, 3 * B), f32)
    pair = ((2, length, 3 * B), bf16)
    shapes = [((3, rows, length), bf16), ((rows, length), bf16), ((H // 2, 8, length), f32)]

    half = width // 2
    packed = jnp.concatenate([my_half(w) for w in qkv], axis=-1)
    mine = Gather(packed).merge()
    wqkv = over_cores(mine)
    wio_part, wu_part = later(packed)
    wio_gather = Gather(tie(wio_part, mine))
    (x1,) = call(turn_kernel, [tall], [], (tie(tokens, packed),), None, 1)
    attend = functools.partial(attend_kernel, 1, size)
    turned = [((3 * rows, width), bf16)]
    wa_t, qkv1a, o1a, lse1a = call(attend, turned + shapes, [bias], (x1, wqkv, seg_rows))
    wio_mine = wio_gather.merge(o1a)
    wio = over_cores(wio_mine)
    wu_part = tie(wu_part, wio_mine)
    wu_gather = Gather(wu_part)
    attend = functools.partial(attend_kernel, 2, size)
    wb_t, qkv1b, o1b, lse1b = call(
        attend, turned + shapes, [bias], (x1, wqkv, tie(seg_rows, wio_mine, wu_part))
    )
    o1, wo_t, wi_t, y1, n11, stat11, yr1, z1, slope1 = call(
        feed_in_kernel,
        [tall, ((width, width), bf16), ((hidden, width), bf16), tall32, tall]
        + [((8, length), f32), tall, wide, wide],
        [],
        (o1a, o1b, x1, wio),
    )
    wu_groups = over_cores(wu_gather.merge(o1b))
    wu, wu_t, next1, x2, n21, stat12 = call(
        functools.partial(feed_out_kernel, shards),
        [((hidden, width), bf16), ((width, hidden), bf16), tall32, tall, tall]
        + [((8, length), f32)],
        [],
        (y1, z1, wio, wu_groups),
    )
    attend = functools.partial(attend_kernel, 0, size)
    qkv2a, o2a, lse2a = call(attend, shapes, [bias], (x2, wa_t, seg_rows), limit=6)
    qkv2b, o2b, lse2b = call(attend, shapes, [bias], (x2, wb_t, seg_rows), limit=6)
    o2, mixed, z2, du2, yr2, dfr2, dar2, dh2, do2, acc = call(
        feed_last_kernel,
        [tall, ((length, width), bf16), wide, wide, tall, tall, tall, tall32, tall]
        + [((4, width, 128), f32)],
        [((2, width, B), f32)],
        (o2a, o2b, next1, wio, wu, wo_t, wi_t, wu_t, cotangent, scale_rows),
        limit=10,
    )
    back = [bias, pair, pair]
    dqkv2 = []
    for group, (qkv, lse) in enumerate(((qkv2a, lse2a), (qkv2b, lse2b))):
        kernel = functools.partial(attend_back_kernel, group * rows, size)
        dqkv2 += call(kernel, shapes[:1], back, (qkv, o2, do2, lse, seg_rows), limit=10)
    joined = [((3 * width, length), bf16)]
    (grad1,) = call(
        functools.partial(input_kernel, False), [tall32], joined, (wqkv, dh2, *dqkv2), None, 3, 4
    )
    dh1, do1, du1, dfr1, dar1, acc = call(
        feed_back_kernel,
        [tall32, tall, wide, tall, tall, ((4, width, 128), f32)],
        [],
        (grad1, n11, n21, stat11, stat12, slope1, wio, wu, acc),
        alias={5: 2, 8: 5},
    )
    keep_u, send_u = call(
        functools.partial(outer_grad_kernel, shards),
        [((half, hidden + width + 128), bf16)] * 2,
        [],
        (core, z1, z2, dfr1, dfr2, o1, o2, dar1, dar2, acc),
        [SM] + [VM] * 9,
        limit=4,
    )
    outer = Sum(keep_u, send_u)
    keep_i, send_i = call(
        functools.partial(inner_grad_kernel, shards),
        [((half, hidden), bf16)] * 2,
        [],
        (core, yr1, yr2, du1, du2),
        [SM] + [VM] * 4,
        limit=4,
        deps=(send_u,),
    )
    parts = []

    def part(p, seg):
        qkv, lse = ((qkv1a, lse1a), (qkv1b, lse1b))[p // 2]
        args = (qkv, o1, do1, lse, seg)
        specs = [VM] * 5
        outs = [((3, 2 * size, length), bf16)]
        if p % 2:
            args += (core, x1, x2, parts[-1], dqkv2[p // 2])
            specs += [SM] + [VM] * 4
            outs += [((half, 3 * rows), bf16)] * 2
        kernel = functools.partial(attend_part_kernel, p, size, shards)
        results = call(kernel, outs, back, args, specs, 15, 10)
        parts.append(results[0])
        return results[1:]

    y_bit = bits_of("dp")[-2]
    x_bits = bits_of("shard")
    outer.after(send_i)
    for label in x_bits:
        outer.halve(*label)
    inner = Sum(keep_i, tie(send_i, outer.sent))
    part(0, tie(seg_rows, outer.sent))
    inner.after(parts[0])
    inner.halve(*y_bit)
    first = Sum(*part(1, tie(seg_rows, inner.sent)))
    outer.after(parts[1])
    outer.halve(*y_bit)
    inner.after(parts[1])
    for label in x_bits:
        inner.halve(*label)
    part(2, tie(seg_rows, inner.sent, outer.sent, first.sent))
    for one in (first, inner, outer):
        one.after(parts[2])
    for label in x_bits:
        first.halve(*label)
    feed = join(outer, inner)
    feed.scatter()
    second = Sum(*part(3, tie(seg_rows, feed.keep, first.sent)))
    feed.after(second.sent)
    feed.settle()
    for label in x_bits:
        second.halve(*label)
    feed.after(second.sent)
    feed.collect()
    first.after(second.sent)
    heads = join(first, second)
    heads.halve(*y_bit)
    (input_grad,) = call(
        functools.partial(input_kernel, True),
        [((length, width), f32)],
        joined,
        (wqkv, dh1, *parts),
        None,
        5,
        5,
        deps=(heads.sent,),
    )
    feed.double(*y_bit)
    feed.finish()
    heads.scatter()
    heads.settle()
    heads.collect()
    inner_at = hidden + width + 128
    dwu = [feed.columns(at, at + width) for at in range(0, hidden, width)]
    dwu = jnp.concatenate(dwu, axis=0)
    dwo = feed.columns(hidden, hidden + width)
    dpar = feed.columns(hidden + width, inner_at)
    dwi = feed.columns(inner_at, inner_at + hidden)
    heads.value = copy_after(heads.value, dwu, dwi, dwo)
    heads.double(*y_bit)
    heads.finish()
    dqkv = [
        jnp.concatenate([heads.columns(c, c + half) for c in (at, at + 3 * half)], axis=1)
        for at in range(0, 3 * half, half)
    ]
    return (mixed, input_grad, *dqkv, dwo, dwi, dwu, *(dpar[:, i] for i in range(4)))


def body(
    tokens,
    segment_ids,
    row_counts,
    global_count,
    cotangent,
    query_weight,
    key_weight,
    value_weight,
    output_weight,
    inner_weight,
    outer_weight,
    attn_gain,
    attn_bias,
    feed_gain,
    feed_bias,
):
    length, width = tokens.shape
    hidden = inner_weight.shape[1]
    half = width // 2
    weights = (query_weight, key_weight, value_weight, output_weight)
    weights += ((attn_gain, attn_bias, feed_gain, feed_bias), inner_weight, outer_weight)
    seg_rows = jnp.broadcast_to(segment_ids.astype(f32)[None], (8, length))
    valid = (jnp.arange(length) < row_counts[0]).astype(f32)
    tokens_total = lax.axis_size("dp") * lax.axis_size("shard") * length
    factor = jnp.float32(tokens_total) / global_count[0].astype(f32)
    scale_rows = jnp.broadcast_to((valid * factor)[None], (8, length))
    return compute(tokens, seg_rows, scale_rows, cotangent, weights, hidden)


def solution(mesh):
    rows = P(("dp", "shard"))
    rows_two = P(("dp", "shard"), None)
    two = P("shard", None)
    one = P("shard")
    in_specs = (rows_two, rows, rows, P(), rows_two) + (two,) * 6 + (one,) * 4
    out_specs = (rows_two, rows_two) + (two,) * 6 + (one,) * 4
    return jax.shard_map(body, mesh=mesh, in_specs=in_specs, out_specs=out_specs, check_vma=False)
```

```python
import functools

import jax
import jax.numpy as jnp
from jax import lax
from jax.experimental import pallas as pl
from jax.experimental.pallas import tpu as pltpu
from jax.sharding import PartitionSpec as P

H = 8
B = 256
CHUNK = 256
norm_eps = 1e-05
masked_score = -1e30
bf16 = jnp.bfloat16
f32 = jnp.float32


def nn(left, right):
    return lax.dot_general(left, right, (((1,), (0,)), ((), ())), preferred_element_type=f32)


def nt(left, right):
    return lax.dot_general(left, right, (((1,), (1,)), ((), ())), preferred_element_type=f32)


def band(block, blocks):
    return max(0, block - 1) * B, min(blocks, block + 2) * B


def key_blocks(block, blocks):
    low, high = band(block, blocks)
    for at in range(low, high, B):
        step = (block * B - at) // B + 1
        yield slice(at, at + B), slice(step * B, (step + 1) * B), slice(at - low, at - low + B)


def query_blocks(block, blocks):
    low, high = band(block, blocks)
    first = low - block * B + B
    return slice(low, high), slice(first, first + high - low)


def fill_bias(seg_ref, bias_ref):
    column = seg_ref[...].T[:, 0:1]
    blocks = bias_ref.shape[0] // B
    for block in range(blocks):
        row = seg_ref[0:1, block * B : (block + 1) * B]
        for keys, cols, _ in key_blocks(block, blocks):
            bias_ref[keys, cols] = jnp.where(column[keys] == row, 0.0, masked_score)


def bias_of(bias_ref, block, blocks):
    parts = [bias_ref[keys, cols] for keys, cols, _ in key_blocks(block, blocks)]
    return jnp.concatenate(parts, axis=0)


def attend_head(head, size, qkv_ref, bias_ref, o_ref, lse_ref):
    blocks = qkv_ref.shape[2] // B
    rows = pl.ds(pl.multiple_of(head * size, size), size)
    key = qkv_ref[1, rows, :].T
    for block in range(blocks):
        low, high = band(block, blocks)
        tile = slice(block * B, (block + 1) * B)
        score = nn(key[low:high], qkv_ref[0, rows, tile]) + bias_of(bias_ref, block, blocks)
        top = jnp.max(score, axis=0, keepdims=True)
        weight = jnp.exp(score - top)
        total = jnp.sum(weight, axis=0, keepdims=True)
        mixed = nn(qkv_ref[2, rows, low:high], weight.astype(bf16)) * (1.0 / total)
        o_ref[rows, tile] = mixed.astype(bf16)
        lse_ref[head, :, tile] = jnp.broadcast_to(top + jnp.log(total), (8, B))


def attend_head_back(
    head, out, size, qkv_ref, o_ref, do_ref, lse_ref, bias_ref, prob_ref, ds_ref, dqkv_ref
):
    length = qkv_ref.shape[2]
    blocks = length // B
    scale = size**-0.5
    rows = pl.ds(pl.multiple_of(head * size, size), size)
    outs = pl.ds(pl.multiple_of(out * size, size), size)
    key_t = qkv_ref[1, rows, :]
    key = key_t.T
    value = qkv_ref[2, rows, :].T
    do_t = do_ref[rows, :]
    delta = jnp.sum(do_t.astype(f32) * o_ref[rows, :].astype(f32), axis=0, keepdims=True)
    for block in range(blocks):
        low, high = band(block, blocks)
        tile = slice(block * B, (block + 1) * B)
        score = nn(key[low:high], qkv_ref[0, rows, tile]) + bias_of(bias_ref, block, blocks)
        prob = jnp.exp(score - lse_ref[head, 0:1, tile])
        prob_low = prob.astype(bf16)
        dprob = nn(value[low:high], do_t[:, tile])
        dscore = (prob * (dprob - delta[:, tile])).astype(bf16)
        for keys, cols, part in key_blocks(block, blocks):
            prob_ref[keys, cols] = prob_low[part]
            ds_ref[keys, cols] = dscore[part]
        dq = nn(key_t[:, low:high], dscore) * scale
        dqkv_ref[0, outs, tile] = dq.astype(bf16)
    query = qkv_ref[0, rows, :].T
    do = do_t.T
    for block in range(blocks):
        tile = slice(block * B, (block + 1) * B)
        queries, cols = query_blocks(block, blocks)
        dv = nn(prob_ref[tile, cols], do[queries])
        dqkv_ref[2, outs, tile] = dv.astype(bf16).T
        dk = nn(ds_ref[tile, cols], query[queries])
        dqkv_ref[1, outs, tile] = dk.astype(bf16).T


def normalize(values):
    center = values - jnp.mean(values, axis=0, keepdims=True)
    spread = jnp.mean(center * center, axis=0, keepdims=True)
    scale = lax.rsqrt(spread + norm_eps)
    return center * scale, scale


def normalize_back(dn, n, scale):
    mean_one = jnp.mean(dn, axis=0, keepdims=True)
    mean_two = jnp.mean(dn * n, axis=0, keepdims=True)
    return (dn - mean_one - n * mean_two) * scale


def gelu_pair(u):
    c0 = 0.7978845608028654
    c1 = c0 * 0.044715
    square = u * u
    t = jnp.tanh(u * (c0 + c1 * square))
    half = 0.5 * u
    cdf = 0.5 + 0.5 * t
    z = u * cdf
    slope = cdf + half * (1.0 - t * t) * (c0 + (3.0 * c1) * square)
    return z, slope


def lanes_sum(values):
    return values[:, :128] + values[:, 128:]


def turn_kernel(x_ref, x_t_ref):
    x_t_ref[...] = x_ref[...].T


def attend_kernel(first, size, x_ref, w_ref, seg_ref, *refs):
    if first:
        group, w_t_ref = first - 1, refs[0]
        count = w_t_ref.shape[0] // 3
        for i in range(3):
            at = i * x_ref.shape[0] + group * count
            w_t_ref[i * count : (i + 1) * count, :] = w_ref[:, at : at + count].T
        refs = refs[1:]
    else:
        w_t_ref = w_ref
    qkv_ref, o_ref, lse_ref, bias_ref = refs
    rows = o_ref.shape[0]
    fill_bias(seg_ref, bias_ref)
    for at in range(0, x_ref.shape[1], B):
        cols = slice(at, at + B)
        query = nn(w_t_ref[:rows, :], x_ref[:, cols]).astype(bf16)
        qkv_ref[0, :, cols] = query * jnp.asarray(size**-0.5, bf16)
        qkv_ref[1, :, cols] = nn(w_t_ref[rows : 2 * rows, :], x_ref[:, cols]).astype(bf16)
        qkv_ref[2, :, cols] = nn(w_t_ref[2 * rows :, :], x_ref[:, cols]).astype(bf16)

    def two_heads(pair, carry):
        for one in range(2):
            attend_head(2 * pair + one, size, qkv_ref, bias_ref, o_ref, lse_ref)
        return carry

    lax.fori_loop(0, rows // size // 2, two_heads, 0)


def join_heads(oa_ref, ob_ref, o_ref):
    rows = oa_ref.shape[0]
    o_ref[:rows, :] = oa_ref[...]
    o_ref[rows:, :] = ob_ref[...]


def feed_in_kernel(
    oa_ref,
    ob_ref,
    x_ref,
    wio_ref,
    o_ref,
    wo_t_ref,
    wi_t_ref,
    y_ref,
    n1_ref,
    stat_ref,
    yr_ref,
    z_ref,
    slope_ref,
):
    width = wio_ref.shape[0]
    hidden = wio_ref.shape[1] - width - 128
    join_heads(oa_ref, ob_ref, o_ref)
    wo_t_ref[...] = wio_ref[:, hidden : hidden + width].T
    wi_t_ref[...] = wio_ref[:, :hidden].T
    params = wio_ref[:, hidden + width :].astype(f32)
    gain_one, bias_one = params[:, 0:1], params[:, 1:2]
    for at in range(0, x_ref.shape[1], B):
        cols = slice(at, at + B)
        h = x_ref[:, cols].astype(f32) + nn(wo_t_ref[...], o_ref[:, cols])
        n1, s1 = normalize(h)
        n1_ref[:, cols] = n1.astype(bf16)
        stat_ref[:, cols] = jnp.broadcast_to(s1, (8, B))
        y = n1 * gain_one + bias_one
        yr_ref[:, cols] = y.astype(bf16)
        y_ref[:, cols] = y
        for f in range(0, hidden, CHUNK):
            u = nn(wi_t_ref[f : f + CHUNK, :], yr_ref[:, cols])
            z, slope = gelu_pair(u)
            z_ref[f : f + CHUNK, cols] = z.astype(bf16)
            slope_ref[f : f + CHUNK, cols] = slope.astype(bf16)


def feed_out_kernel(
    shards,
    y_ref,
    z_ref,
    wio_ref,
    groups_ref,
    wu_ref,
    wu_t_ref,
    next_ref,
    x2_ref,
    n2_ref,
    stat_ref,
):
    hidden, width = wu_ref.shape
    count = hidden // width
    rows = width // shards
    for shard in range(shards):
        for group in range(count):
            at = (shard * count + group) * rows
            part = slice(shard * rows, (shard + 1) * rows)
            wu_ref[at : at + rows, :] = groups_ref[part, group * width : (group + 1) * width]
    wu_t_ref[...] = wu_ref[...].T
    params = wio_ref[:, hidden + width :].astype(f32)
    gain_two, bias_two = params[:, 2:3], params[:, 3:4]
    for at in range(0, y_ref.shape[1], B):
        cols = slice(at, at + B)
        h2 = y_ref[:, cols] + nn(wu_t_ref[...], z_ref[:, cols])
        n2, s2 = normalize(h2)
        n2_ref[:, cols] = n2.astype(bf16)
        stat_ref[:, cols] = jnp.broadcast_to(s2, (8, B))
        out = n2 * gain_two + bias_two
        next_ref[:, cols] = out
        x2_ref[:, cols] = out.astype(bf16)


def feed_last_kernel(
    oa_ref,
    ob_ref,
    x_ref,
    wio_ref,
    wu_ref,
    wo_t_ref,
    wi_t_ref,
    wu_t_ref,
    cot_ref,
    scale_ref,
    o_ref,
    mixed_ref,
    z_ref,
    du_ref,
    yr_ref,
    dfr_ref,
    dar_ref,
    dh_ref,
    do_ref,
    acc_ref,
    n1_ref,
):
    width = wio_ref.shape[0]
    hidden = wio_ref.shape[1] - width - 128
    join_heads(oa_ref, ob_ref, o_ref)
    params = wio_ref[:, hidden + width :].astype(f32)
    gain_one, bias_one = params[:, 0:1], params[:, 1:2]
    gain_two, bias_two = params[:, 2:3], params[:, 3:4]
    acc_ref[...] = jnp.zeros_like(acc_ref)

    for at in range(0, x_ref.shape[1], B):
        cols = slice(at, at + B)
        slot = at // B % 2
        h = x_ref[:, cols] + nn(wo_t_ref[...], o_ref[:, cols])
        n1, s1 = normalize(h)
        n1_ref[slot] = n1
        y = n1 * gain_one + bias_one
        yr_ref[:, cols] = y.astype(bf16)
        dh_ref[:, cols] = y
        for f in range(0, hidden, CHUNK):
            u = nn(wi_t_ref[f : f + CHUNK, :], yr_ref[:, cols])
            z, slope = gelu_pair(u)
            z_ref[f : f + CHUNK, cols] = z.astype(bf16)
            du_ref[f : f + CHUNK, cols] = slope.astype(bf16)
        h2 = dh_ref[:, cols] + nn(wu_t_ref[...], z_ref[:, cols])
        n2, s2 = normalize(h2)
        out = n2 * gain_two + bias_two
        mixed_ref[cols, :] = out.astype(bf16).T
        grad = cot_ref[cols, :].T * scale_ref[0:1, cols]
        acc_ref[2] += lanes_sum(grad * n2)
        acc_ref[3] += lanes_sum(grad)
        dh2 = normalize_back(grad * gain_two, n2, s2)
        dh_ref[:, cols] = dh2
        dfr_ref[:, cols] = dh2.astype(bf16)
        for f in range(0, hidden, CHUNK):
            dz = nn(wu_ref[f : f + CHUNK, :], dfr_ref[:, cols])
            slope = du_ref[f : f + CHUNK, cols].astype(f32)
            du_ref[f : f + CHUNK, cols] = (dz * slope).astype(bf16)
        dy = dh_ref[:, cols] + nn(wio_ref[:, :hidden], du_ref[:, cols])
        acc_ref[0] += lanes_sum(dy * n1_ref[slot])
        acc_ref[1] += lanes_sum(dy)
        dh = normalize_back(dy * gain_one, n1_ref[slot], s1)
        dh_ref[:, cols] = dh
        dar_ref[:, cols] = dh.astype(bf16)
        do_ref[:, cols] = nn(wio_ref[:, hidden : hidden + width], dar_ref[:, cols]).astype(bf16)


def feed_back_kernel(
    g_ref,
    n1_ref,
    n2_ref,
    stat1_ref,
    stat2_ref,
    slope_ref,
    wio_ref,
    wu_ref,
    acc_in_ref,
    dh_ref,
    do_ref,
    du_ref,
    dfr_ref,
    dar_ref,
    acc_ref,
):
    width = wio_ref.shape[0]
    hidden = wio_ref.shape[1] - width - 128
    params = wio_ref[:, hidden + width :].astype(f32)
    gain_one, gain_two = params[:, 0:1], params[:, 2:3]
    acc_ref[...] = acc_in_ref[...]
    for at in range(0, g_ref.shape[1], B):
        cols = slice(at, at + B)
        grad = g_ref[:, cols]
        n2 = n2_ref[:, cols].astype(f32)
        acc_ref[2] += lanes_sum(grad * n2)
        acc_ref[3] += lanes_sum(grad)
        dh2 = normalize_back(grad * gain_two, n2, stat2_ref[0:1, cols])
        dh_ref[:, cols] = dh2
        dfr_ref[:, cols] = dh2.astype(bf16)
        for f in range(0, hidden, CHUNK):
            dz = nn(wu_ref[f : f + CHUNK, :], dfr_ref[:, cols])
            slope = slope_ref[f : f + CHUNK, cols].astype(f32)
            du_ref[f : f + CHUNK, cols] = (dz * slope).astype(bf16)
        dy = dh_ref[:, cols] + nn(wio_ref[:, :hidden], du_ref[:, cols])
        n1 = n1_ref[:, cols].astype(f32)
        acc_ref[0] += lanes_sum(dy * n1)
        acc_ref[1] += lanes_sum(dy)
        dh = normalize_back(dy * gain_one, n1, stat1_ref[0:1, cols])
        dh_ref[:, cols] = dh
        dar_ref[:, cols] = dh.astype(bf16)
        do_ref[:, cols] = nn(wio_ref[:, hidden : hidden + width], dar_ref[:, cols]).astype(bf16)


def place(value, first, unit, core, keep_ref, send_ref, cols):
    for at in range(0, value.shape[0], unit):
        block = (first + at) // unit
        rows = slice(block // 2 * unit, block // 2 * unit + unit)
        part = value[at : at + unit]

        @pl.when(core == block % 2)
        def _():
            keep_ref[rows, cols] = part

        @pl.when(core != block % 2)
        def _():
            send_ref[rows, cols] = part


def partial_kernel(
    z_ref, dfr_ref, du_ref, yr_ref, o_ref, dar_ref, outer_ref, inner_ref, output_ref
):
    for first in range(0, z_ref.shape[0], CHUNK):
        part = slice(first, first + CHUNK)
        outer_ref[part, :] = nt(z_ref[part, :], dfr_ref[...]).astype(bf16)
        inner_ref[part, :] = nt(du_ref[part, :], yr_ref[...]).astype(bf16)
    for first in range(0, o_ref.shape[0], CHUNK):
        part = slice(first, first + CHUNK)
        output_ref[part, :] = nt(o_ref[part, :], dar_ref[...]).astype(bf16)


def outer_grad_kernel(
    shards,
    core_ref,
    z_ref,
    dfr_ref,
    more_ref,
    o_ref,
    dar_ref,
    more_o_ref,
    acc_ref,
    keep_ref,
    send_ref,
):
    core = core_ref[0]
    hidden, width = z_ref.shape[0], dfr_ref.shape[0]
    unit = width // shards // 2
    groups = hidden // width
    per_group = hidden // shards // groups
    for first in range(0, hidden, 256):
        part = slice(first, first + 256)
        dwu = nt(z_ref[part, :], dfr_ref[...]) + more_ref[part, :].astype(f32)
        dwu = dwu.astype(bf16)
        for at in range(0, 256, per_group):
            block = (first + at) // per_group
            shard, group = block // groups, block % groups
            cols = slice(group * width, (group + 1) * width)
            rows = dwu[at : at + per_group]
            place(rows, shard * per_group, unit, core, keep_ref, send_ref, cols)
    for first in range(0, width, CHUNK):
        part = slice(first, first + CHUNK)
        dwo = nt(o_ref[part, :], dar_ref[...]) + more_o_ref[part, :].astype(f32)
        place(dwo.astype(bf16), first, unit, core, keep_ref, send_ref, slice(hidden, hidden + width))
    lane = lax.broadcasted_iota(jnp.int32, (width, 128), 1)
    dpar = jnp.zeros((width, 128), f32)
    for i in range(4):
        dpar = jnp.where(lane == i, jnp.sum(acc_ref[i], axis=1, keepdims=True), dpar)
    last = slice(hidden + width, hidden + width + 128)
    place(dpar.astype(bf16), 0, unit, core, keep_ref, send_ref, last)


def inner_grad_kernel(shards, core_ref, yr_ref, du_ref, more_ref, keep_ref, send_ref):
    core = core_ref[0]
    width, hidden = yr_ref.shape[0], du_ref.shape[0]
    unit = width // shards // 2
    for first in range(0, hidden, CHUNK):
        part = slice(first, first + CHUNK)
        dwi_t = nt(du_ref[part, :], yr_ref[...]) + more_ref[part, :].astype(f32)
        place(dwi_t.astype(bf16).T, 0, unit, core, keep_ref, send_ref, part)


def attend_back_kernel(
    first, size, qkv_ref, o_ref, do_ref, lse_ref, seg_ref, x_ref, dqkv_ref, more_ref, *refs
):
    bias_ref, prob_ref, ds_ref = refs
    rows = dqkv_ref.shape[1]
    fill_bias(seg_ref, bias_ref)
    here = slice(first, first + rows)

    def two_heads(pair, carry):
        for one in range(2):
            head = 2 * pair + one
            attend_head_back(
                head,
                head,
                size,
                qkv_ref,
                o_ref.at[here],
                do_ref.at[here],
                lse_ref,
                bias_ref,
                prob_ref.at[one],
                ds_ref.at[one],
                dqkv_ref,
            )
        return carry

    lax.fori_loop(0, rows // size // 2, two_heads, 0)
    for i in range(3):
        more_ref[:, i * rows : (i + 1) * rows] = nt(x_ref[...], dqkv_ref[i]).astype(bf16)


def attend_part_kernel(
    p, size, shards, qkv_ref, o_ref, do_ref, lse_ref, seg_ref, *refs
):
    grads = p % 2 == 1
    if grads:
        core_ref, x1_ref, before_ref, more_ref = refs[:4]
        dqkv_ref, keep_ref, send_ref, bias_ref, prob_ref, ds_ref = refs[4:]
    else:
        dqkv_ref, bias_ref, prob_ref, ds_ref = refs
    fill_bias(seg_ref, bias_ref)
    rows = qkv_ref.shape[1]
    here = slice(p // 2 * rows, (p // 2 + 1) * rows)
    for one in range(2):
        attend_head_back(
            p % 2 * 2 + one,
            one,
            size,
            qkv_ref,
            o_ref.at[here],
            do_ref.at[here],
            lse_ref,
            bias_ref,
            prob_ref.at[one],
            ds_ref.at[one],
            dqkv_ref,
        )
    if not grads:
        return
    core = core_ref[0]
    unit = x1_ref.shape[0] // shards // 2
    for i in range(3):
        joined = jnp.concatenate([before_ref[i], dqkv_ref[i]], axis=0)
        cols = slice(i * rows, (i + 1) * rows)
        dw = nt(x1_ref[...], joined) + more_ref[:, cols].astype(f32)
        place(dw.astype(bf16), 0, unit, core, keep_ref, send_ref, cols)


def input_kernel(turned, w_ref, dh_ref, *refs):
    parts, grad_ref, join_ref = refs[:-2], refs[-2], refs[-1]
    length = dh_ref.shape[1]
    at = 0
    for i in range(3):
        for part in parts:
            rows = part.shape[1]
            join_ref[at : at + rows, :] = part[i]
            at += rows
    for at in range(0, length, B):
        cols = slice(at, at + B)
        grad = dh_ref[:, cols] + nn(w_ref[...], join_ref[:, cols])
        if turned:
            grad_ref[cols, :] = grad.T
        else:
            grad_ref[:, cols] = grad


VM = pl.BlockSpec(memory_space=pltpu.VMEM)
SM = pl.BlockSpec(memory_space=pltpu.SMEM)


def call(kernel, outs, scratch, args, specs=None, cost=10, limit=6, alias={}, deps=()):
    count, after = len(args), len(args) + len(deps)

    def run(*refs):
        kernel(*refs[:count], *refs[after:])

    return pl.pallas_call(
        run,
        out_shape=[jax.ShapeDtypeStruct(shape, dtype) for shape, dtype in outs],
        in_specs=(specs if specs else [VM] * count) + [pl.BlockSpec(memory_space=pl.ANY)] * len(deps),
        out_specs=[VM] * len(outs),
        scratch_shapes=[pltpu.VMEM(*one) for one in scratch],
        input_output_aliases=alias,
        cost_estimate=pl.CostEstimate(
            flops=cost * 1000000000, bytes_accessed=cost * 3000000, transcendentals=0
        ),
        compiler_params=pltpu.CompilerParams(vmem_limit_bytes=limit * 2**20),
    )(*args, *deps)


def flip(value, axis, bit):
    count = lax.axis_size(axis)
    return lax.ppermute(value, axis, [(i, i ^ bit) for i in range(count)])


def bit_of(axis, bit):
    return lax.rem(lax.div(lax.axis_index(axis), bit), 2)


def bits_of(axis):
    count = lax.axis_size(axis)
    found = []
    bit = count // 2
    while bit:
        found.append((axis, bit))
        bit //= 2
    return found


def both(bit, mine, other, dim):
    low = jnp.concatenate([mine, other], axis=dim)
    high = jnp.concatenate([other, mine], axis=dim)
    return jnp.where(bit == 0, low, high)


def my_half(block):
    rows = block.shape[0] // 2
    return lax.dynamic_slice_in_dim(block, bit_of("dp", 1) * rows, rows, axis=0)[None]


class Gather:
    def __init__(self, mine):
        *steps, self.last = reversed(bits_of("shard"))
        for axis, bit in steps:
            mine = both(bit_of(axis, bit), mine, flip(mine, axis, bit), 0)
        self.mine = mine
        self.came = flip(mine, *self.last)

    def merge(self, *after):
        came = tie(self.came, *after) if after else self.came
        return both(bit_of(*self.last), self.mine, came, 0)


def over_cores(mine):
    full = both(bit_of("dp", 1), mine, flip(mine, "dp", 1), 1)
    return full.reshape(-1, mine.shape[-1])


class Sum:
    def __init__(self, keep, send):
        self.labels = bits_of("shard") + bits_of("dp")[:-1]
        self.cols = keep.shape[1]
        self.unit = keep.shape[0] // 2 ** len(self.labels)
        self.keep = keep
        self.sent = send
        self.came = [flip(send, "dp", 1)]
        self.value = None
        self.left = list(self.labels)

    def after(self, other):
        if self.value is None:
            self.keep = tie(self.keep, other)
        else:
            self.value = tie(self.value, other)

    def settle(self):
        if self.value is not None:
            return
        total = self.keep.astype(f32)
        for came in self.came:
            total += came.astype(f32)
        self.value = total.astype(bf16).reshape((2,) * len(self.left) + (self.unit, self.cols))

    def halve(self, axis, bit):
        self.settle()
        dim = self.left.index((axis, bit))
        me = bit_of(axis, bit)
        self.sent = lax.dynamic_index_in_dim(self.value, 1 - me, dim, keepdims=False)
        self.keep = lax.dynamic_index_in_dim(self.value, me, dim, keepdims=False)
        self.came = [flip(self.sent, axis, bit)]
        self.left.remove((axis, bit))
        self.value = None

    def masks(self):
        count = len(self.last)
        for k in range(1, 2**count):
            bits = (bit for i, (_, bit) in enumerate(self.last) if k >> (count - 1 - i) & 1)
            yield k, sum(bits)

    def scatter(self):
        self.settle()
        self.last = list(self.left)
        value = self.value.reshape(-1, self.unit, self.cols)
        me = 0
        for axis, bit in self.last:
            me = 2 * me + bit_of(axis, bit)
        self.keep = lax.dynamic_index_in_dim(value, me, 0, keepdims=False)
        self.came = []
        for k, mask in self.masks():
            send = lax.dynamic_index_in_dim(value, lax.bitwise_xor(me, k), 0, keepdims=False)
            self.came.append(flip(send, "dp", mask))
        self.left = []
        self.value = None

    def collect(self):
        self.settle()
        pieces = [self.value]
        for _, mask in self.masks():
            pieces.append(flip(self.value, "dp", mask))
        for axis, bit in reversed(self.last):
            me = bit_of(axis, bit)
            pairs = zip(pieces[::2], pieces[1::2])
            pieces = [both(me, low[None], high[None], 0) for low, high in pairs]
        self.value = pieces[0]
        self.left = list(self.last)

    def double(self, axis, bit):
        order = [label for label in self.labels if label in self.left or label == (axis, bit)]
        dim = order.index((axis, bit))
        mine = jnp.expand_dims(self.value, dim)
        self.value = both(bit_of(axis, bit), mine, flip(mine, axis, bit), dim)
        self.left = order

    def finish(self):
        self.value = self.value.reshape(-1, self.cols)
        self.other = flip(self.value, "dp", 1)

    def columns(self, first, last):
        mine, other = self.value[:, first:last], self.other[:, first:last]
        return both(bit_of("dp", 1), mine, other, 0).astype(f32)


def copy_kernel(value_ref, copy_ref):
    copy_ref[...] = value_ref[...]


def copy_after(value, *deps):
    flat = value.reshape(-1, value.shape[-1])
    out = [(flat.shape, flat.dtype)]
    (copy,) = call(copy_kernel, out, [], (flat,), None, 1, deps=deps)
    return copy.reshape(value.shape)


def join(*sums):
    for one in sums:
        one.settle()
    joined = object.__new__(Sum)
    joined.labels, joined.unit, joined.left = sums[0].labels, sums[0].unit, sums[0].left
    joined.last = getattr(sums[0], "last", None)
    joined.cols = sum(one.cols for one in sums)
    joined.value = jnp.concatenate([one.value for one in sums], axis=-1)
    return joined


def tie(value, *others):
    return lax.optimization_barrier((value,) + others)[0]


def compute(tokens, seg_rows, scale_rows, cotangent, weights, hidden):
    length, width = tokens.shape
    *qkv, wo_block, vectors, wi_block, wu_block = weights

    def later(done):
        *args, _ = lax.optimization_barrier((wo_block, wi_block, wu_block, *vectors, done))
        wo, wi, wu, *params = args
        stacked = jnp.pad(jnp.stack(params, axis=1), ((0, 0), (0, 128 - len(params))))
        groups = jnp.split(wu, hidden // width, axis=0)
        parts = ((wi, wo, stacked), groups)
        return [jnp.concatenate([my_half(w) for w in part], axis=-1) for part in parts]

    size = width // H
    rows = width // 2
    shards = lax.axis_size("shard")
    core = bit_of("dp", 1).reshape(1)
    tall = ((width, length), bf16)
    tall32 = ((width, length), f32)
    wide = ((hidden, length), bf16)
    bias = ((length, 3 * B), f32)
    pair = ((2, length, 3 * B), bf16)
    shapes = [((3, rows, length), bf16), ((rows, length), bf16), ((H // 2, 8, length), f32)]

    half = width // 2
    packed = jnp.concatenate([my_half(w) for w in qkv], axis=-1)
    mine = Gather(packed).merge()
    wqkv = over_cores(mine)
    wio_part, wu_part = later(packed)
    wio_gather = Gather(tie(wio_part, mine))
    (x1,) = call(turn_kernel, [tall], [], (tie(tokens, packed),), None, 1)
    attend = functools.partial(attend_kernel, 1, size)
    turned = [((3 * rows, width), bf16)]
    wa_t, qkv1a, o1a, lse1a = call(attend, turned + shapes, [bias], (x1, wqkv, seg_rows))
    wio_mine = wio_gather.merge(o1a)
    wio = over_cores(wio_mine)
    wu_part = tie(wu_part, wio_mine)
    wu_gather = Gather(wu_part)
    attend = functools.partial(attend_kernel, 2, size)
    wb_t, qkv1b, o1b, lse1b = call(
        attend, turned + shapes, [bias], (x1, wqkv, tie(seg_rows, wio_mine, wu_part))
    )
    o1, wo_t, wi_t, y1, n11, stat11, yr1, z1, slope1 = call(
        feed_in_kernel,
        [tall, ((width, width), bf16), ((hidden, width), bf16), tall32, tall]
        + [((8, length), f32), tall, wide, wide],
        [],
        (o1a, o1b, x1, wio),
    )
    wu_groups = over_cores(wu_gather.merge(o1b))
    wu, wu_t, next1, x2, n21, stat12 = call(
        functools.partial(feed_out_kernel, shards),
        [((hidden, width), bf16), ((width, hidden), bf16), tall32, tall, tall]
        + [((8, length), f32)],
        [],
        (y1, z1, wio, wu_groups),
    )
    attend = functools.partial(attend_kernel, 0, size)
    qkv2a, o2a, lse2a = call(attend, shapes, [bias], (x2, wa_t, seg_rows), limit=6)
    qkv2b, o2b, lse2b = call(attend, shapes, [bias], (x2, wb_t, seg_rows), limit=6)
    o2, mixed, z2, du2, yr2, dfr2, dar2, dh2, do2, acc = call(
        feed_last_kernel,
        [tall, ((length, width), bf16), wide, wide, tall, tall, tall, tall32, tall]
        + [((4, width, 128), f32)],
        [((2, width, B), f32)],
        (o2a, o2b, next1, wio, wu, wo_t, wi_t, wu_t, cotangent, scale_rows),
        limit=10,
    )
    back = [bias, pair, pair]
    more_u, more_i, more_o = call(
        partial_kernel,
        [((hidden, width), bf16)] * 2 + [((width, width), bf16)],
        [],
        (z2, dfr2, du2, yr2, o2, dar2),
        limit=4,
    )
    dqkv2, more = [], []
    more_qkv = shapes[:1] + [((width, 3 * rows), bf16)]
    for group, (qkv, lse) in enumerate(((qkv2a, lse2a), (qkv2b, lse2b))):
        kernel = functools.partial(attend_back_kernel, group * rows, size)
        args = (qkv, o2, do2, lse, seg_rows, x2)
        found = call(kernel, more_qkv, back, args, limit=10, deps=(more_u,))
        dqkv2.append(found[0])
        more.append(found[1])
    joined = [((3 * width, length), bf16)]
    (grad1,) = call(
        functools.partial(input_kernel, False), [tall32], joined, (wqkv, dh2, *dqkv2), None, 3, 4
    )
    dh1, do1, du1, dfr1, dar1, acc = call(
        feed_back_kernel,
        [tall32, tall, wide, tall, tall, ((4, width, 128), f32)],
        [],
        (grad1, n11, n21, stat11, stat12, slope1, wio, wu, acc),
        alias={5: 2, 8: 5},
    )
    keep_u, send_u = call(
        functools.partial(outer_grad_kernel, shards),
        [((half, hidden + width + 128), bf16)] * 2,
        [],
        (core, z1, dfr1, more_u, o1, dar1, more_o, acc),
        [SM] + [VM] * 7,
        limit=4,
    )
    outer = Sum(keep_u, send_u)
    keep_i, send_i = call(
        functools.partial(inner_grad_kernel, shards),
        [((half, hidden), bf16)] * 2,
        [],
        (core, yr1, du1, more_i),
        [SM] + [VM] * 3,
        limit=4,
        deps=(send_u,),
    )
    parts = []

    def part(p, seg):
        qkv, lse = ((qkv1a, lse1a), (qkv1b, lse1b))[p // 2]
        args = (qkv, o1, do1, lse, seg)
        specs = [VM] * 5
        outs = [((3, 2 * size, length), bf16)]
        if p % 2:
            args += (core, x1, parts[-1], more[p // 2])
            specs += [SM] + [VM] * 3
            outs += [((half, 3 * rows), bf16)] * 2
        kernel = functools.partial(attend_part_kernel, p, size, shards)
        results = call(kernel, outs, back, args, specs, 15, 10)
        parts.append(results[0])
        return results[1:]

    y_bit = bits_of("dp")[-2]
    x_bits = bits_of("shard")
    outer.after(send_i)
    for label in x_bits:
        outer.halve(*label)
    inner = Sum(keep_i, tie(send_i, outer.sent))
    part(0, tie(seg_rows, outer.sent))
    inner.after(parts[0])
    inner.halve(*y_bit)
    first = Sum(*part(1, tie(seg_rows, inner.sent)))
    outer.after(parts[1])
    outer.halve(*y_bit)
    inner.after(parts[1])
    for label in x_bits:
        inner.halve(*label)
    part(2, tie(seg_rows, inner.sent, outer.sent, first.sent))
    for one in (first, inner, outer):
        one.after(parts[2])
    for label in x_bits:
        first.halve(*label)
    feed = join(outer, inner)
    feed.scatter()
    second = Sum(*part(3, tie(seg_rows, feed.keep, first.sent)))
    feed.after(second.sent)
    feed.settle()
    for label in x_bits:
        second.halve(*label)
    feed.after(second.sent)
    feed.collect()
    first.after(second.sent)
    heads = join(first, second)
    heads.halve(*y_bit)
    (input_grad,) = call(
        functools.partial(input_kernel, True),
        [((length, width), f32)],
        joined,
        (wqkv, dh1, *parts),
        None,
        5,
        5,
        deps=(heads.sent,),
    )
    feed.double(*y_bit)
    feed.finish()
    heads.scatter()
    heads.settle()
    heads.collect()
    inner_at = hidden + width + 128
    dwu = [feed.columns(at, at + width) for at in range(0, hidden, width)]
    dwu = jnp.concatenate(dwu, axis=0)
    dwo = feed.columns(hidden, hidden + width)
    dpar = feed.columns(hidden + width, inner_at)
    dwi = feed.columns(inner_at, inner_at + hidden)
    heads.value = copy_after(heads.value, dwu, dwi, dwo)
    heads.double(*y_bit)
    heads.finish()
    dqkv = [
        jnp.concatenate([heads.columns(c, c + half) for c in (at, at + 3 * half)], axis=1)
        for at in range(0, 3 * half, half)
    ]
    return (mixed, input_grad, *dqkv, dwo, dwi, dwu, *(dpar[:, i] for i in range(4)))


def body(
    tokens,
    segment_ids,
    row_counts,
    global_count,
    cotangent,
    query_weight,
    key_weight,
    value_weight,
    output_weight,
    inner_weight,
    outer_weight,
    attn_gain,
    attn_bias,
    feed_gain,
    feed_bias,
):
    length, width = tokens.shape
    hidden = inner_weight.shape[1]
    half = width // 2
    weights = (query_weight, key_weight, value_weight, output_weight)
    weights += ((attn_gain, attn_bias, feed_gain, feed_bias), inner_weight, outer_weight)
    seg_rows = jnp.broadcast_to(segment_ids.astype(f32)[None], (8, length))
    valid = (jnp.arange(length) < row_counts[0]).astype(f32)
    tokens_total = lax.axis_size("dp") * lax.axis_size("shard") * length
    factor = jnp.float32(tokens_total) / global_count[0].astype(f32)
    scale_rows = jnp.broadcast_to((valid * factor)[None], (8, length))
    return compute(tokens, seg_rows, scale_rows, cotangent, weights, hidden)


def solution(mesh):
    rows = P(("dp", "shard"))
    rows_two = P(("dp", "shard"), None)
    two = P("shard", None)
    one = P("shard")
    in_specs = (rows_two, rows, rows, P(), rows_two) + (two,) * 6 + (one,) * 4
    out_specs = (rows_two, rows_two) + (two,) * 6 + (one,) * 4
    return jax.shard_map(body, mesh=mesh, in_specs=in_specs, out_specs=out_specs, check_vma=False)
```

```python
import functools

import jax
import jax.numpy as jnp
from jax import lax
from jax.experimental import pallas as pl
from jax.experimental.pallas import tpu as pltpu
from jax.sharding import PartitionSpec as P

H = 8
B = 256
CHUNK = 256
norm_eps = 1e-05
masked_score = -1e30
bf16 = jnp.bfloat16
f32 = jnp.float32


def nn(left, right):
    return lax.dot_general(left, right, (((1,), (0,)), ((), ())), preferred_element_type=f32)


def nt(left, right):
    return lax.dot_general(left, right, (((1,), (1,)), ((), ())), preferred_element_type=f32)


def band(block, blocks):
    return max(0, block - 1) * B, min(blocks, block + 2) * B


def key_blocks(block, blocks):
    low, high = band(block, blocks)
    for at in range(low, high, B):
        step = (block * B - at) // B + 1
        yield slice(at, at + B), slice(step * B, (step + 1) * B), slice(at - low, at - low + B)


def query_blocks(block, blocks):
    low, high = band(block, blocks)
    first = low - block * B + B
    return slice(low, high), slice(first, first + high - low)


def fill_bias(seg_ref, bias_ref):
    column = seg_ref[...].T[:, 0:1]
    blocks = bias_ref.shape[0] // B
    for block in range(blocks):
        row = seg_ref[0:1, block * B : (block + 1) * B]
        for keys, cols, _ in key_blocks(block, blocks):
            bias_ref[keys, cols] = jnp.where(column[keys] == row, 0.0, masked_score)


def bias_of(bias_ref, block, blocks):
    parts = [bias_ref[keys, cols] for keys, cols, _ in key_blocks(block, blocks)]
    return jnp.concatenate(parts, axis=0)


def attend_head(head, size, qkv_ref, bias_ref, o_ref, lse_ref):
    blocks = qkv_ref.shape[2] // B
    rows = pl.ds(pl.multiple_of(head * size, size), size)
    key = qkv_ref[1, rows, :].T
    for block in range(blocks):
        low, high = band(block, blocks)
        tile = slice(block * B, (block + 1) * B)
        score = nn(key[low:high], qkv_ref[0, rows, tile]) + bias_of(bias_ref, block, blocks)
        top = jnp.max(score, axis=0, keepdims=True)
        weight = jnp.exp(score - top)
        total = jnp.sum(weight, axis=0, keepdims=True)
        mixed = nn(qkv_ref[2, rows, low:high], weight.astype(bf16)) * (1.0 / total)
        o_ref[rows, tile] = mixed.astype(bf16)
        lse_ref[head, :, tile] = jnp.broadcast_to(top + jnp.log(total), (8, B))


def attend_head_back(
    head, out, size, qkv_ref, o_ref, do_ref, lse_ref, bias_ref, prob_ref, ds_ref, dqkv_ref
):
    length = qkv_ref.shape[2]
    blocks = length // B
    scale = size**-0.5
    rows = pl.ds(pl.multiple_of(head * size, size), size)
    outs = pl.ds(pl.multiple_of(out * size, size), size)
    key_t = qkv_ref[1, rows, :]
    key = key_t.T
    value = qkv_ref[2, rows, :].T
    do_t = do_ref[rows, :]
    delta = jnp.sum(do_t.astype(f32) * o_ref[rows, :].astype(f32), axis=0, keepdims=True)
    for block in range(blocks):
        low, high = band(block, blocks)
        tile = slice(block * B, (block + 1) * B)
        score = nn(key[low:high], qkv_ref[0, rows, tile]) + bias_of(bias_ref, block, blocks)
        prob = jnp.exp(score - lse_ref[head, 0:1, tile])
        prob_low = prob.astype(bf16)
        dprob = nn(value[low:high], do_t[:, tile])
        dscore = (prob * (dprob - delta[:, tile])).astype(bf16)
        for keys, cols, part in key_blocks(block, blocks):
            prob_ref[keys, cols] = prob_low[part]
            ds_ref[keys, cols] = dscore[part]
        dq = nn(key_t[:, low:high], dscore) * scale
        dqkv_ref[0, outs, tile] = dq.astype(bf16)
    query = qkv_ref[0, rows, :].T
    do = do_t.T
    for block in range(blocks):
        tile = slice(block * B, (block + 1) * B)
        queries, cols = query_blocks(block, blocks)
        dv = nn(prob_ref[tile, cols], do[queries])
        dqkv_ref[2, outs, tile] = dv.astype(bf16).T
        dk = nn(ds_ref[tile, cols], query[queries])
        dqkv_ref[1, outs, tile] = dk.astype(bf16).T


def normalize(values):
    center = values - jnp.mean(values, axis=0, keepdims=True)
    spread = jnp.mean(center * center, axis=0, keepdims=True)
    scale = lax.rsqrt(spread + norm_eps)
    return center * scale, scale


def normalize_back(dn, n, scale):
    mean_one = jnp.mean(dn, axis=0, keepdims=True)
    mean_two = jnp.mean(dn * n, axis=0, keepdims=True)
    return (dn - mean_one - n * mean_two) * scale


def gelu_pair(u):
    c0 = 0.7978845608028654
    c1 = c0 * 0.044715
    square = u * u
    t = jnp.tanh(u * (c0 + c1 * square))
    half = 0.5 * u
    cdf = 0.5 + 0.5 * t
    z = u * cdf
    slope = cdf + half * (1.0 - t * t) * (c0 + (3.0 * c1) * square)
    return z, slope


def lanes_sum(values):
    return values[:, :128] + values[:, 128:]


def turn_kernel(x_ref, x_t_ref):
    x_t_ref[...] = x_ref[...].T


def attend_kernel(first, size, x_ref, w_ref, seg_ref, *refs):
    if first:
        group, w_t_ref = first - 1, refs[0]
        count = w_t_ref.shape[0] // 3
        for i in range(3):
            at = i * x_ref.shape[0] + group * count
            w_t_ref[i * count : (i + 1) * count, :] = w_ref[:, at : at + count].T
        refs = refs[1:]
    else:
        w_t_ref = w_ref
    qkv_ref, o_ref, lse_ref, bias_ref = refs
    rows = o_ref.shape[0]
    fill_bias(seg_ref, bias_ref)
    for at in range(0, x_ref.shape[1], B):
        cols = slice(at, at + B)
        query = nn(w_t_ref[:rows, :], x_ref[:, cols]).astype(bf16)
        qkv_ref[0, :, cols] = query * jnp.asarray(size**-0.5, bf16)
        qkv_ref[1, :, cols] = nn(w_t_ref[rows : 2 * rows, :], x_ref[:, cols]).astype(bf16)
        qkv_ref[2, :, cols] = nn(w_t_ref[2 * rows :, :], x_ref[:, cols]).astype(bf16)

    def two_heads(pair, carry):
        for one in range(2):
            attend_head(2 * pair + one, size, qkv_ref, bias_ref, o_ref, lse_ref)
        return carry

    lax.fori_loop(0, rows // size // 2, two_heads, 0)


def join_heads(oa_ref, ob_ref, o_ref):
    rows = oa_ref.shape[0]
    o_ref[:rows, :] = oa_ref[...]
    o_ref[rows:, :] = ob_ref[...]


def feed_in_kernel(
    oa_ref,
    ob_ref,
    x_ref,
    wio_ref,
    o_ref,
    wo_t_ref,
    wi_t_ref,
    y_ref,
    n1_ref,
    stat_ref,
    yr_ref,
    z_ref,
    slope_ref,
):
    width = wio_ref.shape[0]
    hidden = wio_ref.shape[1] - width - 128
    join_heads(oa_ref, ob_ref, o_ref)
    wo_t_ref[...] = wio_ref[:, hidden : hidden + width].T
    wi_t_ref[...] = wio_ref[:, :hidden].T
    params = wio_ref[:, hidden + width :].astype(f32)
    gain_one, bias_one = params[:, 0:1], params[:, 1:2]
    for at in range(0, x_ref.shape[1], B):
        cols = slice(at, at + B)
        h = x_ref[:, cols].astype(f32) + nn(wo_t_ref[...], o_ref[:, cols])
        n1, s1 = normalize(h)
        n1_ref[:, cols] = n1.astype(bf16)
        stat_ref[:, cols] = jnp.broadcast_to(s1, (8, B))
        y = n1 * gain_one + bias_one
        yr_ref[:, cols] = y.astype(bf16)
        y_ref[:, cols] = y
        for f in range(0, hidden, CHUNK):
            u = nn(wi_t_ref[f : f + CHUNK, :], yr_ref[:, cols])
            z, slope = gelu_pair(u)
            z_ref[f : f + CHUNK, cols] = z.astype(bf16)
            slope_ref[f : f + CHUNK, cols] = slope.astype(bf16)


def feed_out_kernel(
    shards,
    y_ref,
    z_ref,
    wio_ref,
    groups_ref,
    wu_ref,
    wu_t_ref,
    next_ref,
    x2_ref,
    n2_ref,
    stat_ref,
):
    hidden, width = wu_ref.shape
    count = hidden // width
    rows = width // shards
    for shard in range(shards):
        for group in range(count):
            at = (shard * count + group) * rows
            part = slice(shard * rows, (shard + 1) * rows)
            wu_ref[at : at + rows, :] = groups_ref[part, group * width : (group + 1) * width]
    wu_t_ref[...] = wu_ref[...].T
    params = wio_ref[:, hidden + width :].astype(f32)
    gain_two, bias_two = params[:, 2:3], params[:, 3:4]
    for at in range(0, y_ref.shape[1], B):
        cols = slice(at, at + B)
        h2 = y_ref[:, cols] + nn(wu_t_ref[...], z_ref[:, cols])
        n2, s2 = normalize(h2)
        n2_ref[:, cols] = n2.astype(bf16)
        stat_ref[:, cols] = jnp.broadcast_to(s2, (8, B))
        out = n2 * gain_two + bias_two
        next_ref[:, cols] = out
        x2_ref[:, cols] = out.astype(bf16)


def feed_last_kernel(
    oa_ref,
    ob_ref,
    x_ref,
    wio_ref,
    wu_ref,
    wo_t_ref,
    wi_t_ref,
    wu_t_ref,
    cot_ref,
    scale_ref,
    o_ref,
    mixed_ref,
    z_ref,
    du_ref,
    yr_ref,
    dfr_ref,
    dar_ref,
    dh_ref,
    do_ref,
    acc_ref,
    n1_ref,
):
    width = wio_ref.shape[0]
    hidden = wio_ref.shape[1] - width - 128
    join_heads(oa_ref, ob_ref, o_ref)
    params = wio_ref[:, hidden + width :].astype(f32)
    gain_one, bias_one = params[:, 0:1], params[:, 1:2]
    gain_two, bias_two = params[:, 2:3], params[:, 3:4]
    acc_ref[...] = jnp.zeros_like(acc_ref)

    for at in range(0, x_ref.shape[1], B):
        cols = slice(at, at + B)
        slot = at // B % 2
        h = x_ref[:, cols] + nn(wo_t_ref[...], o_ref[:, cols])
        n1, s1 = normalize(h)
        n1_ref[slot] = n1
        y = n1 * gain_one + bias_one
        yr_ref[:, cols] = y.astype(bf16)
        dh_ref[:, cols] = y
        for f in range(0, hidden, CHUNK):
            u = nn(wi_t_ref[f : f + CHUNK, :], yr_ref[:, cols])
            z, slope = gelu_pair(u)
            z_ref[f : f + CHUNK, cols] = z.astype(bf16)
            du_ref[f : f + CHUNK, cols] = slope.astype(bf16)
        h2 = dh_ref[:, cols] + nn(wu_t_ref[...], z_ref[:, cols])
        n2, s2 = normalize(h2)
        out = n2 * gain_two + bias_two
        mixed_ref[cols, :] = out.astype(bf16).T
        grad = cot_ref[cols, :].T * scale_ref[0:1, cols]
        acc_ref[2] += lanes_sum(grad * n2)
        acc_ref[3] += lanes_sum(grad)
        dh2 = normalize_back(grad * gain_two, n2, s2)
        dh_ref[:, cols] = dh2
        dfr_ref[:, cols] = dh2.astype(bf16)
        for f in range(0, hidden, CHUNK):
            dz = nn(wu_ref[f : f + CHUNK, :], dfr_ref[:, cols])
            slope = du_ref[f : f + CHUNK, cols].astype(f32)
            du_ref[f : f + CHUNK, cols] = (dz * slope).astype(bf16)
        dy = dh_ref[:, cols] + nn(wio_ref[:, :hidden], du_ref[:, cols])
        acc_ref[0] += lanes_sum(dy * n1_ref[slot])
        acc_ref[1] += lanes_sum(dy)
        dh = normalize_back(dy * gain_one, n1_ref[slot], s1)
        dh_ref[:, cols] = dh
        dar_ref[:, cols] = dh.astype(bf16)
        do_ref[:, cols] = nn(wio_ref[:, hidden : hidden + width], dar_ref[:, cols]).astype(bf16)


def feed_back_kernel(
    g_ref,
    n1_ref,
    n2_ref,
    stat1_ref,
    stat2_ref,
    slope_ref,
    wio_ref,
    wu_ref,
    acc_in_ref,
    dh_ref,
    do_ref,
    du_ref,
    dfr_ref,
    dar_ref,
    acc_ref,
):
    width = wio_ref.shape[0]
    hidden = wio_ref.shape[1] - width - 128
    params = wio_ref[:, hidden + width :].astype(f32)
    gain_one, gain_two = params[:, 0:1], params[:, 2:3]
    acc_ref[...] = acc_in_ref[...]
    for at in range(0, g_ref.shape[1], B):
        cols = slice(at, at + B)
        grad = g_ref[:, cols]
        n2 = n2_ref[:, cols].astype(f32)
        acc_ref[2] += lanes_sum(grad * n2)
        acc_ref[3] += lanes_sum(grad)
        dh2 = normalize_back(grad * gain_two, n2, stat2_ref[0:1, cols])
        dh_ref[:, cols] = dh2
        dfr_ref[:, cols] = dh2.astype(bf16)
        for f in range(0, hidden, CHUNK):
            dz = nn(wu_ref[f : f + CHUNK, :], dfr_ref[:, cols])
            slope = slope_ref[f : f + CHUNK, cols].astype(f32)
            du_ref[f : f + CHUNK, cols] = (dz * slope).astype(bf16)
        dy = dh_ref[:, cols] + nn(wio_ref[:, :hidden], du_ref[:, cols])
        n1 = n1_ref[:, cols].astype(f32)
        acc_ref[0] += lanes_sum(dy * n1)
        acc_ref[1] += lanes_sum(dy)
        dh = normalize_back(dy * gain_one, n1, stat1_ref[0:1, cols])
        dh_ref[:, cols] = dh
        dar_ref[:, cols] = dh.astype(bf16)
        do_ref[:, cols] = nn(wio_ref[:, hidden : hidden + width], dar_ref[:, cols]).astype(bf16)


def place(value, first, unit, core, keep_ref, send_ref, cols):
    for at in range(0, value.shape[0], unit):
        block = (first + at) // unit
        rows = slice(block // 2 * unit, block // 2 * unit + unit)
        part = value[at : at + unit]

        @pl.when(core == block % 2)
        def _():
            keep_ref[rows, cols] = part

        @pl.when(core != block % 2)
        def _():
            send_ref[rows, cols] = part


def partial_kernel(
    z_ref, dfr_ref, du_ref, yr_ref, o_ref, dar_ref, outer_ref, inner_ref, output_ref
):
    for first in range(0, z_ref.shape[0], CHUNK):
        part = slice(first, first + CHUNK)
        outer_ref[part, :] = nt(z_ref[part, :], dfr_ref[...]).astype(bf16)
        inner_ref[part, :] = nt(du_ref[part, :], yr_ref[...]).astype(bf16)
    for first in range(0, o_ref.shape[0], CHUNK):
        part = slice(first, first + CHUNK)
        output_ref[part, :] = nt(o_ref[part, :], dar_ref[...]).astype(bf16)


def outer_grad_kernel(
    shards,
    core_ref,
    z_ref,
    dfr_ref,
    more_ref,
    o_ref,
    dar_ref,
    more_o_ref,
    acc_ref,
    keep_ref,
    send_ref,
):
    core = core_ref[0]
    hidden, width = z_ref.shape[0], dfr_ref.shape[0]
    unit = width // shards // 2
    groups = hidden // width
    per_group = hidden // shards // groups
    for first in range(0, hidden, 256):
        part = slice(first, first + 256)
        dwu = nt(z_ref[part, :], dfr_ref[...]) + more_ref[part, :].astype(f32)
        dwu = dwu.astype(bf16)
        for at in range(0, 256, per_group):
            block = (first + at) // per_group
            shard, group = block // groups, block % groups
            cols = slice(group * width, (group + 1) * width)
            rows = dwu[at : at + per_group]
            place(rows, shard * per_group, unit, core, keep_ref, send_ref, cols)
    for first in range(0, width, CHUNK):
        part = slice(first, first + CHUNK)
        dwo = nt(o_ref[part, :], dar_ref[...]) + more_o_ref[part, :].astype(f32)
        place(dwo.astype(bf16), first, unit, core, keep_ref, send_ref, slice(hidden, hidden + width))
    lane = lax.broadcasted_iota(jnp.int32, (width, 128), 1)
    dpar = jnp.zeros((width, 128), f32)
    for i in range(4):
        dpar = jnp.where(lane == i, jnp.sum(acc_ref[i], axis=1, keepdims=True), dpar)
    last = slice(hidden + width, hidden + width + 128)
    place(dpar.astype(bf16), 0, unit, core, keep_ref, send_ref, last)


def inner_grad_kernel(shards, core_ref, yr_ref, du_ref, more_ref, keep_ref, send_ref):
    core = core_ref[0]
    width, hidden = yr_ref.shape[0], du_ref.shape[0]
    unit = width // shards // 2
    for first in range(0, hidden, CHUNK):
        part = slice(first, first + CHUNK)
        dwi_t = nt(du_ref[part, :], yr_ref[...]) + more_ref[part, :].astype(f32)
        place(dwi_t.astype(bf16).T, 0, unit, core, keep_ref, send_ref, part)


def attend_back_kernel(
    first, size, qkv_ref, o_ref, do_ref, lse_ref, seg_ref, x_ref, dqkv_ref, more_ref, *refs
):
    bias_ref, prob_ref, ds_ref = refs
    rows = dqkv_ref.shape[1]
    fill_bias(seg_ref, bias_ref)
    here = slice(first, first + rows)

    def two_heads(pair, carry):
        for one in range(2):
            head = 2 * pair + one
            attend_head_back(
                head,
                head,
                size,
                qkv_ref,
                o_ref.at[here],
                do_ref.at[here],
                lse_ref,
                bias_ref,
                prob_ref.at[one],
                ds_ref.at[one],
                dqkv_ref,
            )
        return carry

    lax.fori_loop(0, rows // size // 2, two_heads, 0)
    for i in range(3):
        more_ref[:, i * rows : (i + 1) * rows] = nt(x_ref[...], dqkv_ref[i]).astype(bf16)


def attend_part_kernel(
    p, size, shards, qkv_ref, o_ref, do_ref, lse_ref, seg_ref, *refs
):
    grads = p % 2 == 1
    if grads:
        core_ref, x1_ref, before_ref, more_ref = refs[:4]
        dqkv_ref, keep_ref, send_ref, bias_ref, prob_ref, ds_ref = refs[4:]
    else:
        dqkv_ref, bias_ref, prob_ref, ds_ref = refs
    fill_bias(seg_ref, bias_ref)
    rows = qkv_ref.shape[1]
    here = slice(p // 2 * rows, (p // 2 + 1) * rows)
    for one in range(2):
        attend_head_back(
            p % 2 * 2 + one,
            one,
            size,
            qkv_ref,
            o_ref.at[here],
            do_ref.at[here],
            lse_ref,
            bias_ref,
            prob_ref.at[one],
            ds_ref.at[one],
            dqkv_ref,
        )
    if not grads:
        return
    core = core_ref[0]
    unit = x1_ref.shape[0] // shards // 2
    for i in range(3):
        joined = jnp.concatenate([before_ref[i], dqkv_ref[i]], axis=0)
        cols = slice(i * rows, (i + 1) * rows)
        dw = nt(x1_ref[...], joined) + more_ref[:, cols].astype(f32)
        place(dw.astype(bf16), 0, unit, core, keep_ref, send_ref, cols)


def input_kernel(turned, w_ref, dh_ref, *refs):
    parts, grad_ref, join_ref = refs[:-2], refs[-2], refs[-1]
    length = dh_ref.shape[1]
    at = 0
    for i in range(3):
        for part in parts:
            rows = part.shape[1]
            join_ref[at : at + rows, :] = part[i]
            at += rows
    for at in range(0, length, B):
        cols = slice(at, at + B)
        grad = dh_ref[:, cols] + nn(w_ref[...], join_ref[:, cols])
        if turned:
            grad_ref[cols, :] = grad.T
        else:
            grad_ref[:, cols] = grad


VM = pl.BlockSpec(memory_space=pltpu.VMEM)
SM = pl.BlockSpec(memory_space=pltpu.SMEM)


def call(kernel, outs, scratch, args, specs=None, cost=10, limit=6, alias={}, deps=()):
    count, after = len(args), len(args) + len(deps)

    def run(*refs):
        kernel(*refs[:count], *refs[after:])

    return pl.pallas_call(
        run,
        out_shape=[jax.ShapeDtypeStruct(shape, dtype) for shape, dtype in outs],
        in_specs=(specs if specs else [VM] * count) + [pl.BlockSpec(memory_space=pl.ANY)] * len(deps),
        out_specs=[VM] * len(outs),
        scratch_shapes=[pltpu.VMEM(*one) for one in scratch],
        input_output_aliases=alias,
        cost_estimate=pl.CostEstimate(
            flops=cost * 1000000000, bytes_accessed=cost * 3000000, transcendentals=0
        ),
        compiler_params=pltpu.CompilerParams(vmem_limit_bytes=limit * 2**20),
    )(*args, *deps)


def flip(value, axis, bit):
    count = lax.axis_size(axis)
    return lax.ppermute(value, axis, [(i, i ^ bit) for i in range(count)])


def bit_of(axis, bit):
    return lax.rem(lax.div(lax.axis_index(axis), bit), 2)


def bits_of(axis):
    count = lax.axis_size(axis)
    found = []
    bit = count // 2
    while bit:
        found.append((axis, bit))
        bit //= 2
    return found


def both(bit, mine, other, dim):
    low = jnp.concatenate([mine, other], axis=dim)
    high = jnp.concatenate([other, mine], axis=dim)
    return jnp.where(bit == 0, low, high)


def my_half(block):
    rows = block.shape[0] // 2
    return lax.dynamic_slice_in_dim(block, bit_of("dp", 1) * rows, rows, axis=0)[None]


class Gather:
    def __init__(self, mine):
        *steps, self.last = reversed(bits_of("shard"))
        for axis, bit in steps:
            mine = both(bit_of(axis, bit), mine, flip(mine, axis, bit), 0)
        self.mine = mine
        self.came = flip(mine, *self.last)

    def merge(self, *after):
        came = tie(self.came, *after) if after else self.came
        return both(bit_of(*self.last), self.mine, came, 0)


def over_cores(mine):
    full = both(bit_of("dp", 1), mine, flip(mine, "dp", 1), 1)
    return full.reshape(-1, mine.shape[-1])


class Sum:
    def __init__(self, keep, send):
        self.labels = bits_of("shard") + bits_of("dp")[:-1]
        self.cols = keep.shape[1]
        self.unit = keep.shape[0] // 2 ** len(self.labels)
        self.keep = keep
        self.sent = send
        self.came = [flip(send, "dp", 1)]
        self.value = None
        self.left = list(self.labels)

    def after(self, other):
        if self.value is None:
            self.keep = tie(self.keep, other)
        else:
            self.value = tie(self.value, other)

    def settle(self):
        if self.value is not None:
            return
        total = self.keep.astype(f32)
        for came in self.came:
            total += came.astype(f32)
        self.value = total.astype(bf16).reshape((2,) * len(self.left) + (self.unit, self.cols))

    def halve(self, axis, bit):
        self.settle()
        dim = self.left.index((axis, bit))
        me = bit_of(axis, bit)
        self.sent = lax.dynamic_index_in_dim(self.value, 1 - me, dim, keepdims=False)
        self.keep = lax.dynamic_index_in_dim(self.value, me, dim, keepdims=False)
        self.came = [flip(self.sent, axis, bit)]
        self.left.remove((axis, bit))
        self.value = None

    def masks(self):
        count = len(self.last)
        for k in range(1, 2**count):
            bits = (bit for i, (_, bit) in enumerate(self.last) if k >> (count - 1 - i) & 1)
            yield k, sum(bits)

    def scatter(self):
        self.settle()
        self.last = list(self.left)
        value = self.value.reshape(-1, self.unit, self.cols)
        me = 0
        for axis, bit in self.last:
            me = 2 * me + bit_of(axis, bit)
        self.keep = lax.dynamic_index_in_dim(value, me, 0, keepdims=False)
        self.came = []
        for k, mask in self.masks():
            send = lax.dynamic_index_in_dim(value, lax.bitwise_xor(me, k), 0, keepdims=False)
            self.came.append(flip(send, "dp", mask))
        self.left = []
        self.value = None

    def collect(self):
        self.settle()
        pieces = [self.value]
        for _, mask in self.masks():
            pieces.append(flip(self.value, "dp", mask))
        for axis, bit in reversed(self.last):
            me = bit_of(axis, bit)
            pairs = zip(pieces[::2], pieces[1::2])
            pieces = [both(me, low[None], high[None], 0) for low, high in pairs]
        self.value = pieces[0]
        self.left = list(self.last)

    def double(self, axis, bit):
        order = [label for label in self.labels if label in self.left or label == (axis, bit)]
        dim = order.index((axis, bit))
        mine = jnp.expand_dims(self.value, dim)
        self.value = both(bit_of(axis, bit), mine, flip(mine, axis, bit), dim)
        self.left = order

    def finish(self):
        self.value = self.value.reshape(-1, self.cols)
        self.other = flip(self.value, "dp", 1)

    def columns(self, first, last):
        mine, other = self.value[:, first:last], self.other[:, first:last]
        return both(bit_of("dp", 1), mine, other, 0).astype(f32)


def copy_kernel(value_ref, copy_ref):
    copy_ref[...] = value_ref[...]


def copy_after(value, *deps):
    flat = value.reshape(-1, value.shape[-1])
    out = [(flat.shape, flat.dtype)]
    (copy,) = call(copy_kernel, out, [], (flat,), None, 1, deps=deps)
    return copy.reshape(value.shape)


def join(*sums):
    for one in sums:
        one.settle()
    joined = object.__new__(Sum)
    joined.labels, joined.unit, joined.left = sums[0].labels, sums[0].unit, sums[0].left
    joined.last = getattr(sums[0], "last", None)
    joined.cols = sum(one.cols for one in sums)
    joined.value = jnp.concatenate([one.value for one in sums], axis=-1)
    return joined


def tie(value, *others):
    return lax.optimization_barrier((value,) + others)[0]


def compute(tokens, seg_rows, scale_rows, cotangent, weights, hidden):
    length, width = tokens.shape
    *qkv, wo_block, vectors, wi_block, wu_block = weights

    def later(done):
        *args, _ = lax.optimization_barrier((wo_block, wi_block, wu_block, *vectors, done))
        wo, wi, wu, *params = args
        stacked = jnp.pad(jnp.stack(params, axis=1), ((0, 0), (0, 128 - len(params))))
        groups = jnp.split(wu, hidden // width, axis=0)
        parts = ((wi, wo, stacked), groups)
        return [jnp.concatenate([my_half(w) for w in part], axis=-1) for part in parts]

    size = width // H
    rows = width // 2
    shards = lax.axis_size("shard")
    core = bit_of("dp", 1).reshape(1)
    tall = ((width, length), bf16)
    tall32 = ((width, length), f32)
    wide = ((hidden, length), bf16)
    bias = ((length, 3 * B), f32)
    pair = ((2, length, 3 * B), bf16)
    shapes = [((3, rows, length), bf16), ((rows, length), bf16), ((H // 2, 8, length), f32)]

    half = width // 2
    packed = jnp.concatenate([my_half(w) for w in qkv], axis=-1)
    mine = Gather(packed).merge()
    wqkv = over_cores(mine)
    wio_part, wu_part = later(packed)
    wio_gather = Gather(tie(wio_part, mine))
    (x1,) = call(turn_kernel, [tall], [], (tie(tokens, packed),), None, 1)
    attend = functools.partial(attend_kernel, 1, size)
    turned = [((3 * rows, width), bf16)]
    wa_t, qkv1a, o1a, lse1a = call(attend, turned + shapes, [bias], (x1, wqkv, seg_rows))
    wio_mine = wio_gather.merge(o1a)
    wio = over_cores(wio_mine)
    wu_part = tie(wu_part, wio_mine)
    wu_gather = Gather(wu_part)
    attend = functools.partial(attend_kernel, 2, size)
    wb_t, qkv1b, o1b, lse1b = call(
        attend, turned + shapes, [bias], (x1, wqkv, tie(seg_rows, wio_mine, wu_part))
    )
    o1, wo_t, wi_t, y1, n11, stat11, yr1, z1, slope1 = call(
        feed_in_kernel,
        [tall, ((width, width), bf16), ((hidden, width), bf16), tall32, tall]
        + [((8, length), f32), tall, wide, wide],
        [],
        (o1a, o1b, x1, wio),
    )
    wu_groups = over_cores(wu_gather.merge(o1b))
    wu, wu_t, next1, x2, n21, stat12 = call(
        functools.partial(feed_out_kernel, shards),
        [((hidden, width), bf16), ((width, hidden), bf16), tall32, tall, tall]
        + [((8, length), f32)],
        [],
        (y1, z1, wio, wu_groups),
    )
    attend = functools.partial(attend_kernel, 0, size)
    qkv2a, o2a, lse2a = call(attend, shapes, [bias], (x2, wa_t, seg_rows), limit=6)
    qkv2b, o2b, lse2b = call(attend, shapes, [bias], (x2, wb_t, seg_rows), limit=6)
    o2, mixed, z2, du2, yr2, dfr2, dar2, dh2, do2, acc = call(
        feed_last_kernel,
        [tall, ((length, width), bf16), wide, wide, tall, tall, tall, tall32, tall]
        + [((4, width, 128), f32)],
        [((2, width, B), f32)],
        (o2a, o2b, next1, wio, wu, wo_t, wi_t, wu_t, cotangent, scale_rows),
        limit=10,
    )
    back = [bias, pair, pair]
    more_u, more_i, more_o = call(
        partial_kernel,
        [((hidden, width), bf16)] * 2 + [((width, width), bf16)],
        [],
        (z2, dfr2, du2, yr2, o2, dar2),
        limit=4,
    )
    dqkv2, more = [], []
    more_qkv = shapes[:1] + [((width, 3 * rows), bf16)]
    for group, (qkv, lse) in enumerate(((qkv2a, lse2a), (qkv2b, lse2b))):
        kernel = functools.partial(attend_back_kernel, group * rows, size)
        args = (qkv, o2, do2, lse, seg_rows, x2)
        found = call(kernel, more_qkv, back, args, limit=10, deps=(more_u,))
        dqkv2.append(found[0])
        more.append(found[1])
    joined = [((3 * width, length), bf16)]
    (grad1,) = call(
        functools.partial(input_kernel, False), [tall32], joined, (wqkv, dh2, *dqkv2), None, 3, 4
    )
    dh1, do1, du1, dfr1, dar1, acc = call(
        feed_back_kernel,
        [tall32, tall, wide, tall, tall, ((4, width, 128), f32)],
        [],
        (grad1, n11, n21, stat11, stat12, slope1, wio, wu, acc),
        alias={5: 2, 8: 5},
    )
    keep_u, send_u = call(
        functools.partial(outer_grad_kernel, shards),
        [((half, hidden + width + 128), bf16)] * 2,
        [],
        (core, z1, dfr1, more_u, o1, dar1, more_o, acc),
        [SM] + [VM] * 7,
        limit=4,
    )
    outer = Sum(keep_u, send_u)
    y_bit = bits_of("dp")[-2]
    x_bits = bits_of("shard")
    outer = Sum(keep_u, send_u)
    for label in x_bits:
        outer.halve(*label)
    keep_i, send_i = call(
        functools.partial(inner_grad_kernel, shards),
        [((half, hidden), bf16)] * 2,
        [],
        (core, yr1, du1, more_i),
        [SM] + [VM] * 3,
        limit=4,
        deps=(outer.sent,),
    )
    inner = Sum(keep_i, send_i)
    parts = []

    def part(p, *deps):
        qkv, lse = ((qkv1a, lse1a), (qkv1b, lse1b))[p // 2]
        args = (qkv, o1, do1, lse, seg_rows)
        specs = [VM] * 5
        outs = [((3, 2 * size, length), bf16)]
        if p % 2:
            args += (core, x1, parts[-1], more[p // 2])
            specs += [SM] + [VM] * 3
            outs += [((half, 3 * rows), bf16)] * 2
        kernel = functools.partial(attend_part_kernel, p, size, shards)
        results = call(kernel, outs, back, args, specs, 15, 10, deps=deps)
        parts.append(results[0])
        return results[1:]

    part(0, send_i)
    outer.keep = copy_after(outer.keep, parts[0])
    outer.halve(*y_bit)
    for label in x_bits:
        inner.halve(*label)
    first = Sum(*part(1, outer.sent, inner.sent))
    part(2, parts[1])
    outer.keep = copy_after(outer.keep, parts[1])
    inner.halve(*y_bit)
    for label in x_bits:
        first.halve(*label)
    outer.settle()
    second = Sum(*part(3, inner.sent, first.sent, outer.value))
    feed = join(outer, inner)
    feed.scatter()
    for label in x_bits:
        second.halve(*label)
    heads = join(first, second)
    heads.halve(*y_bit)
    heads.settle()
    feed.keep = copy_after(feed.keep, heads.value)
    feed.settle()
    feed.collect()
    (input_grad,) = call(
        functools.partial(input_kernel, True),
        [((length, width), f32)],
        joined,
        (wqkv, dh1, *parts),
        None,
        5,
        5,
        deps=(heads.sent,),
    )
    feed.double(*y_bit)
    feed.finish()
    heads.scatter()
    heads.settle()
    heads.collect()
    inner_at = hidden + width + 128
    dwu = [feed.columns(at, at + width) for at in range(0, hidden, width)]
    dwu = jnp.concatenate(dwu, axis=0)
    dwo = feed.columns(hidden, hidden + width)
    dpar = feed.columns(hidden + width, inner_at)
    dwi = feed.columns(inner_at, inner_at + hidden)
    heads.value = copy_after(heads.value, feed.value)
    heads.double(*y_bit)
    heads.finish()
    dqkv = [
        jnp.concatenate([heads.columns(c, c + half) for c in (at, at + 3 * half)], axis=1)
        for at in range(0, 3 * half, half)
    ]
    return (mixed, input_grad, *dqkv, dwo, dwi, dwu, *(dpar[:, i] for i in range(4)))


def body(
    tokens,
    segment_ids,
    row_counts,
    global_count,
    cotangent,
    query_weight,
    key_weight,
    value_weight,
    output_weight,
    inner_weight,
    outer_weight,
    attn_gain,
    attn_bias,
    feed_gain,
    feed_bias,
):
    length, width = tokens.shape
    hidden = inner_weight.shape[1]
    half = width // 2
    weights = (query_weight, key_weight, value_weight, output_weight)
    weights += ((attn_gain, attn_bias, feed_gain, feed_bias), inner_weight, outer_weight)
    seg_rows = jnp.broadcast_to(segment_ids.astype(f32)[None], (8, length))
    valid = (jnp.arange(length) < row_counts[0]).astype(f32)
    tokens_total = lax.axis_size("dp") * lax.axis_size("shard") * length
    factor = jnp.float32(tokens_total) / global_count[0].astype(f32)
    scale_rows = jnp.broadcast_to((valid * factor)[None], (8, length))
    return compute(tokens, seg_rows, scale_rows, cotangent, weights, hidden)


def solution(mesh):
    rows = P(("dp", "shard"))
    rows_two = P(("dp", "shard"), None)
    two = P("shard", None)
    one = P("shard")
    in_specs = (rows_two, rows, rows, P(), rows_two) + (two,) * 6 + (one,) * 4
    out_specs = (rows_two, rows_two) + (two,) * 6 + (one,) * 4
    return jax.shard_map(body, mesh=mesh, in_specs=in_specs, out_specs=out_specs, check_vma=False)
```

```python
import functools

import jax
import jax.numpy as jnp
from jax import lax
from jax.experimental import pallas as pl
from jax.experimental.pallas import tpu as pltpu
from jax.sharding import PartitionSpec as P

H = 8
B = 256
CHUNK = 256
norm_eps = 1e-05
masked_score = -1e30
bf16 = jnp.bfloat16
f32 = jnp.float32


def nn(left, right):
    return lax.dot_general(left, right, (((1,), (0,)), ((), ())), preferred_element_type=f32)


def nt(left, right):
    return lax.dot_general(left, right, (((1,), (1,)), ((), ())), preferred_element_type=f32)


def band(block, blocks):
    return max(0, block - 1) * B, min(blocks, block + 2) * B


def key_blocks(block, blocks):
    low, high = band(block, blocks)
    for at in range(low, high, B):
        step = (block * B - at) // B + 1
        yield slice(at, at + B), slice(step * B, (step + 1) * B), slice(at - low, at - low + B)


def query_blocks(block, blocks):
    low, high = band(block, blocks)
    first = low - block * B + B
    return slice(low, high), slice(first, first + high - low)


def fill_bias(seg_ref, bias_ref):
    column = seg_ref[...].T[:, 0:1]
    blocks = bias_ref.shape[0] // B
    for block in range(blocks):
        row = seg_ref[0:1, block * B : (block + 1) * B]
        for keys, cols, _ in key_blocks(block, blocks):
            bias_ref[keys, cols] = jnp.where(column[keys] == row, 0.0, masked_score)


def bias_of(bias_ref, block, blocks):
    parts = [bias_ref[keys, cols] for keys, cols, _ in key_blocks(block, blocks)]
    return jnp.concatenate(parts, axis=0)


def attend_head(head, size, qkv_ref, bias_ref, o_ref, lse_ref):
    blocks = qkv_ref.shape[2] // B
    rows = pl.ds(pl.multiple_of(head * size, size), size)
    key = qkv_ref[1, rows, :].T
    for block in range(blocks):
        low, high = band(block, blocks)
        tile = slice(block * B, (block + 1) * B)
        score = nn(key[low:high], qkv_ref[0, rows, tile]) + bias_of(bias_ref, block, blocks)
        top = jnp.max(score, axis=0, keepdims=True)
        weight = jnp.exp(score - top)
        total = jnp.sum(weight, axis=0, keepdims=True)
        mixed = nn(qkv_ref[2, rows, low:high], weight.astype(bf16)) * (1.0 / total)
        o_ref[rows, tile] = mixed.astype(bf16)
        lse_ref[head, :, tile] = jnp.broadcast_to(top + jnp.log(total), (8, B))


def attend_head_back(
    head, out, size, qkv_ref, o_ref, do_ref, lse_ref, bias_ref, prob_ref, ds_ref, dqkv_ref
):
    length = qkv_ref.shape[2]
    blocks = length // B
    scale = size**-0.5
    rows = pl.ds(pl.multiple_of(head * size, size), size)
    outs = pl.ds(pl.multiple_of(out * size, size), size)
    key_t = qkv_ref[1, rows, :]
    key = key_t.T
    value = qkv_ref[2, rows, :].T
    do_t = do_ref[rows, :]
    delta = jnp.sum(do_t.astype(f32) * o_ref[rows, :].astype(f32), axis=0, keepdims=True)
    for block in range(blocks):
        low, high = band(block, blocks)
        tile = slice(block * B, (block + 1) * B)
        score = nn(key[low:high], qkv_ref[0, rows, tile]) + bias_of(bias_ref, block, blocks)
        prob = jnp.exp(score - lse_ref[head, 0:1, tile])
        prob_low = prob.astype(bf16)
        dprob = nn(value[low:high], do_t[:, tile])
        dscore = (prob * (dprob - delta[:, tile])).astype(bf16)
        for keys, cols, part in key_blocks(block, blocks):
            prob_ref[keys, cols] = prob_low[part]
            ds_ref[keys, cols] = dscore[part]
        dq = nn(key_t[:, low:high], dscore) * scale
        dqkv_ref[0, outs, tile] = dq.astype(bf16)
    query = qkv_ref[0, rows, :].T
    do = do_t.T
    for block in range(blocks):
        tile = slice(block * B, (block + 1) * B)
        queries, cols = query_blocks(block, blocks)
        dv = nn(prob_ref[tile, cols], do[queries])
        dqkv_ref[2, outs, tile] = dv.astype(bf16).T
        dk = nn(ds_ref[tile, cols], query[queries])
        dqkv_ref[1, outs, tile] = dk.astype(bf16).T


def normalize(values):
    center = values - jnp.mean(values, axis=0, keepdims=True)
    spread = jnp.mean(center * center, axis=0, keepdims=True)
    scale = lax.rsqrt(spread + norm_eps)
    return center * scale, scale


def normalize_back(dn, n, scale):
    mean_one = jnp.mean(dn, axis=0, keepdims=True)
    mean_two = jnp.mean(dn * n, axis=0, keepdims=True)
    return (dn - mean_one - n * mean_two) * scale


def gelu_pair(u):
    c0 = 0.7978845608028654
    c1 = c0 * 0.044715
    square = u * u
    t = jnp.tanh(u * (c0 + c1 * square))
    half = 0.5 * u
    cdf = 0.5 + 0.5 * t
    z = u * cdf
    slope = cdf + half * (1.0 - t * t) * (c0 + (3.0 * c1) * square)
    return z, slope


def lanes_sum(values):
    return values[:, :128] + values[:, 128:]


def turn_kernel(x_ref, x_t_ref):
    x_t_ref[...] = x_ref[...].T


def attend_kernel(first, size, x_ref, w_ref, seg_ref, *refs):
    if first:
        group, w_t_ref = first - 1, refs[0]
        count = w_t_ref.shape[0] // 3
        for i in range(3):
            at = i * x_ref.shape[0] + group * count
            w_t_ref[i * count : (i + 1) * count, :] = w_ref[:, at : at + count].T
        refs = refs[1:]
    else:
        w_t_ref = w_ref
    qkv_ref, o_ref, lse_ref, bias_ref = refs
    rows = o_ref.shape[0]
    fill_bias(seg_ref, bias_ref)
    for at in range(0, x_ref.shape[1], B):
        cols = slice(at, at + B)
        query = nn(w_t_ref[:rows, :], x_ref[:, cols]).astype(bf16)
        qkv_ref[0, :, cols] = query * jnp.asarray(size**-0.5, bf16)
        qkv_ref[1, :, cols] = nn(w_t_ref[rows : 2 * rows, :], x_ref[:, cols]).astype(bf16)
        qkv_ref[2, :, cols] = nn(w_t_ref[2 * rows :, :], x_ref[:, cols]).astype(bf16)

    def two_heads(pair, carry):
        for one in range(2):
            attend_head(2 * pair + one, size, qkv_ref, bias_ref, o_ref, lse_ref)
        return carry

    lax.fori_loop(0, rows // size // 2, two_heads, 0)


def join_heads(oa_ref, ob_ref, o_ref):
    rows = oa_ref.shape[0]
    o_ref[:rows, :] = oa_ref[...]
    o_ref[rows:, :] = ob_ref[...]


def feed_in_kernel(
    oa_ref,
    ob_ref,
    x_ref,
    wio_ref,
    o_ref,
    wo_t_ref,
    wi_t_ref,
    y_ref,
    n1_ref,
    stat_ref,
    yr_ref,
    z_ref,
    slope_ref,
):
    width = wio_ref.shape[0]
    hidden = wio_ref.shape[1] - width - 128
    join_heads(oa_ref, ob_ref, o_ref)
    wo_t_ref[...] = wio_ref[:, hidden : hidden + width].T
    wi_t_ref[...] = wio_ref[:, :hidden].T
    params = wio_ref[:, hidden + width :].astype(f32)
    gain_one, bias_one = params[:, 0:1], params[:, 1:2]
    for at in range(0, x_ref.shape[1], B):
        cols = slice(at, at + B)
        h = x_ref[:, cols].astype(f32) + nn(wo_t_ref[...], o_ref[:, cols])
        n1, s1 = normalize(h)
        n1_ref[:, cols] = n1.astype(bf16)
        stat_ref[:, cols] = jnp.broadcast_to(s1, (8, B))
        y = n1 * gain_one + bias_one
        yr_ref[:, cols] = y.astype(bf16)
        y_ref[:, cols] = y
        for f in range(0, hidden, CHUNK):
            u = nn(wi_t_ref[f : f + CHUNK, :], yr_ref[:, cols])
            z, slope = gelu_pair(u)
            z_ref[f : f + CHUNK, cols] = z.astype(bf16)
            slope_ref[f : f + CHUNK, cols] = slope.astype(bf16)


def feed_out_kernel(
    shards,
    y_ref,
    z_ref,
    wio_ref,
    groups_ref,
    wu_ref,
    wu_t_ref,
    next_ref,
    x2_ref,
    n2_ref,
    stat_ref,
):
    hidden, width = wu_ref.shape
    count = hidden // width
    rows = width // shards
    for shard in range(shards):
        for group in range(count):
            at = (shard * count + group) * rows
            part = slice(shard * rows, (shard + 1) * rows)
            wu_ref[at : at + rows, :] = groups_ref[part, group * width : (group + 1) * width]
    wu_t_ref[...] = wu_ref[...].T
    params = wio_ref[:, hidden + width :].astype(f32)
    gain_two, bias_two = params[:, 2:3], params[:, 3:4]
    for at in range(0, y_ref.shape[1], B):
        cols = slice(at, at + B)
        h2 = y_ref[:, cols] + nn(wu_t_ref[...], z_ref[:, cols])
        n2, s2 = normalize(h2)
        n2_ref[:, cols] = n2.astype(bf16)
        stat_ref[:, cols] = jnp.broadcast_to(s2, (8, B))
        out = n2 * gain_two + bias_two
        next_ref[:, cols] = out
        x2_ref[:, cols] = out.astype(bf16)


def feed_last_kernel(
    oa_ref,
    ob_ref,
    x_ref,
    wio_ref,
    wu_ref,
    wo_t_ref,
    wi_t_ref,
    wu_t_ref,
    cot_ref,
    scale_ref,
    o_ref,
    mixed_ref,
    z_ref,
    du_ref,
    yr_ref,
    dfr_ref,
    dar_ref,
    dh_ref,
    do_ref,
    acc_ref,
    n1_ref,
):
    width = wio_ref.shape[0]
    hidden = wio_ref.shape[1] - width - 128
    join_heads(oa_ref, ob_ref, o_ref)
    params = wio_ref[:, hidden + width :].astype(f32)
    gain_one, bias_one = params[:, 0:1], params[:, 1:2]
    gain_two, bias_two = params[:, 2:3], params[:, 3:4]
    acc_ref[...] = jnp.zeros_like(acc_ref)

    for at in range(0, x_ref.shape[1], B):
        cols = slice(at, at + B)
        slot = at // B % 2
        h = x_ref[:, cols] + nn(wo_t_ref[...], o_ref[:, cols])
        n1, s1 = normalize(h)
        n1_ref[slot] = n1
        y = n1 * gain_one + bias_one
        yr_ref[:, cols] = y.astype(bf16)
        dh_ref[:, cols] = y
        for f in range(0, hidden, CHUNK):
            u = nn(wi_t_ref[f : f + CHUNK, :], yr_ref[:, cols])
            z, slope = gelu_pair(u)
            z_ref[f : f + CHUNK, cols] = z.astype(bf16)
            du_ref[f : f + CHUNK, cols] = slope.astype(bf16)
        h2 = dh_ref[:, cols] + nn(wu_t_ref[...], z_ref[:, cols])
        n2, s2 = normalize(h2)
        out = n2 * gain_two + bias_two
        mixed_ref[cols, :] = out.astype(bf16).T
        grad = cot_ref[cols, :].T * scale_ref[0:1, cols]
        acc_ref[2] += lanes_sum(grad * n2)
        acc_ref[3] += lanes_sum(grad)
        dh2 = normalize_back(grad * gain_two, n2, s2)
        dh_ref[:, cols] = dh2
        dfr_ref[:, cols] = dh2.astype(bf16)
        for f in range(0, hidden, CHUNK):
            dz = nn(wu_ref[f : f + CHUNK, :], dfr_ref[:, cols])
            slope = du_ref[f : f + CHUNK, cols].astype(f32)
            du_ref[f : f + CHUNK, cols] = (dz * slope).astype(bf16)
        dy = dh_ref[:, cols] + nn(wio_ref[:, :hidden], du_ref[:, cols])
        acc_ref[0] += lanes_sum(dy * n1_ref[slot])
        acc_ref[1] += lanes_sum(dy)
        dh = normalize_back(dy * gain_one, n1_ref[slot], s1)
        dh_ref[:, cols] = dh
        dar_ref[:, cols] = dh.astype(bf16)
        do_ref[:, cols] = nn(wio_ref[:, hidden : hidden + width], dar_ref[:, cols]).astype(bf16)


def feed_back_kernel(
    g_ref,
    n1_ref,
    n2_ref,
    stat1_ref,
    stat2_ref,
    slope_ref,
    wio_ref,
    wu_ref,
    acc_in_ref,
    dh_ref,
    do_ref,
    du_ref,
    dfr_ref,
    dar_ref,
    acc_ref,
):
    width = wio_ref.shape[0]
    hidden = wio_ref.shape[1] - width - 128
    params = wio_ref[:, hidden + width :].astype(f32)
    gain_one, gain_two = params[:, 0:1], params[:, 2:3]
    acc_ref[...] = acc_in_ref[...]
    for at in range(0, g_ref.shape[1], B):
        cols = slice(at, at + B)
        grad = g_ref[:, cols]
        n2 = n2_ref[:, cols].astype(f32)
        acc_ref[2] += lanes_sum(grad * n2)
        acc_ref[3] += lanes_sum(grad)
        dh2 = normalize_back(grad * gain_two, n2, stat2_ref[0:1, cols])
        dh_ref[:, cols] = dh2
        dfr_ref[:, cols] = dh2.astype(bf16)
        for f in range(0, hidden, CHUNK):
            dz = nn(wu_ref[f : f + CHUNK, :], dfr_ref[:, cols])
            slope = slope_ref[f : f + CHUNK, cols].astype(f32)
            du_ref[f : f + CHUNK, cols] = (dz * slope).astype(bf16)
        dy = dh_ref[:, cols] + nn(wio_ref[:, :hidden], du_ref[:, cols])
        n1 = n1_ref[:, cols].astype(f32)
        acc_ref[0] += lanes_sum(dy * n1)
        acc_ref[1] += lanes_sum(dy)
        dh = normalize_back(dy * gain_one, n1, stat1_ref[0:1, cols])
        dh_ref[:, cols] = dh
        dar_ref[:, cols] = dh.astype(bf16)
        do_ref[:, cols] = nn(wio_ref[:, hidden : hidden + width], dar_ref[:, cols]).astype(bf16)


def place(value, first, unit, core, keep_ref, send_ref, cols):
    for at in range(0, value.shape[0], unit):
        block = (first + at) // unit
        rows = slice(block // 2 * unit, block // 2 * unit + unit)
        part = value[at : at + unit]

        @pl.when(core == block % 2)
        def _():
            keep_ref[rows, cols] = part

        @pl.when(core != block % 2)
        def _():
            send_ref[rows, cols] = part


def partial_kernel(
    z_ref, dfr_ref, du_ref, yr_ref, o_ref, dar_ref, outer_ref, inner_ref, output_ref
):
    for first in range(0, z_ref.shape[0], CHUNK):
        part = slice(first, first + CHUNK)
        outer_ref[part, :] = nt(z_ref[part, :], dfr_ref[...]).astype(bf16)
        inner_ref[part, :] = nt(du_ref[part, :], yr_ref[...]).astype(bf16)
    for first in range(0, o_ref.shape[0], CHUNK):
        part = slice(first, first + CHUNK)
        output_ref[part, :] = nt(o_ref[part, :], dar_ref[...]).astype(bf16)


def outer_grad_kernel(
    shards,
    core_ref,
    z_ref,
    dfr_ref,
    more_ref,
    o_ref,
    dar_ref,
    more_o_ref,
    acc_ref,
    keep_ref,
    send_ref,
):
    core = core_ref[0]
    hidden, width = z_ref.shape[0], dfr_ref.shape[0]
    unit = width // shards // 2
    groups = hidden // width
    per_group = hidden // shards // groups
    for first in range(0, hidden, 256):
        part = slice(first, first + 256)
        dwu = nt(z_ref[part, :], dfr_ref[...]) + more_ref[part, :].astype(f32)
        dwu = dwu.astype(bf16)
        for at in range(0, 256, per_group):
            block = (first + at) // per_group
            shard, group = block // groups, block % groups
            cols = slice(group * width, (group + 1) * width)
            rows = dwu[at : at + per_group]
            place(rows, shard * per_group, unit, core, keep_ref, send_ref, cols)
    for first in range(0, width, CHUNK):
        part = slice(first, first + CHUNK)
        dwo = nt(o_ref[part, :], dar_ref[...]) + more_o_ref[part, :].astype(f32)
        place(dwo.astype(bf16), first, unit, core, keep_ref, send_ref, slice(hidden, hidden + width))
    lane = lax.broadcasted_iota(jnp.int32, (width, 128), 1)
    dpar = jnp.zeros((width, 128), f32)
    for i in range(4):
        dpar = jnp.where(lane == i, jnp.sum(acc_ref[i], axis=1, keepdims=True), dpar)
    last = slice(hidden + width, hidden + width + 128)
    place(dpar.astype(bf16), 0, unit, core, keep_ref, send_ref, last)


def inner_grad_kernel(shards, core_ref, yr_ref, du_ref, more_ref, keep_ref, send_ref):
    core = core_ref[0]
    width, hidden = yr_ref.shape[0], du_ref.shape[0]
    unit = width // shards // 2
    for first in range(0, hidden, CHUNK):
        part = slice(first, first + CHUNK)
        dwi_t = nt(du_ref[part, :], yr_ref[...]) + more_ref[part, :].astype(f32)
        place(dwi_t.astype(bf16).T, 0, unit, core, keep_ref, send_ref, part)


def attend_back_kernel(
    first, size, qkv_ref, o_ref, do_ref, lse_ref, seg_ref, x_ref, dqkv_ref, more_ref, *refs
):
    bias_ref, prob_ref, ds_ref = refs
    rows = dqkv_ref.shape[1]
    fill_bias(seg_ref, bias_ref)
    here = slice(first, first + rows)

    def two_heads(pair, carry):
        for one in range(2):
            head = 2 * pair + one
            attend_head_back(
                head,
                head,
                size,
                qkv_ref,
                o_ref.at[here],
                do_ref.at[here],
                lse_ref,
                bias_ref,
                prob_ref.at[one],
                ds_ref.at[one],
                dqkv_ref,
            )
        return carry

    lax.fori_loop(0, rows // size // 2, two_heads, 0)
    for i in range(3):
        more_ref[:, i * rows : (i + 1) * rows] = nt(x_ref[...], dqkv_ref[i]).astype(bf16)


def attend_part_kernel(
    p, size, shards, qkv_ref, o_ref, do_ref, lse_ref, seg_ref, *refs
):
    grads = p % 2 == 1
    if grads:
        core_ref, x1_ref, before_ref, more_ref = refs[:4]
        dqkv_ref, keep_ref, send_ref, bias_ref, prob_ref, ds_ref = refs[4:]
    else:
        dqkv_ref, bias_ref, prob_ref, ds_ref = refs
    fill_bias(seg_ref, bias_ref)
    rows = qkv_ref.shape[1]
    here = slice(p // 2 * rows, (p // 2 + 1) * rows)
    for one in range(2):
        attend_head_back(
            p % 2 * 2 + one,
            one,
            size,
            qkv_ref,
            o_ref.at[here],
            do_ref.at[here],
            lse_ref,
            bias_ref,
            prob_ref.at[one],
            ds_ref.at[one],
            dqkv_ref,
        )
    if not grads:
        return
    core = core_ref[0]
    unit = x1_ref.shape[0] // shards // 2
    for i in range(3):
        joined = jnp.concatenate([before_ref[i], dqkv_ref[i]], axis=0)
        cols = slice(i * rows, (i + 1) * rows)
        dw = nt(x1_ref[...], joined) + more_ref[:, cols].astype(f32)
        place(dw.astype(bf16), 0, unit, core, keep_ref, send_ref, cols)


def input_kernel(turned, w_ref, dh_ref, *refs):
    parts, grad_ref, join_ref = refs[:-2], refs[-2], refs[-1]
    length = dh_ref.shape[1]
    at = 0
    for i in range(3):
        for part in parts:
            rows = part.shape[1]
            join_ref[at : at + rows, :] = part[i]
            at += rows
    for at in range(0, length, B):
        cols = slice(at, at + B)
        grad = dh_ref[:, cols] + nn(w_ref[...], join_ref[:, cols])
        if turned:
            grad_ref[cols, :] = grad.T
        else:
            grad_ref[:, cols] = grad


VM = pl.BlockSpec(memory_space=pltpu.VMEM)
SM = pl.BlockSpec(memory_space=pltpu.SMEM)


def call(kernel, outs, scratch, args, specs=None, cost=10, limit=6, alias={}, deps=()):
    count, after = len(args), len(args) + len(deps)

    def run(*refs):
        kernel(*refs[:count], *refs[after:])

    return pl.pallas_call(
        run,
        out_shape=[jax.ShapeDtypeStruct(shape, dtype) for shape, dtype in outs],
        in_specs=(specs if specs else [VM] * count) + [pl.BlockSpec(memory_space=pl.ANY)] * len(deps),
        out_specs=[VM] * len(outs),
        scratch_shapes=[pltpu.VMEM(*one) for one in scratch],
        input_output_aliases=alias,
        cost_estimate=pl.CostEstimate(
            flops=cost * 1000000000, bytes_accessed=cost * 3000000, transcendentals=0
        ),
        compiler_params=pltpu.CompilerParams(vmem_limit_bytes=limit * 2**20),
    )(*args, *deps)


def flip(value, axis, bit):
    count = lax.axis_size(axis)
    return lax.ppermute(value, axis, [(i, i ^ bit) for i in range(count)])


def bit_of(axis, bit):
    return lax.rem(lax.div(lax.axis_index(axis), bit), 2)


def bits_of(axis):
    count = lax.axis_size(axis)
    found = []
    bit = count // 2
    while bit:
        found.append((axis, bit))
        bit //= 2
    return found


def both(bit, mine, other, dim):
    low = jnp.concatenate([mine, other], axis=dim)
    high = jnp.concatenate([other, mine], axis=dim)
    return jnp.where(bit == 0, low, high)


def my_half(block):
    rows = block.shape[0] // 2
    return lax.dynamic_slice_in_dim(block, bit_of("dp", 1) * rows, rows, axis=0)[None]


class Gather:
    def __init__(self, mine):
        *steps, self.last = reversed(bits_of("shard"))
        for axis, bit in steps:
            mine = both(bit_of(axis, bit), mine, flip(mine, axis, bit), 0)
        self.mine = mine
        self.came = flip(mine, *self.last)

    def merge(self, *after):
        came = tie(self.came, *after) if after else self.came
        return both(bit_of(*self.last), self.mine, came, 0)


def over_cores(mine):
    full = both(bit_of("dp", 1), mine, flip(mine, "dp", 1), 1)
    return full.reshape(-1, mine.shape[-1])


class Sum:
    def __init__(self, keep, send):
        self.labels = bits_of("shard") + bits_of("dp")[:-1]
        self.cols = keep.shape[1]
        self.unit = keep.shape[0] // 2 ** len(self.labels)
        self.keep = keep
        self.sent = send
        self.came = [flip(send, "dp", 1)]
        self.value = None
        self.left = list(self.labels)

    def after(self, other):
        if self.value is None:
            self.keep = tie(self.keep, other)
        else:
            self.value = tie(self.value, other)

    def settle(self):
        if self.value is not None:
            return
        total = self.keep.astype(f32)
        for came in self.came:
            total += came.astype(f32)
        self.value = total.astype(bf16).reshape((2,) * len(self.left) + (self.unit, self.cols))

    def halve(self, axis, bit):
        self.settle()
        dim = self.left.index((axis, bit))
        me = bit_of(axis, bit)
        self.sent = lax.dynamic_index_in_dim(self.value, 1 - me, dim, keepdims=False)
        self.keep = lax.dynamic_index_in_dim(self.value, me, dim, keepdims=False)
        self.came = [flip(self.sent, axis, bit)]
        self.left.remove((axis, bit))
        self.value = None

    def masks(self):
        count = len(self.last)
        for k in range(1, 2**count):
            bits = (bit for i, (_, bit) in enumerate(self.last) if k >> (count - 1 - i) & 1)
            yield k, sum(bits)

    def scatter(self):
        self.settle()
        self.last = list(self.left)
        value = self.value.reshape(-1, self.unit, self.cols)
        me = 0
        for axis, bit in self.last:
            me = 2 * me + bit_of(axis, bit)
        self.keep = lax.dynamic_index_in_dim(value, me, 0, keepdims=False)
        self.came = []
        for k, mask in self.masks():
            send = lax.dynamic_index_in_dim(value, lax.bitwise_xor(me, k), 0, keepdims=False)
            self.came.append(flip(send, "dp", mask))
        self.left = []
        self.value = None

    def collect(self):
        self.settle()
        pieces = [self.value]
        for _, mask in self.masks():
            pieces.append(flip(self.value, "dp", mask))
        for axis, bit in reversed(self.last):
            me = bit_of(axis, bit)
            pairs = zip(pieces[::2], pieces[1::2])
            pieces = [both(me, low[None], high[None], 0) for low, high in pairs]
        self.value = pieces[0]
        self.left = list(self.last)

    def double(self, axis, bit):
        order = [label for label in self.labels if label in self.left or label == (axis, bit)]
        dim = order.index((axis, bit))
        mine = jnp.expand_dims(self.value, dim)
        self.value = both(bit_of(axis, bit), mine, flip(mine, axis, bit), dim)
        self.left = order

    def finish(self):
        self.value = self.value.reshape(-1, self.cols)
        self.other = flip(self.value, "dp", 1)

    def columns(self, first, last):
        mine, other = self.value[:, first:last], self.other[:, first:last]
        return both(bit_of("dp", 1), mine, other, 0).astype(f32)


def copy_kernel(value_ref, copy_ref):
    copy_ref[...] = value_ref[...]


def copy_after(value, *deps):
    flat = value.reshape(-1, value.shape[-1])
    out = [(flat.shape, flat.dtype)]
    (copy,) = call(copy_kernel, out, [], (flat,), None, 1, deps=deps)
    return copy.reshape(value.shape)


def join(*sums):
    for one in sums:
        one.settle()
    joined = object.__new__(Sum)
    joined.labels, joined.unit, joined.left = sums[0].labels, sums[0].unit, sums[0].left
    joined.last = getattr(sums[0], "last", None)
    joined.cols = sum(one.cols for one in sums)
    joined.value = jnp.concatenate([one.value for one in sums], axis=-1)
    return joined


def tie(value, *others):
    return lax.optimization_barrier((value,) + others)[0]


def compute(tokens, seg_rows, scale_rows, cotangent, weights, hidden):
    length, width = tokens.shape
    *qkv, wo_block, vectors, wi_block, wu_block = weights

    def later(done):
        *args, _ = lax.optimization_barrier((wo_block, wi_block, wu_block, *vectors, done))
        wo, wi, wu, *params = args
        stacked = jnp.pad(jnp.stack(params, axis=1), ((0, 0), (0, 128 - len(params))))
        groups = jnp.split(wu, hidden // width, axis=0)
        parts = ((wi, wo, stacked), groups)
        return [jnp.concatenate([my_half(w) for w in part], axis=-1) for part in parts]

    size = width // H
    rows = width // 2
    shards = lax.axis_size("shard")
    core = bit_of("dp", 1).reshape(1)
    tall = ((width, length), bf16)
    tall32 = ((width, length), f32)
    wide = ((hidden, length), bf16)
    bias = ((length, 3 * B), f32)
    pair = ((2, length, 3 * B), bf16)
    shapes = [((3, rows, length), bf16), ((rows, length), bf16), ((H // 2, 8, length), f32)]

    half = width // 2
    packed = jnp.concatenate([my_half(w) for w in qkv], axis=-1)
    mine = Gather(packed).merge()
    wqkv = over_cores(mine)
    wio_part, wu_part = later(packed)
    wio_gather = Gather(tie(wio_part, mine))
    (x1,) = call(turn_kernel, [tall], [], (tie(tokens, packed),), None, 1)
    attend = functools.partial(attend_kernel, 1, size)
    turned = [((3 * rows, width), bf16)]
    wa_t, qkv1a, o1a, lse1a = call(attend, turned + shapes, [bias], (x1, wqkv, seg_rows))
    wio_mine = wio_gather.merge(o1a)
    wio = over_cores(wio_mine)
    wu_part = tie(wu_part, wio_mine)
    wu_gather = Gather(wu_part)
    attend = functools.partial(attend_kernel, 2, size)
    wb_t, qkv1b, o1b, lse1b = call(
        attend, turned + shapes, [bias], (x1, wqkv, tie(seg_rows, wio_mine, wu_part))
    )
    o1, wo_t, wi_t, y1, n11, stat11, yr1, z1, slope1 = call(
        feed_in_kernel,
        [tall, ((width, width), bf16), ((hidden, width), bf16), tall32, tall]
        + [((8, length), f32), tall, wide, wide],
        [],
        (o1a, o1b, x1, wio),
    )
    wu_groups = over_cores(wu_gather.merge(o1b))
    wu, wu_t, next1, x2, n21, stat12 = call(
        functools.partial(feed_out_kernel, shards),
        [((hidden, width), bf16), ((width, hidden), bf16), tall32, tall, tall]
        + [((8, length), f32)],
        [],
        (y1, z1, wio, wu_groups),
    )
    attend = functools.partial(attend_kernel, 0, size)
    qkv2a, o2a, lse2a = call(attend, shapes, [bias], (x2, wa_t, seg_rows), limit=6)
    qkv2b, o2b, lse2b = call(attend, shapes, [bias], (x2, wb_t, seg_rows), limit=6)
    o2, mixed, z2, du2, yr2, dfr2, dar2, dh2, do2, acc = call(
        feed_last_kernel,
        [tall, ((length, width), bf16), wide, wide, tall, tall, tall, tall32, tall]
        + [((4, width, 128), f32)],
        [((2, width, B), f32)],
        (o2a, o2b, next1, wio, wu, wo_t, wi_t, wu_t, cotangent, scale_rows),
        limit=10,
    )
    back = [bias, pair, pair]
    more_u, more_i, more_o = call(
        partial_kernel,
        [((hidden, width), bf16)] * 2 + [((width, width), bf16)],
        [],
        (z2, dfr2, du2, yr2, o2, dar2),
        limit=4,
    )
    dqkv2, more = [], []
    more_qkv = shapes[:1] + [((width, 3 * rows), bf16)]
    for group, (qkv, lse) in enumerate(((qkv2a, lse2a), (qkv2b, lse2b))):
        kernel = functools.partial(attend_back_kernel, group * rows, size)
        args = (qkv, o2, do2, lse, seg_rows, x2)
        found = call(kernel, more_qkv, back, args, limit=10, deps=(more_u,))
        dqkv2.append(found[0])
        more.append(found[1])
    joined = [((3 * width, length), bf16)]
    (grad1,) = call(
        functools.partial(input_kernel, False), [tall32], joined, (wqkv, dh2, *dqkv2), None, 3, 4
    )
    dh1, do1, du1, dfr1, dar1, acc = call(
        feed_back_kernel,
        [tall32, tall, wide, tall, tall, ((4, width, 128), f32)],
        [],
        (grad1, n11, n21, stat11, stat12, slope1, wio, wu, acc),
        alias={5: 2, 8: 5},
    )
    keep_u, send_u = call(
        functools.partial(outer_grad_kernel, shards),
        [((half, hidden + width + 128), bf16)] * 2,
        [],
        (core, z1, dfr1, more_u, o1, dar1, more_o, acc),
        [SM] + [VM] * 7,
        limit=4,
    )
    outer = Sum(keep_u, send_u)
    y_bit = bits_of("dp")[-2]
    x_bits = bits_of("shard")
    outer = Sum(keep_u, send_u)
    for label in x_bits:
        outer.halve(*label)
    keep_i, send_i = call(
        functools.partial(inner_grad_kernel, shards),
        [((half, hidden), bf16)] * 2,
        [],
        (core, yr1, du1, more_i),
        [SM] + [VM] * 3,
        limit=4,
        deps=(outer.sent,),
    )
    inner = Sum(keep_i, send_i)
    parts = []

    def part(p, *deps):
        qkv, lse = ((qkv1a, lse1a), (qkv1b, lse1b))[p // 2]
        args = (qkv, o1, do1, lse, seg_rows)
        specs = [VM] * 5
        outs = [((3, 2 * size, length), bf16)]
        if p % 2:
            args += (core, x1, parts[-1], more[p // 2])
            specs += [SM] + [VM] * 3
            outs += [((half, 3 * rows), bf16)] * 2
        kernel = functools.partial(attend_part_kernel, p, size, shards)
        results = call(kernel, outs, back, args, specs, 15, 10, deps=deps)
        parts.append(results[0])
        return results[1:]

    part(0, send_i)
    outer.keep = copy_after(outer.keep, parts[0])
    outer.halve(*y_bit)
    for label in x_bits:
        inner.halve(*label)
    first = Sum(*part(1, outer.sent, inner.sent))
    part(2, parts[1])
    outer.keep = copy_after(outer.keep, parts[1])
    inner.halve(*y_bit)
    for label in x_bits:
        first.halve(*label)
    outer.settle()
    second = Sum(*part(3, inner.sent, first.sent, outer.value))
    feed = join(outer, inner)
    feed.scatter()
    for label in x_bits:
        second.halve(*label)
    heads = join(first, second)
    heads.halve(*y_bit)
    feed.settle()
    feed.collect()
    (input_grad,) = call(
        functools.partial(input_kernel, True),
        [((length, width), f32)],
        joined,
        (wqkv, dh1, *parts),
        None,
        5,
        5,
        deps=(heads.sent,),
    )
    feed.double(*y_bit)
    feed.finish()
    heads.scatter()
    heads.settle()
    heads.collect()
    inner_at = hidden + width + 128
    dwu = [feed.columns(at, at + width) for at in range(0, hidden, width)]
    dwu = jnp.concatenate(dwu, axis=0)
    dwo = feed.columns(hidden, hidden + width)
    dpar = feed.columns(hidden + width, inner_at)
    dwi = feed.columns(inner_at, inner_at + hidden)
    heads.value = copy_after(heads.value, feed.value)
    heads.double(*y_bit)
    heads.finish()
    dqkv = [
        jnp.concatenate([heads.columns(c, c + half) for c in (at, at + 3 * half)], axis=1)
        for at in range(0, 3 * half, half)
    ]
    return (mixed, input_grad, *dqkv, dwo, dwi, dwu, *(dpar[:, i] for i in range(4)))


def body(
    tokens,
    segment_ids,
    row_counts,
    global_count,
    cotangent,
    query_weight,
    key_weight,
    value_weight,
    output_weight,
    inner_weight,
    outer_weight,
    attn_gain,
    attn_bias,
    feed_gain,
    feed_bias,
):
    length, width = tokens.shape
    hidden = inner_weight.shape[1]
    half = width // 2
    weights = (query_weight, key_weight, value_weight, output_weight)
    weights += ((attn_gain, attn_bias, feed_gain, feed_bias), inner_weight, outer_weight)
    seg_rows = jnp.broadcast_to(segment_ids.astype(f32)[None], (8, length))
    valid = (jnp.arange(length) < row_counts[0]).astype(f32)
    tokens_total = lax.axis_size("dp") * lax.axis_size("shard") * length
    factor = jnp.float32(tokens_total) / global_count[0].astype(f32)
    scale_rows = jnp.broadcast_to((valid * factor)[None], (8, length))
    return compute(tokens, seg_rows, scale_rows, cotangent, weights, hidden)


def solution(mesh):
    rows = P(("dp", "shard"))
    rows_two = P(("dp", "shard"), None)
    two = P("shard", None)
    one = P("shard")
    in_specs = (rows_two, rows, rows, P(), rows_two) + (two,) * 6 + (one,) * 4
    out_specs = (rows_two, rows_two) + (two,) * 6 + (one,) * 4
    return jax.shard_map(body, mesh=mesh, in_specs=in_specs, out_specs=out_specs, check_vma=False)
```
